32 devices in a mesh: item: 4 (over x, core), seq: 8 (over z, y).
Axes of the slice: x: 2, y: 2, z: 4, core: 2. Of those that a mesh axis runs over, the one named last changes fastest.
Arguments:
- byte_in: bfloat16 [16, 2048, 768], P('item', 'seq'), may hold values from -6 to 6
- lengths: int32 [16], P('item'), may hold values from 1024 to 2048, as said below
- latent_init: bfloat16 [256, 1280], replicated, may hold values from -6 to 6
- gain_kv: float32 [768], replicated, may hold values from 0.1 to 1.9
- gain_q: float32 [1280], replicated, may hold values from 0.1 to 1.9
- gain_mlp: float32 [1280], replicated, may hold values from 0.1 to 1.9
- w_query: bfloat16 [1280, 256], replicated, may hold values from -0.15625 to 0.15625
- w_key: bfloat16 [768, 256], replicated, may hold values from -0.21875 to 0.21875
- w_value: bfloat16 [768, 1280], replicated, may hold values from -0.21875 to 0.21875
- w_out: bfloat16 [1280, 1280], replicated, may hold values from -2.5 to 2.5
- w_up: bfloat16 [1280, 1280], replicated, may hold values from -0.15625 to 0.15625
- w_down: bfloat16 [1280, 1280], replicated, may hold values from -0.15625 to 0.15625
- d_out: bfloat16 [16, 256, 1280], P('item'), may hold values from -6 to 6
Outputs:
- latents_out: bfloat16 [16, 256, 1280], P('item')
- byte_grad: float32 [16, 2048, 768], P('item', 'seq')
- latent_grad: float32 [256, 1280], replicated
- gain_kv_grad: float32 [768], replicated
- gain_q_grad: float32 [1280], replicated
- gain_mlp_grad: float32 [1280], replicated
- query_grad: float32 [1280, 256], replicated
- key_grad: float32 [768, 256], replicated
- value_grad: float32 [768, 1280], replicated
- out_grad: float32 [1280, 1280], replicated
- up_grad: float32 [1280, 1280], replicated
- down_grad: float32 [1280, 1280], replicated
The draws below stay inside these ranges and needn't reach their ends.
Inputs may be any that keep to these rules, and one draw needn't show every extreme that they name: `lengths`: in every group of 4 consecutive items, one item uses all 2048 bytes; every item uses at least half of them.
All inputs are finite; a program needn't handle non-finite values.
Results may differ from the reference program's by a relative error of at most 0.02.
Values may be sent and summed in bfloat16 or wider, within the bound.
No kernel may reach another device: no remote copies, remote signals or barrier semaphores. Data moves between devices by JAX's collectives and lax.ppermute only.
A program may use at most 192 MiB of HBM per device.

```python
import jax
import jax.numpy as jnp
from jax import lax

CKV = 768
D = 1280
LATENTS = 256
HEADS = 8
QK = 256
V = 1280
FF = 1280
SLOT = 2048
ITEM_DEV = 4
ITEMS = 16
N_SEQ = 8


def draw_lengths(key, part):
    key = jax.random.fold_in(key, 7)
    key_base, key_pick = jax.random.split(key)
    length_base = jax.random.randint(key_base, (ITEMS,), SLOT // 2, SLOT + 1)
    chosen_one = jax.random.randint(key_pick, (ITEMS // ITEM_DEV,), 0, ITEM_DEV)
    positions = jnp.arange(ITEMS, dtype=jnp.int32)
    is_full = positions % ITEM_DEV == chosen_one[positions // ITEM_DEV]
    return jnp.where(is_full, SLOT, length_base).astype(jnp.int32)


def levels(own_key, extent, shards, low, top_value):
    def one(axis_at, blocks):
        heights = jax.random.uniform(jax.random.fold_in(jax.random.fold_in(own_key, 6), axis_at), (blocks,), jnp.float32, low / len(shards), top_value / len(shards))
        return jnp.repeat(jnp.exp(heights), extent[axis_at] // blocks).reshape((-1,) + (1,) * (len(extent) - axis_at - 1))

    gain = one(*shards[0])
    for cut in shards[1:]:
        gain = gain * one(*cut)
    return gain


def gaussian(rng, shape, scale, reach, cuts=(), kind=jnp.bfloat16):
    drawn = scale * jax.random.normal(rng, shape, jnp.float32)
    if cuts:
        drawn = drawn * levels(rng, shape, cuts, -0.22, 0.18)
    return jnp.clip(drawn, -reach, reach).astype(kind)


def setup_inputs(seed: int = 0) -> dict:
    splits = jax.random.split(jax.random.key(seed), 14)
    return {
        "byte_in": gaussian(splits[0], (ITEMS, SLOT, CKV), 1.0, 6.0, ((0, 4), (1, 8))),
        "lengths": draw_lengths(jax.random.fold_in(splits[13], 71), 0),
        "latent_init": gaussian(splits[2], (LATENTS, D), 1.0, 6.0),
        "gain_kv": jnp.clip(1.0 + 0.18 * jax.random.normal(splits[3], (CKV,), jnp.float32), 0.1, 1.9),
        "gain_q": jnp.clip(1.0 + 0.18 * jax.random.normal(splits[4], (D,), jnp.float32), 0.1, 1.9),
        "gain_mlp": jnp.clip(1.0 + 0.18 * jax.random.normal(splits[5], (D,), jnp.float32), 0.1, 1.9),
        "w_query": gaussian(splits[6], (D, QK), D ** -0.5, 0.15625),
        "w_key": gaussian(splits[7], (CKV, QK), CKV ** -0.5, 0.21875),
        "w_value": gaussian(splits[8], (CKV, V), CKV ** -0.5, 0.21875),
        "w_out": gaussian(splits[9], (V, D), (max(1, V * 8 // SLOT)) ** -0.5, 2.5),
        "w_up": gaussian(splits[10], (D, FF), D ** -0.5, 0.15625),
        "w_down": gaussian(splits[11], (FF, D), FF ** -0.5, 0.15625),
        "d_out": gaussian(splits[12], (ITEMS, LATENTS, D), 1.0, 6.0, ((0, 4),)),
    }


@jax.custom_vjp
def low(v):
    return lax.optimization_barrier(v.astype(jnp.bfloat16)).astype(jnp.float32)

@jax.custom_vjp
def low_back(v):
    return v

def low_keep(v):
    return (low(v), None)

def low_pass(kept, grad):
    return (grad,)

def back_keep(v):
    return (v, None)

def back_low(kept, grad):
    return (low(grad),)
low.defvjp(low_keep, low_pass)
low_back.defvjp(back_keep, back_low)
EPS = 1e-05
NEG = -1e+30
HIGH = lax.Precision.HIGHEST

def layer_norm(vector, gain_vec):
    average = lax.optimization_barrier(jnp.mean(vector, axis=-1, keepdims=True))
    centered = vector - average
    spread = lax.optimization_barrier(jnp.mean(centered * centered, axis=-1, keepdims=True))
    return centered * lax.rsqrt(spread + EPS) * gain_vec

def forward(byte_f, latent32, gain_kv, gain_q, gain_mlp, w_query, w_key, w_value, w_out, w_up, w_down, lengths):
    qk_size = QK // HEADS
    v_size = V // HEADS
    block_len = SLOT // N_SEQ
    lat_low = low(layer_norm(latent32, gain_q))
    queries = low_back(low(jnp.dot(lat_low, w_query, precision=HIGH)))
    query_heads = queries.reshape(LATENTS, HEADS, qk_size)

    def per_item(carry, inputs):
        byte_row, length_one = inputs
        byte_low = low(layer_norm(byte_row, gain_kv))
        key_proj = low_back(low(jnp.dot(byte_low, w_key, precision=HIGH)))
        value_proj = low_back(low(jnp.dot(byte_low, w_value, precision=HIGH)))
        scores = jnp.einsum('lhd,shd->hls', query_heads, key_proj.reshape(SLOT, HEADS, qk_size), precision=HIGH) * qk_size ** (-0.5)
        scores = low_back(scores)
        key_mask = jnp.arange(SLOT, dtype=jnp.int32) < length_one
        scores = jnp.where(key_mask[None, None, :], scores, NEG)
        row_max = lax.optimization_barrier(jnp.max(scores, axis=-1, keepdims=True))
        exponent = jnp.exp(scores - row_max)
        soft = low(exponent / lax.optimization_barrier(jnp.sum(exponent, axis=-1, keepdims=True)))
        soft_blocks = soft.reshape(HEADS, LATENTS, N_SEQ, block_len)
        value_blocks = value_proj.reshape(N_SEQ, block_len, HEADS, v_size)
        block_sum = low(jnp.einsum('hlns,nshd->nlhd', soft_blocks, value_blocks, precision=HIGH))
        attended = lax.optimization_barrier(jnp.sum(block_sum, axis=0)).reshape(LATENTS, V)
        attended = low_back(low(attended))
        mixed = latent32 + low_back(jnp.dot(attended, w_out, precision=HIGH))
        hidden_low = low(layer_norm(mixed, gain_mlp))
        upward = low_back(jnp.dot(hidden_low, w_up, precision=HIGH))
        activated = low(jax.nn.gelu(upward, approximate=False))
        return (carry, mixed + jnp.dot(activated, w_down, precision=HIGH))
    unused_carry, outputs = lax.scan(jax.checkpoint(per_item), jnp.zeros((), jnp.float32), (byte_f, lengths))
    return outputs

def reference(byte_in, lengths, latent_init, gain_kv, gain_q, gain_mlp, w_query, w_key, w_value, w_out, w_up, w_down, d_out):
    floats = tuple((tensor.astype(jnp.float32) for tensor in (byte_in, latent_init, gain_kv, gain_q, gain_mlp, w_query, w_key, w_value, w_out, w_up, w_down)))

    def wrapped(*params):
        return forward(*params, lengths)
    outputs, pull_back = jax.vjp(wrapped, *floats)
    grads = pull_back(d_out.astype(jnp.float32))
    return (outputs.astype(jnp.bfloat16), grads[0], grads[1], grads[2], grads[3], grads[4], grads[5], grads[6], grads[7], grads[8], grads[9], grads[10])
```

```python
import jax
import jax.numpy as jnp
from jax import lax
from jax.sharding import PartitionSpec as P

HEADS = 8
QK = 256
V = 1280
LSE_ROWS = 16
EPS = 1e-05
NEG = -1e30
f32 = jnp.float32
bf16 = jnp.bfloat16


def normalize(vector):
    average = jnp.mean(vector, axis=-1, keepdims=True)
    centered = vector - average
    inverse = lax.rsqrt(jnp.mean(centered * centered, axis=-1, keepdims=True) + EPS)
    return (centered * inverse, inverse)


def norm_back(grad_hat, hat_vec, inverse):
    return inverse * (
        grad_hat
        - jnp.mean(grad_hat, axis=-1, keepdims=True)
        - hat_vec * jnp.mean(grad_hat * hat_vec, axis=-1, keepdims=True)
    )


def exact_gelu(vector):
    return jax.nn.gelu(vector, approximate=False)


def pack_payload(sums, lse):
    high = lax.reduce_precision(lse, 8, 7)
    rest = lse - high
    return jnp.concatenate([sums.astype(bf16), high.astype(bf16), rest.astype(bf16)], axis=0)


def unpack_payload(payload):
    sums = payload[:V].astype(f32)
    high = payload[V : V + HEADS].astype(f32)
    return sums, high + payload[V + HEADS :].astype(f32)


def combine(first, second):
    sums_a, lse_a = unpack_payload(first)
    sums_b, lse_b = unpack_payload(second)
    top = jnp.maximum(lse_a, lse_b)
    weight_a = jnp.exp(lse_a - top)
    weight_b = jnp.exp(lse_b - top)
    total = weight_a + weight_b

    def spread(weight):
        return jnp.repeat(weight / total, V // HEADS, axis=0)

    sums = sums_a * spread(weight_a) + sums_b * spread(weight_b)
    return pack_payload(sums, top + jnp.log(total))


def swap_bit(array, axis, bit):
    size = lax.axis_size(axis)
    return lax.ppermute(array, axis, [(i, i ^ (1 << bit)) for i in range(size)])


def bit_of(axis, bit):
    return (lax.axis_index(axis) >> bit) & 1


def all_combine(halves):
    size = lax.axis_size("seq")
    low = bit_of("seq", 0)
    keep = lax.dynamic_index_in_dim(halves, low, 0, keepdims=False)
    send = lax.dynamic_index_in_dim(halves, 1 - low, 0, keepdims=False)
    mine = combine(keep, swap_bit(send, "seq", 0))
    if size == 8:
        place = lax.axis_index("seq") >> 1
        inward = lax.ppermute(mine, "seq", [(0, 2), (1, 3), (6, 4), (7, 5)])
        mine = combine(mine, inward)
        across = lax.ppermute(mine, "seq", [(2, 4), (3, 5), (4, 2), (5, 3)])
        mine = combine(
            jnp.where(place == 1, mine, across), jnp.where(place == 1, across, mine)
        )
        outward = lax.ppermute(mine, "seq", [(2, 0), (3, 1), (4, 6), (5, 7)])
        mine = jnp.where((place == 1) | (place == 2), mine, outward)
    else:
        bit = 1
        while (1 << bit) < size:
            other = swap_bit(mine, "seq", bit)
            is_low = bit_of("seq", bit) == 0
            mine = combine(
                jnp.where(is_low, mine, other), jnp.where(is_low, other, mine)
            )
            bit += 1
    other = swap_bit(mine, "seq", 0)
    return jnp.where(
        low == 0,
        jnp.concatenate([mine, other], axis=1),
        jnp.concatenate([other, mine], axis=1),
    )


def bits_of(axis):
    count = lax.axis_size(axis).bit_length() - 1
    return [(axis, bit) for bit in range(count)]


def scatter_sum(blocks, steps, names):
    left = list(names)
    for axis, bit in steps:
        at = left.index((axis, bit))
        mine = bit_of(axis, bit)
        keep = lax.dynamic_index_in_dim(blocks, mine, at, keepdims=False)
        send = lax.dynamic_index_in_dim(blocks, 1 - mine, at, keepdims=False)
        got = swap_bit(send, axis, bit)
        blocks = (keep.astype(f32) + got.astype(f32)).astype(bf16)
        left.pop(at)
    return blocks


def per_device(
    byte_in,
    lengths,
    latent_init,
    gain_kv,
    gain_q,
    gain_mlp,
    w_query,
    w_key,
    w_value,
    w_out,
    w_up,
    w_down,
    d_out,
):
    item_count, slot_local, byte_width = byte_in.shape
    latent_count, lat_width = latent_init.shape
    ff_width = w_up.shape[1]
    n_item = lax.axis_size("item")
    n_seq = lax.axis_size("seq")
    qk_size = QK // HEADS
    v_size = V // HEADS
    score_scale = qk_size ** (-0.5)
    seq_rank = lax.axis_index("seq")
    lat_float = latent_init.astype(f32)
    lat_hat, lat_inverse = normalize(lat_float)
    lat_low = (lat_hat * gain_q).astype(bf16)
    queries = jnp.dot(lat_low, w_query, preferred_element_type=f32).astype(bf16)
    query_heads = queries.reshape(latent_count, HEADS, qk_size)
    byte_hat, byte_inverse = normalize(byte_in.astype(f32))
    byte_low = (byte_hat * gain_kv).astype(bf16)
    key_proj = jnp.einsum("isc,ck->isk", byte_low, w_key, preferred_element_type=f32).astype(bf16)
    value_proj = jnp.einsum("isc,ck->isk", byte_low, w_value, preferred_element_type=f32).astype(
        bf16
    )
    key_heads = key_proj.reshape(item_count, slot_local, HEADS, qk_size)
    value_heads = value_proj.reshape(item_count, slot_local, HEADS, v_size)
    positions = seq_rank * slot_local + jnp.arange(slot_local, dtype=jnp.int32)
    key_mask = positions[None, :] < lengths[:, None]

    raw_scores = (
        jnp.einsum("lhd,ishd->ihsl", query_heads, key_heads, preferred_element_type=f32)
        * score_scale
    )
    scores = jnp.where(key_mask[:, None, :, None], raw_scores, NEG)
    local_max = jnp.max(scores, axis=2, keepdims=True)
    powers = jnp.exp(scores - local_max)
    local_total = jnp.sum(powers, axis=2, keepdims=True)
    local_sums = jnp.einsum(
        "ihsl,ishd->ihdl", powers.astype(bf16), value_heads, preferred_element_type=f32
    )
    local_sums = (local_sums / local_total).reshape(item_count, V, latent_count)
    local_lse = (local_max + jnp.log(local_total)).reshape(item_count, HEADS, latent_count)
    half = latent_count // 2
    attended_items = []
    lse_items = []
    for item in range(item_count):
        payload = pack_payload(local_sums[item], local_lse[item])
        whole = all_combine(jnp.stack([payload[:, :half], payload[:, half:]]))
        attended_items.append(whole[:V])
        lse_items.append(unpack_payload(whole)[1])
    attn_low = jnp.swapaxes(jnp.stack(attended_items), 1, 2)
    lse = jnp.stack(lse_items)

    mixed = lat_float[None] + jnp.einsum("ilk,kd->ild", attn_low, w_out, preferred_element_type=f32)
    mix_hat, mix_inverse = normalize(mixed)
    hidden_low = (mix_hat * gain_mlp).astype(bf16)
    upward = jnp.einsum("ild,df->ilf", hidden_low, w_up, preferred_element_type=f32)
    activated, gelu_back = jax.vjp(exact_gelu, upward)
    act_low = activated.astype(bf16)
    latents_out = (
        mixed + jnp.einsum("ilf,fd->ild", act_low, w_down, preferred_element_type=f32)
    ).astype(bf16)
    grad_act = jnp.einsum("ild,fd->ilf", d_out, w_down, preferred_element_type=f32)
    grad_up = gelu_back(grad_act)[0].astype(bf16)
    grad_hidden = jnp.einsum("ilf,df->ild", grad_up, w_up, preferred_element_type=f32)
    grad_mixed = d_out.astype(f32) + norm_back(grad_hidden * gain_mlp, mix_hat, mix_inverse)
    grad_branch = grad_mixed.astype(bf16)
    grad_attn = jnp.einsum("ild,kd->ilk", grad_branch, w_out, preferred_element_type=f32).astype(
        bf16
    )

    def columns_of(tensor):
        width = tensor.shape[-1] // n_seq
        return lax.dynamic_slice_in_dim(tensor, seq_rank * width, width, tensor.ndim - 1)

    out_part = jnp.einsum(
        "ilk,ild->kd", columns_of(attn_low), grad_branch, preferred_element_type=f32
    )
    up_part = jnp.einsum(
        "ild,ilf->df", columns_of(hidden_low), grad_up, preferred_element_type=f32
    )
    down_part = jnp.einsum("ilf,ild->fd", columns_of(act_low), d_out, preferred_element_type=f32)
    share = latent_count // n_seq
    resid_part = jnp.sum(
        lax.dynamic_slice_in_dim(grad_mixed, seq_rank * share, share, 1), axis=0
    )
    mlp_part = jnp.sum(grad_hidden * mix_hat, axis=(0, 1)) / n_seq
    matrices = (out_part, up_part, down_part, resid_part)
    share_rows = [part.shape[0] // n_item for part in matrices]
    latent_side = jnp.concatenate(
        [
            part.astype(bf16).reshape(n_item, rows, lat_width)
            for part, rows in zip(matrices, share_rows)
        ],
        axis=1,
    )
    item_bits = bits_of("item")
    seq_bits = bits_of("seq")
    latent_side = latent_side.reshape((2,) * len(item_bits) + latent_side.shape[1:])
    latent_piece = scatter_sum(latent_side, item_bits, item_bits[::-1])
    latent_all = lax.all_gather(latent_piece, ("item", "seq"), axis=0, tiled=False)

    grad_heads = grad_attn.reshape(item_count, latent_count, HEADS, v_size)
    row_dot = jnp.einsum(
        "ilhd,ilhd->ihl",
        grad_heads.astype(f32),
        attn_low.reshape(item_count, latent_count, HEADS, v_size).astype(f32),
    )
    soft = jnp.exp(scores - lse[:, :, None, :])
    soft_low = soft.astype(bf16)
    grad_soft = jnp.einsum("ilhd,ishd->ihsl", grad_heads, value_heads, preferred_element_type=f32)
    grad_scores = (soft * (grad_soft - row_dot[:, :, None, :])).astype(bf16)
    query_part = jnp.einsum(
        "ihsl,ishd->lhd", grad_scores, key_heads, preferred_element_type=f32
    ).reshape(latent_count, QK)
    grad_keys = (
        (
            jnp.einsum("ihsl,lhd->ishd", grad_scores, query_heads, preferred_element_type=f32)
            * score_scale
        )
        .astype(bf16)
        .reshape(item_count, slot_local, QK)
    )
    grad_values = (
        jnp.einsum("ihsl,ilhd->ishd", soft_low, grad_heads, preferred_element_type=f32)
        .astype(bf16)
        .reshape(item_count, slot_local, V)
    )
    grad_byte_low = jnp.einsum(
        "isk,ck->isc", grad_keys, w_key, preferred_element_type=f32
    ) + jnp.einsum("isk,ck->isc", grad_values, w_value, preferred_element_type=f32)
    gain_kv_part = jnp.sum(grad_byte_low * byte_hat, axis=(0, 1))
    byte_grad = norm_back(grad_byte_low * gain_kv, byte_hat, byte_inverse)
    key_part = jnp.einsum("isc,isk->ck", byte_low, grad_keys, preferred_element_type=f32)
    value_part = jnp.einsum("isc,isk->ck", byte_low, grad_values, preferred_element_type=f32)

    key_blocks = byte_width // QK
    gains = jnp.concatenate([gain_kv_part, mlp_part]).reshape(-1, QK)
    gains = jnp.pad(gains, ((0, QK - gains.shape[0]), (0, 0)))
    lower = jnp.concatenate(
        [key_part[i * QK : (i + 1) * QK] for i in range(key_blocks)] + [query_part, gains], axis=1
    )
    byte_side = jnp.concatenate([value_part, lower], axis=0).astype(bf16)
    all_bits = item_bits + seq_bits
    names = item_bits[::-1] + seq_bits[::-1]
    byte_side = byte_side.reshape(
        (2,) * len(names) + (byte_side.shape[0] // (1 << len(names)), V)
    )
    byte_piece = scatter_sum(byte_side, all_bits, names)
    byte_all = lax.all_gather(byte_piece, ("item", "seq"), axis=0, tiled=True)

    value_grad = byte_all[:byte_width].astype(f32)
    lower_sum = byte_all[byte_width:].astype(f32)
    key_grad = jnp.concatenate(
        [lower_sum[:, i * QK : (i + 1) * QK] for i in range(key_blocks)], axis=0
    )
    query_sum = lower_sum[:, byte_width : byte_width + QK]
    gain_rows = lower_sum[:, byte_width + QK :].reshape(-1)
    gain_kv_grad = gain_rows[:byte_width]
    gain_mlp_grad = gain_rows[byte_width : byte_width + lat_width]

    def assemble(first, rows):
        block = latent_all[:, first : first + rows].reshape(n_item, n_seq, rows, lat_width)
        return jnp.swapaxes(block, 0, 1).reshape(-1, lat_width).astype(f32)

    firsts = [sum(share_rows[:i]) for i in range(4)]
    out_grad, up_grad, down_grad, resid_sum = [
        assemble(first, rows) for first, rows in zip(firsts, share_rows)
    ]
    query_low = (query_sum * score_scale).astype(bf16)
    grad_lat_low = jnp.einsum("lk,dk->ld", query_low, w_query, preferred_element_type=f32)
    query_grad = jnp.einsum("ld,lk->dk", lat_low, query_low, preferred_element_type=f32)
    gain_q_grad = jnp.sum(grad_lat_low * lat_hat, axis=0)
    latent_grad = resid_sum + norm_back(grad_lat_low * gain_q, lat_hat, lat_inverse)
    return (
        latents_out,
        byte_grad,
        latent_grad,
        gain_kv_grad,
        gain_q_grad,
        gain_mlp_grad,
        query_grad,
        key_grad,
        value_grad,
        out_grad,
        up_grad,
        down_grad,
    )


def solution(mesh):
    placed = (P("item", "seq", None), P("item")) + (P(),) * 10 + (P("item", None, None),)
    return jax.shard_map(
        per_device,
        mesh=mesh,
        in_specs=placed,
        out_specs=(P("item", None, None), P("item", "seq", None)) + (P(),) * 10,
        check_vma=False,
    )
```

```python
import functools

import jax
import jax.numpy as jnp
from jax import lax
from jax.experimental import pallas as pl
from jax.experimental.pallas import tpu as pltpu
from jax.sharding import PartitionSpec as P

HEADS = 8
QK = 256
V = 1280
QK_HEAD = QK // HEADS
V_HEAD = V // HEADS
SCALE = QK_HEAD**-0.5
ROWS = V + 2 * HEADS
EPS = 1e-05
NEG = -1e30
MIB = 1 << 20
f32 = jnp.float32
bf16 = jnp.bfloat16

IN_VMEM = pl.BlockSpec(memory_space=pltpu.VMEM)
IN_SMEM = pl.BlockSpec(memory_space=pltpu.SMEM)
ANYWHERE = pl.BlockSpec(memory_space=pl.ANY)


def dot(a, b):
    return jnp.dot(a, b, preferred_element_type=f32)


def dot_nt(a, b):
    return lax.dot_general(a, b, (((1,), (1,)), ((), ())), preferred_element_type=f32)


def shape(dims, dtype):
    return jax.ShapeDtypeStruct(dims, dtype)


def cost(flops, moved, powers=0):
    return pl.CostEstimate(flops=flops, bytes_accessed=moved, transcendentals=powers)


class Chain:
    def __init__(self, place):
        self.place = place
        self.token = jnp.zeros((8, 128), f32)

    def launch(self, kernel, inputs, specs, outs, out_specs, mib, price, name, scratch=(), aliases=None, grid=(1,)):
        count = len(inputs) + 1

        def body(*refs):
            refs[count + 1 + len(outs)][...] = jnp.zeros((8, 128), f32)
            kernel(*refs[:count], *refs[count + 1 : count + 1 + len(outs)], *refs[count + 2 + len(outs) :])

        *results, self.token = pl.pallas_call(
            body,
            grid=grid,
            out_shape=[*outs, shape((8, 128), f32)],
            in_specs=[IN_SMEM, *specs, ANYWHERE],
            out_specs=[*out_specs, whole(8, 128)],
            scratch_shapes=scratch,
            input_output_aliases=aliases or {},
            compiler_params=pltpu.CompilerParams(vmem_limit_bytes=mib * MIB),
            cost_estimate=price,
            name=name,
        )(self.place, *inputs, self.token)
        return results


def whole(*dims):
    return pl.BlockSpec(dims, lambda i: (0,) * len(dims))


def at_item(item, *dims):
    return pl.BlockSpec((1,) + dims, lambda i: (item,) + (0,) * len(dims))


def place_bit(place_ref, axis, bit):
    return (place_ref[0 if axis == "seq" else 1] >> bit) & 1


def normalize(vector, axis=-1):
    average = jnp.mean(vector, axis=axis, keepdims=True)
    centered = vector - average
    inverse = lax.rsqrt(jnp.mean(centered * centered, axis=axis, keepdims=True) + EPS)
    return (centered * inverse, inverse)


def norm_back(grad_hat, hat, inverse, axis=-1):
    return inverse * (
        grad_hat
        - jnp.mean(grad_hat, axis=axis, keepdims=True)
        - hat * jnp.mean(grad_hat * hat, axis=axis, keepdims=True)
    )


def query_kernel(place_ref, lat_ref, gain_ref, wq_ref, q_ref):
    hat, _ = normalize(lat_ref[...].astype(f32))
    lat_low = (hat * gain_ref[...]).astype(bf16)
    q_ref[...] = dot(lat_low, wq_ref[...]).T.astype(bf16)


def make_queries(chain, latent_init, gain_q, w_query):
    latents, width = latent_init.shape
    return chain.launch(
        query_kernel,
        (latent_init, gain_q[None, :], w_query),
        [whole(latents, width), whole(1, width), whole(width, QK)],
        [shape((QK, latents), bf16)],
        [whole(QK, latents)],
        16,
        cost(2 * latents * width * QK, 4 * latents * width),
        "queries",
    )[0]


def head_queries(q_t, head):
    channel = lax.broadcasted_iota(jnp.int32, q_t.shape, 0)
    return jnp.where(channel // QK_HEAD == head, q_t, jnp.zeros_like(q_t))


def attend_kernel(item, place_ref, x_ref, gain_ref, wk_ref, wv_ref, q_ref, *refs):
    k_ref, v_ref, keep_ref, send_ref = refs[-4:]
    low = place_bit(place_ref, "seq", 0)
    limit = place_ref[2 + item] - place_ref[0] * x_ref.shape[1]
    hat, _ = normalize(x_ref[0].astype(f32))
    byte_low = (hat * gain_ref[...]).astype(bf16)
    keys = dot(byte_low, wk_ref[...]).astype(bf16)
    values = dot(byte_low, wv_ref[...])
    k_ref[0] = keys
    v_ref[0] = values.astype(bf16)
    values_t = values.T.astype(bf16)
    q_t = q_ref[...]
    latents = q_t.shape[1]
    half = latents // 2
    inside = lax.broadcasted_iota(jnp.int32, (keys.shape[0], latents), 0) < limit

    def put(first, block):
        left, right = block[:, :half], block[:, half:]
        rows = pl.ds(first, block.shape[0])
        keep_ref[rows, :] = jnp.where(low == 0, left, right).astype(bf16)
        send_ref[rows, :] = jnp.where(low == 0, right, left).astype(bf16)

    totals = []
    for head in range(HEADS):
        scores = dot(keys, head_queries(q_t, head)) * SCALE
        scores = jnp.where(inside, scores, NEG)
        top = jnp.max(scores, axis=0, keepdims=True)
        powers = jnp.exp(scores - top)
        total = jnp.sum(powers, axis=0, keepdims=True)
        rows = slice(head * V_HEAD, (head + 1) * V_HEAD)
        put(head * V_HEAD, dot(values_t[rows], powers.astype(bf16)) * (1.0 / total))
        totals.append(top + jnp.log(total))
    lse = jnp.concatenate(totals, axis=0)
    high = lse.astype(bf16).astype(f32)
    put(V, jnp.concatenate([high, lse - high], axis=0))


def attend(chain, item, byte_in, gain_kv, w_key, w_value, q_t, stacks):
    items, slot, width = byte_in.shape
    latents = q_t.shape[1]
    half = latents // 2
    inputs = [byte_in, gain_kv, w_key, w_value, q_t, *stacks]
    specs = [at_item(item, slot, width)] + [whole(*array.shape) for array in inputs[1:5]]
    return chain.launch(
        functools.partial(attend_kernel, item),
        inputs,
        specs + [ANYWHERE] * len(stacks),
        [
            shape((items, slot, QK), bf16),
            shape((items, slot, V), bf16),
            shape((ROWS, half), bf16),
            shape((ROWS, half), bf16),
        ],
        [at_item(item, slot, QK), at_item(item, slot, V), whole(ROWS, half), whole(ROWS, half)],
        24,
        cost(2 * slot * (width * (QK + V) + 4 * QK * latents * 4), 5 * MIB),
        "attend",
        aliases={6: 0, 7: 1} if stacks else None,
    )


def merge_kernel(bit, place_ref, mine_ref, other_ref, out_ref):
    swap = place_bit(place_ref, "seq", bit) != 0

    def totals(ref):
        return ref[V : V + HEADS, :].astype(f32) + ref[V + HEADS :, :].astype(f32)

    def ordered(mine, other):
        return jnp.where(swap, other, mine), jnp.where(swap, mine, other)

    lse_a, lse_b = ordered(totals(mine_ref), totals(other_ref))
    top = jnp.maximum(lse_a, lse_b)
    weight_a = jnp.exp(lse_a - top)
    weight_b = jnp.exp(lse_b - top)
    total = weight_a + weight_b
    lse = top + jnp.log(total)
    weight_a = weight_a / total
    weight_b = weight_b / total
    for head in range(HEADS):
        rows = pl.ds(head * V_HEAD, V_HEAD)
        sums_a, sums_b = ordered(mine_ref[rows, :].astype(f32), other_ref[rows, :].astype(f32))
        out_ref[rows, :] = (
            sums_a * weight_a[head : head + 1] + sums_b * weight_b[head : head + 1]
        ).astype(bf16)
    high = lse.astype(bf16).astype(f32)
    out_ref[pl.ds(V, 2 * HEADS), :] = jnp.concatenate([high, lse - high], axis=0).astype(bf16)


def merge(chain, bit, mine, other):
    return chain.launch(
        functools.partial(merge_kernel, bit),
        (mine, other),
        [whole(*mine.shape)] * 2,
        [shape(mine.shape, bf16)],
        [whole(*mine.shape)],
        8,
        cost(8 * mine.size, 6 * mine.size),
        "merge",
    )[0]


def choose_kernel(place_ref, mine_ref, other_ref, out_ref):
    line = place_ref[0] >> 1
    inner = (line == 1) | (line == 2)
    out_ref[...] = jnp.where(inner, mine_ref[...], other_ref[...])


def choose(chain, mine, other):
    return chain.launch(
        choose_kernel,
        (mine, other),
        [whole(*mine.shape)] * 2,
        [shape(mine.shape, bf16)],
        [whole(*mine.shape)],
        8,
        cost(mine.size, 6 * mine.size),
        "choose",
    )[0]


def cotangent_kernel(place_ref, g_ref, w_ref, act_ref):
    for rows in range(0, w_ref.shape[0], TILE):
        act_ref[0, :, pl.ds(rows, TILE)] = dot_nt(g_ref[0], w_ref[pl.ds(rows, TILE), :])


def cotangents(chain, d_out, w_down):
    items, latents, width = d_out.shape
    ff = w_down.shape[0]
    return chain.launch(
        cotangent_kernel,
        (d_out, w_down),
        [pl.BlockSpec((1, latents, width), lambda i: (i, 0, 0)), whole(ff, width)],
        [shape((items, latents, ff), f32)],
        [pl.BlockSpec((1, latents, ff), lambda i: (i, 0, 0))],
        32,
        cost(2 * items * latents * width * ff, 12 * MIB),
        "cotangents",
        grid=(items,),
    )[0]


TILE = 256
ROOT_HALF = 0.7071067811865476
ROOT_TWO_PI = 0.3989422804014327


def latent_kernel(first, last, place_ref, mine_ref, other_ref, lat_ref, gain_ref, g_ref, act_ref, *refs):
    hbm, refs = refs[:3], refs[3:]
    if not first:
        acc_in, mlp_in, refs = refs[0], refs[1], refs[5:]
    out_ref, ga_ref, stat_ref, mlp_ref, refs = refs[0], refs[1], refs[2], refs[3], refs[4:]
    if last:
        keep_ref, send_ref, refs = refs[0], refs[1], refs[2:]
    else:
        acc_ref, refs = refs[0], refs[1:]
    held, (att_s, turn_s, branch_s, sum_s, sems) = refs[:3], refs[3:]
    copies = [pltpu.make_async_copy(src, dst, sems.at[i]) for i, (src, dst) in enumerate(zip(hbm, held))]
    for copy in copies:
        copy.start()
    w_out, w_up, w_down = held
    low, rank, core = place_bit(place_ref, "seq", 0), place_ref[0], place_bit(place_ref, "item", 0)
    latents, width = lat_ref.shape
    ff = act_ref.shape[2]
    share = sum_s.shape[0]
    mine, other = mine_ref[...], other_ref[...]
    left = jnp.where(low == 0, mine, other)
    right = jnp.where(low == 0, other, mine)
    whole = jnp.concatenate([left, right], axis=1)
    att_s[...] = whole[:V]
    stat_ref[0, :HEADS, :] = whole[V : V + HEADS].astype(f32) + whole[V + HEADS :].astype(f32)
    attended = whole[:V].T
    rows = pl.ds(pl.multiple_of(rank * share, 16), share)
    target = sum_s if last else acc_ref

    def add(part, at, size):
        target[:, pl.ds(at, size)] = part if first else part + acc_in[:, pl.ds(at, size)]

    copies[0].wait()
    mixed = lat_ref[...].astype(f32) + jnp.concatenate(
        [dot(attended, w_out[:, pl.ds(at, TILE)]) for at in range(0, width, TILE)], axis=1
    )
    hat, inverse = normalize(mixed)
    gain = gain_ref[...]
    hidden = (hat * gain).astype(bf16)
    copies[1].wait()
    activated, grad_up = [], []
    for at in range(0, ff, TILE):
        upward = dot(hidden, w_up[:, pl.ds(at, TILE)])
        bell = 0.5 + 0.5 * lax.erf(upward * ROOT_HALF)
        slope = bell + upward * (ROOT_TWO_PI * jnp.exp(-0.5 * upward * upward))
        activated.append((upward * bell).astype(bf16))
        grad_up.append((act_ref[0, :, pl.ds(at, TILE)] * slope).astype(bf16))
    activated = jnp.concatenate(activated, axis=1)
    grad_up = jnp.concatenate(grad_up, axis=1)
    copies[2].wait()
    for at in range(0, width, TILE):
        block = mixed[:, at : at + TILE] + dot(activated, w_down[:, pl.ds(at, TILE)])
        out_ref[0, :, pl.ds(at, TILE)] = block.astype(bf16)
    turn_s[...] = activated.T
    add(dot(turn_s[rows, :], g_ref[0]), width + ff, width)
    grad_hidden = jnp.concatenate(
        [dot_nt(grad_up, w_up[pl.ds(at, TILE), :]) for at in range(0, width, TILE)], axis=1
    )
    turn_s[...] = hidden.T
    add(dot(turn_s[rows, :], grad_up), width, ff)
    mlp = jnp.sum(grad_hidden * hat, axis=0, keepdims=True)
    mlp_ref[...] = mlp if first else mlp + mlp_in[...]
    grad_mixed = g_ref[0].astype(f32) + norm_back(grad_hidden * gain, hat, inverse)
    branch = grad_mixed.astype(bf16)
    branch_s[...] = branch
    add(dot(att_s[rows, :], branch), 0, width)
    slab = latents * share // width
    few = pl.ds(pl.multiple_of(rank * slab, 16), slab)
    add(
        jnp.concatenate(
            [branch_s[few, pl.ds(at, latents)] for at in range(0, width, latents)], axis=0
        ).astype(f32),
        2 * width + ff,
        latents,
    )
    for at in range(0, V, TILE):
        ga_ref[0, pl.ds(at, TILE), :] = dot_nt(w_out[pl.ds(at, TILE), :], branch).astype(bf16)
    for head in range(HEADS):
        part = pl.ds(head * V_HEAD, V_HEAD)
        stat_ref[0, pl.ds(HEADS + head, 1), :] = jnp.sum(
            ga_ref[0, part, :].astype(f32) * att_s[part, :].astype(f32), axis=0, keepdims=True
        )
    if last:
        half = share // 2
        kept = pl.ds(pl.multiple_of(core * half, 8), half)
        sent = pl.ds(pl.multiple_of((1 - core) * half, 8), half)
        keep_ref[...] = sum_s[kept, :].astype(bf16)
        send_ref[...] = sum_s[sent, :].astype(bf16)


def latent_step(chain, item, share, mine, other, lat, gain, g, act, weights, carried):
    items, latents, width = g.shape
    ff = act.shape[2]
    total = 2 * width + ff + latents
    first, last = item == 0, item == items - 1
    inputs = [mine, other, lat, gain, g, act, *weights]
    specs = [whole(*array.shape) for array in inputs[:4]]
    specs += [at_item(item, latents, width), at_item(item, latents, ff)] + [ANYWHERE] * 3
    aliases = {}
    if not first:
        acc, mlp, *stacks = carried
        aliases = {12 + i: i for i in range(3)}
        inputs += [acc, mlp, *stacks]
        specs += [whole(*acc.shape), whole(*mlp.shape)] + [ANYWHERE] * 3
    outs = [
        shape((items, latents, width), bf16),
        shape((items, V, latents), bf16),
        shape((items, 2 * HEADS, latents), f32),
        shape((1, width), f32),
    ]
    out_specs = [
        at_item(item, latents, width),
        at_item(item, V, latents),
        at_item(item, 2 * HEADS, latents),
        whole(1, width),
    ]
    if last:
        outs += [shape((share // 2, total), bf16)] * 2
        out_specs += [whole(share // 2, total)] * 2
    else:
        outs += [shape((share, total), f32)]
        out_specs += [whole(share, total)]
    return chain.launch(
        functools.partial(latent_kernel, first, last),
        inputs,
        specs,
        outs,
        out_specs,
        56,
        cost(10 * latents * width * ff, 24 * MIB),
        "latent_step",
        scratch=[pltpu.VMEM(w.shape, bf16) for w in weights]
        + [
            pltpu.VMEM((V, latents), bf16),
            pltpu.VMEM((width, latents), bf16),
            pltpu.VMEM((latents, width), bf16),
            pltpu.VMEM((share, total), f32),
            pltpu.SemaphoreType.DMA((3,)),
        ],
        aliases=aliases,
    )


def bytes_kernel(
    start, last, mlp_scale, place_ref, x_ref, gain_ref, wk_ref, wv_ref, q_ref, k_ref, v_ref, ga_ref, stat_ref, *refs
):
    step = pl.program_id(0)
    if start:
        begin_ref, gain_begin_ref, _, *refs = refs
    if last:
        mlp_ref, grad_ref, keep_ref, send_ref, sum_s, gain_s = refs
    else:
        grad_ref, sum_s, gain_s = refs
    core = place_bit(place_ref, "item", 0)
    slot, width = x_ref.shape[1:]
    limit = place_ref[2 + start + step] - place_ref[0] * slot
    hat, inverse = normalize(x_ref[0].astype(f32))
    gain = gain_ref[...]
    low_t = (hat * gain).T.astype(bf16)
    keys = k_ref[0]
    values = v_ref[0]
    keys_t = keys.T
    q_t = q_ref[...]
    latents = q_t.shape[1]
    inside = lax.broadcasted_iota(jnp.int32, (slot, latents), 0) < limit

    @pl.when(step == 0)
    def _():
        if start:
            sum_s[...] = begin_ref[...]
            gain_s[...] = gain_begin_ref[...]
        else:
            sum_s[...] = jnp.zeros_like(sum_s)
            gain_s[...] = jnp.zeros_like(gain_s)

    grad_values, grad_keys = [], []
    for head in range(HEADS):
        scores = dot(keys, head_queries(q_t, head)) * SCALE
        scores = jnp.where(inside, scores, NEG)
        soft = jnp.exp(scores - stat_ref[0, pl.ds(head, 1), :])
        part = slice(head * V_HEAD, (head + 1) * V_HEAD)
        small = slice(head * QK_HEAD, (head + 1) * QK_HEAD)
        grad_attn = ga_ref[0, pl.ds(head * V_HEAD, V_HEAD), :]
        grad_soft = dot(values[:, part], grad_attn)
        grad_scores = (soft * (grad_soft - stat_ref[0, pl.ds(HEADS + head, 1), :])).astype(bf16)
        grad_values.append(dot_nt(grad_attn, soft.astype(bf16)).astype(bf16))
        grad_keys.append((dot_nt(q_t[small], grad_scores) * SCALE).astype(bf16))
        sum_s[pl.ds(width + head * QK_HEAD, QK_HEAD), pl.ds(width, latents)] += dot(
            keys_t[small], grad_scores
        )
    grad_values = jnp.concatenate(grad_values, axis=0)
    grad_keys = jnp.concatenate(grad_keys, axis=0)
    grad_low = (dot(wv_ref[...], grad_values) + dot(wk_ref[...], grad_keys)).T
    gain_s[...] += jnp.sum(grad_low * hat, axis=0, keepdims=True)
    grad_ref[0] = norm_back(grad_low * gain, hat, inverse)
    for rows in range(0, width, TILE):
        block = low_t[rows : rows + TILE]
        sum_s[pl.ds(rows, TILE), :] += dot_nt(block, grad_values)
        sum_s[pl.ds(width, QK), pl.ds(rows, TILE)] += dot_nt(block, grad_keys)

    if not last:
        return

    @pl.when(step == pl.num_programs(0) - 1)
    def _():
        parts = [gain_s[...], mlp_ref[...] * mlp_scale]
        lanes = pl.ds(width + latents, QK)
        at = width
        for part in parts:
            for first in range(0, part.shape[1], QK):
                sum_s[pl.ds(at, 1), lanes] = part[:, first : first + QK]
                at += 1
        half = sum_s.shape[0] // 2
        keep_ref[...] = sum_s[pl.ds(pl.multiple_of(core * half, 16), half), :].astype(bf16)
        send_ref[...] = sum_s[pl.ds(pl.multiple_of((1 - core) * half, 16), half), :].astype(bf16)


def bytes_step(chain, start, count, byte_in, gain_kv, w_key, w_value, q_t, keys, values, ga, stats, begun, mlp, mlp_scale):
    items, slot, width = byte_in.shape
    latents = q_t.shape[1]
    rows = width + QK
    last = start + count == items
    block = lambda *dims: pl.BlockSpec((1,) + dims, lambda i: (start + i, 0, 0))
    flops = 2 * count * slot * (2 * width * (QK + V) + latents * (5 * 256 * HEADS))
    inputs = [byte_in, gain_kv, w_key, w_value, q_t, keys, values, ga, stats]
    specs = [block(slot, width)] + [whole(*array.shape) for array in inputs[1:5]]
    specs += [block(slot, QK), block(slot, V), block(V, latents), block(2 * HEADS, latents)]
    aliases = {}
    if start:
        grads, total, gains = begun
        inputs += [total, gains, grads]
        specs += [whole(rows, V), whole(1, width), ANYWHERE]
        aliases = {12: 0}
    outs = [shape((items, slot, width), f32)]
    out_specs = [block(slot, width)]
    scratch = [pltpu.VMEM((rows, V), f32), pltpu.VMEM((1, width), f32)]
    if last:
        inputs += [mlp]
        specs += [whole(1, V)]
        outs += [shape((rows // 2, V), bf16)] * 2
        out_specs += [whole(rows // 2, V)] * 2
    else:
        outs += [shape((rows, V), f32), shape((1, width), f32)]
        out_specs += [whole(rows, V), whole(1, width)]
        scratch = []
    return chain.launch(
        functools.partial(bytes_kernel, start, last, mlp_scale),
        inputs,
        specs,
        outs,
        out_specs,
        52,
        cost(flops, 16 * MIB),
        "bytes_step",
        scratch=scratch,
        aliases=aliases,
        grid=(count,),
    )


def swap_bit(array, axis, bit):
    size = lax.axis_size(axis)
    return lax.ppermute(array, axis, [(i, i ^ (1 << bit)) for i in range(size)])


def bit_of(axis, bit):
    return (lax.axis_index(axis) >> bit) & 1


def bits_of(axis):
    return [(axis, bit) for bit in range(lax.axis_size(axis).bit_length() - 1)]


def split_kernel(step, place_ref, keep_ref, got_ref, kept_ref, sent_ref):
    half = kept_ref.shape[0]
    upper = place_bit(place_ref, *step) != 0
    total = (keep_ref[...].astype(f32) + got_ref[...].astype(f32)).astype(bf16)
    kept_ref[...] = jnp.where(upper, total[half:], total[:half])
    sent_ref[...] = jnp.where(upper, total[:half], total[half:])


def split_sum(chain, step, keep, got, stream=0, streams=1):
    rows, width = keep.shape[0] // streams, keep.shape[1]
    half = rows // 2
    if half % 8 == 0:
        block = pl.BlockSpec((rows, width), lambda i: (stream, 0))
        return chain.launch(
            functools.partial(split_kernel, step),
            (keep, got),
            [block] * 2,
            [shape((half, width), bf16)] * 2,
            [whole(half, width)] * 2,
            16,
            cost(rows * width, 6 * rows * width),
            "split_sum",
        )
    total = (keep.astype(f32) + got.astype(f32)).astype(bf16)
    total = total[stream * rows : (stream + 1) * rows]
    take = lambda side: lax.dynamic_slice_in_dim(total, side * half, half, 0)
    bit = bit_of(*step)
    return take(bit), take(1 - bit)


def sum_kernel(place_ref, keep_ref, got_ref, out_ref):
    out_ref[...] = (keep_ref[...].astype(f32) + got_ref[...].astype(f32)).astype(bf16)


def plain_sum(chain, keep, got):
    return chain.launch(
        sum_kernel,
        (keep, got),
        [whole(*keep.shape)] * 2,
        [shape(keep.shape, bf16)],
        [whole(*keep.shape)],
        8,
        cost(keep.size, 6 * keep.size),
        "plain_sum",
    )[0]


def place_kernel(held_ref, *refs):
    block = held_ref[0].astype(f32)
    at = 0
    for ref in refs:
        ref[...] = block[:, at : at + ref.shape[1]]
        at += ref.shape[1]


def place_blocks(blocks, n_item, n_seq, widths):
    count, rows, total = blocks.shape
    bits = n_item.bit_length() - 1

    def target(i):
        item, seq = i // n_seq, i % n_seq
        turned = sum(((item >> bit) & 1) << (bits - 1 - bit) for bit in range(bits))
        return seq * n_item + turned, 0

    return pl.pallas_call(
        place_kernel,
        grid=(count,),
        out_shape=[shape((count * rows, width), f32) for width in widths],
        in_specs=[pl.BlockSpec((1, rows, total), lambda i: (i, 0, 0))],
        out_specs=[pl.BlockSpec((rows, width), target) for width in widths],
        compiler_params=pltpu.CompilerParams(vmem_limit_bytes=16 * MIB),
        cost_estimate=cost(blocks.size, 6 * blocks.size),
        name="place_blocks",
    )(blocks)


def halves_kernel(steps, place_ref, *refs):
    count = len(steps)
    keeps, gots, outs = refs[:count], refs[count : 2 * count], refs[2 * count :]
    for step, keep_ref, got_ref, kept_ref, sent_ref in zip(
        steps, keeps, gots, outs[:count], outs[count:]
    ):
        upper = place_bit(place_ref, *step) != 0
        total = (keep_ref[...].astype(f32) + got_ref[...].astype(f32)).astype(bf16)
        half = total.shape[0] // 2
        kept_ref[...] = jnp.where(upper, total[half:], total[:half])
        sent_ref[...] = jnp.where(upper, total[:half], total[half:])


def sum_halves(chain, steps, keeps, gots, cut=1):
    count = len(steps)
    rows, width = keeps[0].shape[0] // cut, keeps[0].shape[1]
    specs = [
        pl.BlockSpec((rows, width), functools.partial(lambda at, i: (at, 0), at if cut > 1 else 0))
        for at in range(count)
    ]
    results = chain.launch(
        functools.partial(halves_kernel, steps),
        (*keeps, *gots),
        specs * 2,
        [shape((rows // 2, width), bf16)] * (2 * count),
        [whole(rows // 2, width)] * (2 * count),
        24,
        cost(count * rows * width, 6 * count * rows * width),
        "sum_halves",
    )
    return results[:count], results[count:]


def join_kernel(steps, stacked, place_ref, *refs):
    count = len(steps)
    mines, others, outs = refs[:count], refs[count : 2 * count], refs[2 * count :]
    for at, (step, mine_ref, other_ref) in enumerate(zip(steps, mines, others)):
        upper = place_bit(place_ref, *step) != 0
        mine, other = mine_ref[...], other_ref[...]
        half = mine.shape[0]
        out_ref = outs[0] if stacked else outs[at]
        first = 2 * half * at if stacked else 0
        out_ref[pl.ds(first, half), :] = jnp.where(upper, other, mine)
        out_ref[pl.ds(first + half, half), :] = jnp.where(upper, mine, other)


def join(chain, steps, mines, others, stacked=False):
    count = len(steps)
    half, width = mines[0].shape
    sizes = [(2 * half * count, width)] if stacked else [(2 * half, width)] * count
    return chain.launch(
        functools.partial(join_kernel, steps, stacked),
        (*mines, *others),
        [whole(half, width)] * (2 * count),
        [shape(size, bf16) for size in sizes],
        [whole(*size) for size in sizes],
        24,
        cost(count * half * width, 8 * count * half * width),
        "join",
    )


def whole_sum(chain, keep, send, item_bits, seq_bits):
    got = swap_bit(send, *item_bits[0])
    orders = (item_bits[1:] + seq_bits, seq_bits[:1] + item_bits[1:] + seq_bits[1:])
    steps = list(zip(*orders))
    keeps, sends = sum_halves(chain, steps[0], [keep] * 2, [got] * 2, 2)
    for step, following in zip(steps, steps[1:-1]):
        gots = [swap_bit(send, *one) for send, one in zip(sends, step)]
        keeps, sends = sum_halves(chain, following, keeps, gots)
    gots = [swap_bit(send, *one) for send, one in zip(sends, steps[-2])]
    sums = [plain_sum(chain, keep, got) for keep, got in zip(keeps, gots)]
    gots = [swap_bit(total, *one) for total, one in zip(sums, steps[-1])]
    sums = [plain_sum(chain, total, got) for total, got in zip(sums, gots)]
    for step in steps[-2::-1]:
        gots = [swap_bit(total, *one) for total, one in zip(sums, step)]
        sums = join(chain, step, sums, gots, stacked=step == steps[0])
    return sums[0], swap_bit(sums[0], *item_bits[0])


def last_kernel(
    slab, place_ref, mine_ref, other_ref, resid_ref, lat_ref, gain_ref, wq_ref,
    value_ref, key_ref, query_ref, latent_ref, gain_kv_ref, gain_q_ref, gain_mlp_ref, resid_s,
):
    byte_width = value_ref.shape[0]
    latents, width = lat_ref.shape
    upper = place_bit(place_ref, "item", 0) != 0
    half = mine_ref.shape[0]
    rest = byte_width - half
    value_ref[pl.ds(0, half), :] = jnp.where(upper, other_ref[...], mine_ref[...]).astype(f32)
    second = jnp.where(upper, mine_ref[...], other_ref[...])
    value_ref[pl.ds(half, rest), :] = second[:rest].astype(f32)
    lower = second[rest:].astype(f32)
    for at in range(0, byte_width, QK):
        key_ref[pl.ds(at, QK), :] = lower[:, at : at + QK]
    query_t = (lower[:, byte_width : byte_width + latents] * SCALE).astype(bf16)
    gains = lower[:, byte_width + latents :]
    row = 0
    for ref in (gain_kv_ref, gain_mlp_ref):
        for at in range(0, ref.shape[1], QK):
            ref[:, pl.ds(at, QK)] = gains[row : row + 1]
            row += 1
    hat, inverse = normalize(lat_ref[...].astype(f32))
    gain = gain_ref[...]
    lat_low = (hat * gain).astype(bf16)
    query_ref[...] = dot_nt(lat_low.T, query_t)
    grad_lat = dot_nt(query_t.T, wq_ref[...])
    gain_q_ref[...] = jnp.sum(grad_lat * hat, axis=0, keepdims=True)
    parts = width // latents
    for rank in range(latents // slab):
        for part in range(parts):
            resid_s[pl.ds(rank * slab, slab), pl.ds(part * latents, latents)] = resid_ref[
                pl.ds((rank * parts + part) * slab, slab), :
            ]
    latent_ref[...] = resid_s[...] + norm_back(grad_lat * gain, hat, inverse)


def last_step(chain, n_seq, sums, resid, latent_init, gain_q, w_query):
    latents, width = latent_init.shape
    byte_width = 2 * sums[0].shape[0] - QK
    inputs = (*sums, resid, latent_init, gain_q, w_query)
    dims = [(byte_width, V), (byte_width, QK), (width, QK), (latents, width)]
    dims += [(1, byte_width), (1, width), (1, width)]
    return chain.launch(
        functools.partial(last_kernel, latents // n_seq),
        inputs,
        [whole(*array.shape) for array in inputs],
        [shape(dim, f32) for dim in dims],
        [whole(*dim) for dim in dims],
        32,
        cost(4 * latents * width * QK, 12 * MIB),
        "last_step",
        scratch=[pltpu.VMEM((latents, width), f32)],
    )


ORDER = "abcadbCacbadcbadcbdcAdBCD"


def per_device(
    byte_in,
    lengths,
    latent_init,
    gain_kv,
    gain_q,
    gain_mlp,
    w_query,
    w_key,
    w_value,
    w_out,
    w_up,
    w_down,
    d_out,
):
    items, slot, byte_width = byte_in.shape
    latents, width = latent_init.shape
    n_item, n_seq = lax.axis_size("item"), lax.axis_size("seq")
    item_bits, seq_bits = bits_of("item"), bits_of("seq")
    ranks = jnp.stack([lax.axis_index("seq"), lax.axis_index("item")])
    chain = Chain(jnp.concatenate([ranks.astype(jnp.int32), lengths]))
    gain_kv = gain_kv[None, :]
    q_t = make_queries(chain, latent_init, gain_q, w_query)
    stacks = ()
    carried = None
    act = None

    def travel(item):
        nonlocal stacks
        *stacks, keep, send = attend(
            chain, item, byte_in, gain_kv, w_key, w_value, q_t, stacks
        )
        got = swap_bit(send, "seq", 0)
        yield
        mine = merge(chain, 0, keep, got)
        if n_seq == 8:
            inward = lax.ppermute(mine, "seq", [(0, 2), (1, 3), (6, 4), (7, 5)])
            yield
            mine = merge(chain, 2, mine, inward)
            across = lax.ppermute(mine, "seq", [(2, 4), (3, 5), (4, 2), (5, 3)])
            yield
            mine = merge(chain, 2, mine, across)
            outward = lax.ppermute(mine, "seq", [(2, 0), (3, 1), (4, 6), (5, 7)])
            yield
            mine = choose(chain, mine, outward)
        else:
            for axis, bit in seq_bits[1:]:
                got = swap_bit(mine, axis, bit)
                yield
                mine = merge(chain, bit, mine, got)
        yield mine, swap_bit(mine, "seq", 0)

    ways = [travel(item) for item in range(items)]
    halves = [None] * items
    for letter in ORDER:
        item = "abcd".index(letter.lower())
        if letter.islower():
            halves[item] = next(ways[item])
            continue
        if halves[item] is None:
            act = cotangents(chain, d_out, w_down)
            continue
        for way in ways[item : item + 1]:
            for halves_item in way:
                halves[item] = halves_item
        latents_out, ga, stats, mlp, *sums = latent_step(
            chain,
            item,
            width // n_seq,
            *halves[item],
            latent_init,
            gain_mlp[None, :],
            d_out,
            act,
            (w_out, w_up, w_down),
            carried,
        )
        carried = (*sums, mlp, latents_out, ga, stats)
    keys, values = stacks

    keep, send = sums
    for step, following in zip(item_bits, item_bits[1:]):
        keep, send = split_sum(chain, following, keep, swap_bit(send, *step))
    got = swap_bit(send, *item_bits[-1])
    bytes_args = (byte_in, gain_kv, w_key, w_value, q_t, keys, values, ga, stats)
    begun = bytes_step(chain, 0, items // 2, *bytes_args, None, mlp, 1.0 / n_seq)
    latent_piece = plain_sum(chain, keep, got)
    latent_all = lax.all_gather(latent_piece, ("item", "seq"), axis=0, tiled=False)
    byte_grad, keep, send = bytes_step(
        chain, items // 2, items - items // 2, *bytes_args, begun, mlp, 1.0 / n_seq
    )
    byte_halves = whole_sum(chain, keep, send, item_bits, seq_bits)
    widths = (width, width, width, latents)
    if latent_piece.shape[0] % 8 == 0:
        whole_grads = place_blocks(latent_all, n_item, n_seq, widths)
    else:
        count = len(item_bits)
        blocks = latent_all.reshape((2,) * count + (n_seq,) + latent_piece.shape)
        turn = [count] + list(range(count))[::-1] + [count + 1, count + 2]
        blocks = blocks.transpose(turn).reshape(-1, sum(widths)).astype(f32)
        whole_grads = [blocks[:, i * width : i * width + size] for i, size in enumerate(widths)]
    out_grad, up_grad, down_grad, resid = whole_grads
    value_grad, key_grad, query_grad, latent_grad, *gains = last_step(
        chain, n_seq, byte_halves, resid, latent_init, gain_q[None, :], w_query
    )
    gain_kv_grad, gain_q_grad, gain_mlp_grad = [gain.reshape(-1) for gain in gains]
    return (
        latents_out,
        byte_grad,
        latent_grad,
        gain_kv_grad,
        gain_q_grad,
        gain_mlp_grad,
        query_grad,
        key_grad,
        value_grad,
        out_grad,
        up_grad,
        down_grad,
    )


def solution(mesh):
    placed = (P("item", "seq", None), P("item")) + (P(),) * 10 + (P("item", None, None),)
    return jax.shard_map(
        per_device,
        mesh=mesh,
        in_specs=placed,
        out_specs=(P("item", None, None), P("item", "seq", None)) + (P(),) * 10,
        check_vma=False,
    )
```

```python
import functools

import jax
import jax.numpy as jnp
from jax import lax
from jax.experimental import pallas as pl
from jax.experimental.pallas import tpu as pltpu
from jax.sharding import PartitionSpec as P

HEADS = 8
QK = 256
V = 1280
QK_HEAD = QK // HEADS
V_HEAD = V // HEADS
SCALE = QK_HEAD**-0.5
ROWS = V + 2 * HEADS
EPS = 1e-05
NEG = -1e30
MIB = 1 << 20
f32 = jnp.float32
bf16 = jnp.bfloat16

IN_VMEM = pl.BlockSpec(memory_space=pltpu.VMEM)
IN_SMEM = pl.BlockSpec(memory_space=pltpu.SMEM)
ANYWHERE = pl.BlockSpec(memory_space=pl.ANY)


def dot(a, b):
    return jnp.dot(a, b, preferred_element_type=f32)


def dot_nt(a, b):
    return lax.dot_general(a, b, (((1,), (1,)), ((), ())), preferred_element_type=f32)


def shape(dims, dtype):
    return jax.ShapeDtypeStruct(dims, dtype)


def cost(microseconds):
    return pl.CostEstimate(
        flops=int(microseconds * 5e8), bytes_accessed=int(microseconds * 1.5e6), transcendentals=0
    )


class Chain:
    def __init__(self, place):
        self.place = place
        self.token = jnp.zeros((8, 128), f32)

    def launch(self, kernel, inputs, outs, mib, name, time=0.7, far_in=(), far_out=(), scratch=(), aliases=None):
        count, made = len(inputs) + 1, len(outs)

        def body(*refs):
            refs[count + 1 + made][...] = jnp.zeros((8, 128), f32)
            kernel(*refs[:count], *refs[count + 1 : count + 1 + made], *refs[count + 2 + made :])

        *results, self.token = pl.pallas_call(
            body,
            out_shape=[*outs, shape((8, 128), f32)],
            in_specs=[IN_SMEM]
            + [ANYWHERE if i in far_in else IN_VMEM for i in range(count - 1)]
            + [ANYWHERE],
            out_specs=[ANYWHERE if i in far_out else IN_VMEM for i in range(made)] + [IN_VMEM],
            scratch_shapes=scratch,
            input_output_aliases={1 + i: o for i, o in (aliases or {}).items()},
            compiler_params=pltpu.CompilerParams(vmem_limit_bytes=mib * MIB),
            cost_estimate=cost(time),
            name=name,
        )(self.place, *inputs, self.token)
        return results


def place_bit(place_ref, axis, bit):
    return (place_ref[0 if axis == "seq" else 1] >> bit) & 1


def normalize(vector, axis=-1):
    average = jnp.mean(vector, axis=axis, keepdims=True)
    centered = vector - average
    inverse = lax.rsqrt(jnp.mean(centered * centered, axis=axis, keepdims=True) + EPS)
    return (centered * inverse, inverse)


def norm_back(grad_hat, hat, inverse, axis=-1):
    return inverse * (
        grad_hat
        - jnp.mean(grad_hat, axis=axis, keepdims=True)
        - hat * jnp.mean(grad_hat * hat, axis=axis, keepdims=True)
    )


def query_kernel(place_ref, lat_ref, gain_ref, wq_ref, q_ref):
    hat, _ = normalize(lat_ref[...].astype(f32))
    lat_low = (hat * gain_ref[...]).astype(bf16)
    q_ref[...] = dot(lat_low, wq_ref[...]).T.astype(bf16)


def make_queries(chain, latent_init, gain_q, w_query):
    outs = [shape((QK, latent_init.shape[0]), bf16)]
    return chain.launch(query_kernel, (latent_init, gain_q, w_query), outs, 12, "queries",
        1.3)[0]


def head_queries(q_t, head):
    channel = lax.broadcasted_iota(jnp.int32, q_t.shape, 0)
    return jnp.where(channel // QK_HEAD == head, q_t, jnp.zeros_like(q_t))


def attend_kernel(
    item, place_ref, x_ref, gain_ref, wk_ref, wv_ref, q_ref, k_ref, v_ref, keep_ref, send_ref
):
    low = place_bit(place_ref, "seq", 0)
    limit = place_ref[2 + item] - place_ref[0] * x_ref.shape[1]
    hat, _ = normalize(x_ref[item].astype(f32))
    byte_low = (hat * gain_ref[...]).astype(bf16)
    keys = dot(byte_low, wk_ref[...]).astype(bf16)
    values = dot(byte_low, wv_ref[...])
    k_ref[...] = keys
    v_ref[...] = values.astype(bf16)
    values_t = values.T.astype(bf16)
    q_t = q_ref[...]
    latents = q_t.shape[1]
    half = latents // 2
    inside = lax.broadcasted_iota(jnp.int32, (keys.shape[0], latents), 0) < limit

    def put(first, block):
        left, right = block[:, :half], block[:, half:]
        rows = pl.ds(first, block.shape[0])
        keep_ref[rows, :] = jnp.where(low == 0, left, right).astype(bf16)
        send_ref[rows, :] = jnp.where(low == 0, right, left).astype(bf16)

    totals = []
    for head in range(HEADS):
        scores = dot(keys, head_queries(q_t, head)) * SCALE
        scores = jnp.where(inside, scores, NEG)
        top = jnp.max(scores, axis=0, keepdims=True)
        powers = jnp.exp(scores - top)
        total = jnp.sum(powers, axis=0, keepdims=True)
        rows = slice(head * V_HEAD, (head + 1) * V_HEAD)
        put(head * V_HEAD, dot(values_t[rows], powers.astype(bf16)) * (1.0 / total))
        totals.append(top + jnp.log(total))
    lse = jnp.concatenate(totals, axis=0)
    high = lse.astype(bf16).astype(f32)
    put(V, jnp.concatenate([high, lse - high], axis=0))


def attend(chain, item, byte_in, gain_kv, w_key, w_value, q_t):
    slot = byte_in.shape[1]
    half = q_t.shape[1] // 2
    outs = [shape((slot, QK), bf16), shape((slot, V), bf16)] + [shape((ROWS, half), bf16)] * 2
    return chain.launch(
        functools.partial(attend_kernel, item),
        (byte_in, gain_kv, w_key, w_value, q_t),
        outs,
        12,
        "attend",
        3.9,
    )


def merge_kernel(bit, place_ref, mine_ref, other_ref, out_ref):
    swap = place_bit(place_ref, "seq", bit) != 0

    def totals(ref):
        return ref[V : V + HEADS, :].astype(f32) + ref[V + HEADS :, :].astype(f32)

    def ordered(mine, other):
        return jnp.where(swap, other, mine), jnp.where(swap, mine, other)

    lse_a, lse_b = ordered(totals(mine_ref), totals(other_ref))
    top = jnp.maximum(lse_a, lse_b)
    weight_a = jnp.exp(lse_a - top)
    weight_b = jnp.exp(lse_b - top)
    total = weight_a + weight_b
    lse = top + jnp.log(total)
    weight_a = weight_a / total
    weight_b = weight_b / total
    for head in range(HEADS):
        rows = pl.ds(head * V_HEAD, V_HEAD)
        sums_a, sums_b = ordered(mine_ref[rows, :].astype(f32), other_ref[rows, :].astype(f32))
        out_ref[rows, :] = (
            sums_a * weight_a[head : head + 1] + sums_b * weight_b[head : head + 1]
        ).astype(bf16)
    high = lse.astype(bf16).astype(f32)
    out_ref[pl.ds(V, 2 * HEADS), :] = jnp.concatenate([high, lse - high], axis=0).astype(bf16)


def merge(chain, bit, mine, other):
    kernel = functools.partial(merge_kernel, bit)
    return chain.launch(kernel, (mine, other), [shape(mine.shape, bf16)], 8, "merge")[0]


def choose_kernel(place_ref, mine_ref, other_ref, out_ref):
    line = place_ref[0] >> 1
    inner = (line == 1) | (line == 2)
    out_ref[...] = jnp.where(inner, mine_ref[...], other_ref[...])


def choose(chain, mine, other):
    return chain.launch(choose_kernel, (mine, other), [shape(mine.shape, bf16)], 8, "choose")[0]


def cotangent_kernel(item, place_ref, g_ref, w_ref, act_ref):
    for rows in range(0, w_ref.shape[0], TILE):
        act_ref[:, pl.ds(rows, TILE)] = dot_nt(g_ref[item], w_ref[pl.ds(rows, TILE), :])


def cotangent(chain, item, d_out, w_down):
    outs = [shape((d_out.shape[1], w_down.shape[0]), f32)]
    kernel = functools.partial(cotangent_kernel, item)
    return chain.launch(kernel, (d_out, w_down), outs, 12, "cotangent",
        1.6)[0]


TILE = 256
ROOT_HALF = 0.7071067811865476
ROOT_TWO_PI = 0.3989422804014327


def latent_kernel(
    item, last, place_ref, mine_ref, other_ref, lat_ref, gain_ref, g_ref, act_ref, w_out, w_up, w_down, *refs
):
    first = item == 0
    if not first:
        acc_in, mlp_in, _, *refs = refs
    out_ref, ga_ref, stat_ref, mlp_ref, acc_ref, *refs = refs
    if last:
        keep_ref, send_ref, *refs = refs
    out_s, att_s, turn_s, branch_s, sem = refs
    low, rank, core = place_bit(place_ref, "seq", 0), place_ref[0], place_bit(place_ref, "item", 0)
    latents, width = lat_ref.shape
    ff = act_ref.shape[1]
    share = acc_ref.shape[0]
    g = g_ref[item]
    mine, other = mine_ref[...], other_ref[...]
    left = jnp.where(low == 0, mine, other)
    right = jnp.where(low == 0, other, mine)
    whole = jnp.concatenate([left, right], axis=1)
    att_s[...] = whole[:V]
    stat_ref[:HEADS, :] = whole[V : V + HEADS].astype(f32) + whole[V + HEADS :].astype(f32)
    attended = whole[:V].T
    rows = pl.ds(pl.multiple_of(rank * share, 16), share)

    def add(part, at, size):
        acc_ref[:, pl.ds(at, size)] = part if first else part + acc_in[:, pl.ds(at, size)]

    mixed = lat_ref[...].astype(f32) + jnp.concatenate(
        [dot(attended, w_out[:, pl.ds(at, TILE)]) for at in range(0, width, TILE)], axis=1
    )
    hat, inverse = normalize(mixed)
    gain = gain_ref[...]
    hidden = (hat * gain).astype(bf16)
    activated, grad_up = [], []
    for at in range(0, ff, TILE):
        upward = dot(hidden, w_up[:, pl.ds(at, TILE)])
        bell = 0.5 + 0.5 * lax.erf(upward * ROOT_HALF)
        slope = bell + upward * (ROOT_TWO_PI * jnp.exp(-0.5 * upward * upward))
        activated.append((upward * bell).astype(bf16))
        grad_up.append((act_ref[:, pl.ds(at, TILE)] * slope).astype(bf16))
    activated = jnp.concatenate(activated, axis=1)
    grad_up = jnp.concatenate(grad_up, axis=1)
    for at in range(0, width, TILE):
        block = mixed[:, at : at + TILE] + dot(activated, w_down[:, pl.ds(at, TILE)])
        out_s[:, pl.ds(at, TILE)] = block.astype(bf16)
    leaving = pltpu.make_async_copy(out_s, out_ref.at[item], sem)
    leaving.start()
    turn_s[...] = activated.T
    add(dot(turn_s[rows, :], g), width + ff, width)
    grad_hidden = jnp.concatenate(
        [dot_nt(grad_up, w_up[pl.ds(at, TILE), :]) for at in range(0, width, TILE)], axis=1
    )
    turn_s[...] = hidden.T
    add(dot(turn_s[rows, :], grad_up), width, ff)
    mlp = jnp.sum(grad_hidden * hat, axis=0, keepdims=True)
    mlp_ref[...] = mlp if first else mlp + mlp_in[...]
    grad_mixed = g.astype(f32) + norm_back(grad_hidden * gain, hat, inverse)
    branch = grad_mixed.astype(bf16)
    branch_s[...] = branch
    add(dot(att_s[rows, :], branch), 0, width)
    slab = latents * share // width
    few = pl.ds(pl.multiple_of(rank * slab, 16), slab)
    add(
        jnp.concatenate(
            [branch_s[few, pl.ds(at, latents)] for at in range(0, width, latents)], axis=0
        ).astype(f32),
        2 * width + ff,
        latents,
    )
    for at in range(0, V, TILE):
        ga_ref[pl.ds(at, TILE), :] = dot_nt(w_out[pl.ds(at, TILE), :], branch).astype(bf16)
    for head in range(HEADS):
        part = pl.ds(head * V_HEAD, V_HEAD)
        stat_ref[pl.ds(HEADS + head, 1), :] = jnp.sum(
            ga_ref[part, :].astype(f32) * att_s[part, :].astype(f32), axis=0, keepdims=True
        )
    if last:
        half = share // 2
        kept = pl.ds(pl.multiple_of(core * half, 8), half)
        sent = pl.ds(pl.multiple_of((1 - core) * half, 8), half)
        keep_ref[...] = acc_ref[kept, :].astype(bf16)
        send_ref[...] = acc_ref[sent, :].astype(bf16)
    leaving.wait()


def latent_step(chain, item, share, mine, other, lat, gain, g, act, weights, carried):
    items, latents, width = g.shape
    ff = act.shape[1]
    total = 2 * width + ff + latents
    last = item == items - 1
    inputs = [mine, other, lat, gain, g, act, *weights]
    aliases = {}
    if carried:
        inputs += carried
        aliases = {9: 4, 10: 3, 11: 0}
    outs = [
        shape((items, latents, width), bf16),
        shape((V, latents), bf16),
        shape((2 * HEADS, latents), f32),
        shape((1, width), f32),
        shape((share, total), f32),
    ]
    if last:
        outs += [shape((share // 2, total), bf16)] * 2
    return chain.launch(
        functools.partial(latent_kernel, item, last),
        inputs,
        outs,
        20,
        "latent_step",
        8.4,
        far_in=(11,),
        far_out=(0,),
        scratch=[
            pltpu.VMEM((latents, width), bf16),
            pltpu.VMEM((V, latents), bf16),
            pltpu.VMEM((width, latents), bf16),
            pltpu.VMEM((latents, width), bf16),
            pltpu.SemaphoreType.DMA,
        ],
        aliases=aliases,
    )


def bytes_kernel(
    item, last, mlp_scale, place_ref, x_ref, gain_ref, wk_ref, wv_ref, q_ref, k_ref, v_ref, ga_ref, stat_ref, *refs
):
    first = item == 0
    if last:
        mlp_ref, *refs = refs
    if not first:
        sum_in, gain_in, _, *refs = refs
    grad_ref, sum_ref, gain_out, *refs = refs
    if last:
        keep_ref, send_ref, *refs = refs
    grad_s, sem = refs
    core = place_bit(place_ref, "item", 0)
    slot, width = x_ref.shape[1:]
    limit = place_ref[2 + item] - place_ref[0] * slot

    def add(rows, lanes, part):
        at = (pl.ds(*rows), pl.ds(*lanes))
        sum_ref[at] = part if first else part + sum_in[at]

    hat, inverse = normalize(x_ref[item].astype(f32))
    gain = gain_ref[...]
    low_t = (hat * gain).T.astype(bf16)
    keys = k_ref[...]
    values = v_ref[...]
    keys_t = keys.T
    q_t = q_ref[...]
    latents = q_t.shape[1]
    inside = lax.broadcasted_iota(jnp.int32, (slot, latents), 0) < limit

    grad_values, grad_keys = [], []
    for head in range(HEADS):
        scores = dot(keys, head_queries(q_t, head)) * SCALE
        scores = jnp.where(inside, scores, NEG)
        soft = jnp.exp(scores - stat_ref[pl.ds(head, 1), :])
        part = slice(head * V_HEAD, (head + 1) * V_HEAD)
        small = slice(head * QK_HEAD, (head + 1) * QK_HEAD)
        grad_attn = ga_ref[pl.ds(head * V_HEAD, V_HEAD), :]
        grad_soft = dot(values[:, part], grad_attn)
        grad_scores = (soft * (grad_soft - stat_ref[pl.ds(HEADS + head, 1), :])).astype(bf16)
        grad_values.append(dot_nt(grad_attn, soft.astype(bf16)).astype(bf16))
        grad_keys.append((dot_nt(q_t[small], grad_scores) * SCALE).astype(bf16))
        add((width + head * QK_HEAD, QK_HEAD), (width, latents), dot(keys_t[small], grad_scores))
    grad_values = jnp.concatenate(grad_values, axis=0)
    grad_keys = jnp.concatenate(grad_keys, axis=0)
    grad_low = (dot(wv_ref[...], grad_values) + dot(wk_ref[...], grad_keys)).T
    gain_part = jnp.sum(grad_low * hat, axis=0, keepdims=True)
    gain_out[...] = gain_part if first else gain_part + gain_in[...]
    grad_s[...] = norm_back(grad_low * gain, hat, inverse)
    leaving = pltpu.make_async_copy(grad_s, grad_ref.at[item], sem)
    leaving.start()
    for rows in range(0, width, TILE):
        block = low_t[rows : rows + TILE]
        add((rows, TILE), (0, V), dot_nt(block, grad_values))
        add((width, QK), (rows, TILE), dot_nt(block, grad_keys))

    if last:
        at = width
        for part in (gain_out[...], mlp_ref[...] * mlp_scale):
            for begin in range(0, part.shape[1], QK):
                sum_ref[pl.ds(at, 1), pl.ds(width + latents, QK)] = part[:, begin : begin + QK]
                at += 1
        half = sum_ref.shape[0] // 2
        kept = pl.ds(pl.multiple_of(core * half, 16), half)
        sent = pl.ds(pl.multiple_of((1 - core) * half, 16), half)
        keep_ref[...] = sum_ref[kept, :].astype(bf16)
        send_ref[...] = sum_ref[sent, :].astype(bf16)
    elif first:
        sum_ref[pl.ds(width, QK), pl.ds(width + latents, QK)] = jnp.zeros((QK, QK), f32)
    leaving.wait()


def bytes_step(chain, item, byte_in, gain_kv, w_key, w_value, q_t, keys, values, ga, stats, mlp, mlp_scale, begun):
    items, slot, width = byte_in.shape
    rows = width + QK
    last = item == items - 1
    inputs = [byte_in, gain_kv, w_key, w_value, q_t, keys, values, ga, stats]
    if last:
        inputs += [mlp]
    aliases = {}
    far_in = ()
    if begun:
        count = len(inputs)
        inputs += begun
        aliases = {count: 1, count + 1: 2, count + 2: 0}
        far_in = (count + 2,)
    outs = [shape((items, slot, width), f32), shape((rows, V), f32), shape((1, width), f32)]
    if last:
        outs += [shape((rows // 2, V), bf16)] * 2
    return chain.launch(
        functools.partial(bytes_kernel, item, last, mlp_scale),
        inputs,
        outs,
        16,
        "bytes_step",
        6.0,
        far_in=far_in,
        far_out=(0,),
        scratch=[pltpu.VMEM((slot, width), f32), pltpu.SemaphoreType.DMA],
        aliases=aliases,
    )


def swap_bit(array, axis, bit):
    size = lax.axis_size(axis)
    return lax.ppermute(array, axis, [(i, i ^ (1 << bit)) for i in range(size)])


def bit_of(axis, bit):
    return (lax.axis_index(axis) >> bit) & 1


def bits_of(axis):
    return [(axis, bit) for bit in range(lax.axis_size(axis).bit_length() - 1)]


def split_kernel(step, place_ref, keep_ref, got_ref, kept_ref, sent_ref):
    half = kept_ref.shape[0]
    upper = place_bit(place_ref, *step) != 0
    total = (keep_ref[...].astype(f32) + got_ref[...].astype(f32)).astype(bf16)
    kept_ref[...] = jnp.where(upper, total[half:], total[:half])
    sent_ref[...] = jnp.where(upper, total[:half], total[half:])


def split_sum(chain, step, keep, got):
    rows, width = keep.shape
    half = rows // 2
    if half % 8 == 0:
        kernel = functools.partial(split_kernel, step)
        outs = [shape((half, width), bf16)] * 2
        return chain.launch(kernel, (keep, got), outs, 8, "split_sum")
    total = (keep.astype(f32) + got.astype(f32)).astype(bf16)
    take = lambda side: lax.dynamic_slice_in_dim(total, side * half, half, 0)
    bit = bit_of(*step)
    return take(bit), take(1 - bit)


def sum_kernel(place_ref, keep_ref, got_ref, out_ref):
    out_ref[...] = (keep_ref[...].astype(f32) + got_ref[...].astype(f32)).astype(bf16)


def plain_sum(chain, keep, got):
    return chain.launch(sum_kernel, (keep, got), [shape(keep.shape, bf16)], 8, "plain_sum")[0]


def halves_kernel(steps, cut, place_ref, *refs):
    count = len(steps)
    keeps, gots, outs = refs[:count], refs[count : 2 * count], refs[2 * count :]
    stacked = len(outs) == 2
    for at, (step, keep_ref, got_ref) in enumerate(zip(steps, keeps, gots)):
        upper = place_bit(place_ref, *step) != 0
        rows = keep_ref.shape[0] // cut
        part = pl.ds(at * rows if cut > 1 else 0, rows)
        total = (keep_ref[part, :].astype(f32) + got_ref[part, :].astype(f32)).astype(bf16)
        half = rows // 2
        kept_ref, sent_ref = outs if stacked else (outs[at], outs[count + at])
        part = pl.ds(at * half if stacked else 0, half)
        kept_ref[part, :] = jnp.where(upper, total[half:], total[:half])
        sent_ref[part, :] = jnp.where(upper, total[:half], total[half:])


def sum_halves(chain, steps, keeps, gots, cut=1, stacked=False):
    count = len(steps)
    rows, width = keeps[0].shape[0] // cut, keeps[0].shape[1]
    kernel = functools.partial(halves_kernel, steps, cut)
    if stacked:
        outs = [shape((rows // 2 * count, width), bf16)] * 2
        return chain.launch(kernel, (*keeps, *gots), outs, 12, "sum_halves")
    outs = [shape((rows // 2, width), bf16)] * (2 * count)
    results = chain.launch(kernel, (*keeps, *gots), outs, 12, "sum_halves")
    return results[:count], results[count:]


def join_kernel(steps, split, stacked, place_ref, *refs):
    count = len(steps)
    arrays = 1 if split else count
    mines, others, outs = refs[:arrays], refs[arrays : 2 * arrays], refs[2 * arrays :]
    for at, step in enumerate(steps):
        upper = place_bit(place_ref, *step) != 0
        mine_ref, other_ref = (mines[0], others[0]) if split else (mines[at], others[at])
        half = mine_ref.shape[0] // (count if split else 1)
        part = pl.ds(at * half if split else 0, half)
        mine, other = mine_ref[part, :], other_ref[part, :]
        out_ref = outs[0] if stacked else outs[at]
        first = 2 * half * at if stacked else 0
        out_ref[pl.ds(first, half), :] = jnp.where(upper, other, mine)
        out_ref[pl.ds(first + half, half), :] = jnp.where(upper, mine, other)


def join(chain, steps, mines, others, stacked=False):
    count = len(steps)
    rows, width = mines[0].shape
    split = len(mines) == 1
    if split:
        rows //= count
    sizes = [(2 * rows * count, width)] if stacked else [(2 * rows, width)] * count
    kernel = functools.partial(join_kernel, steps, split, stacked)
    outs = [shape(size, bf16) for size in sizes]
    return chain.launch(kernel, (*mines, *others), outs, 12, "join")


def whole_sum(chain, keep, send, item_bits, seq_bits):
    got = swap_bit(send, *item_bits[0])
    orders = (item_bits[1:] + seq_bits, seq_bits[:1] + item_bits[1:] + seq_bits[1:])
    steps = list(zip(*orders))
    common = next(i for i, step in enumerate(steps) if step[0] == step[1])
    yield
    keeps, sends = sum_halves(chain, steps[0], [keep] * 2, [got] * 2, 2, common == 0)
    for at in range(common):
        gots = [swap_bit(send, *one) for send, one in zip(sends, steps[at])]
        yield
        keeps, sends = sum_halves(chain, steps[at + 1], keeps, gots, 1, at + 1 == common)
    keep, send = keeps, sends
    shared = [step[0] for step in steps[common:]]
    for step, following in zip(shared, shared[1:-1]):
        got = swap_bit(send, *step)
        yield
        rows = keep.shape[0] // 2
        keep, send = sum_halves(chain, (following,) * 2, [keep] * 2, [got] * 2, 2, True)
    got = swap_bit(send, *shared[-2])
    yield
    total = plain_sum(chain, keep, got)
    got = swap_bit(total, *shared[-1])
    yield
    total = plain_sum(chain, total, got)
    totals = [total]
    for at in range(len(shared) - 2, -1, -1):
        got = swap_bit(totals[0], *shared[at])
        yield
        totals = join(chain, (shared[at],) * 2, totals, [got], at > 0)
    for step in steps[common - 1 :: -1]:
        gots = [swap_bit(total, *one) for total, one in zip(totals, step)]
        yield
        totals = join(chain, step, totals, gots, step == steps[0])
    other = swap_bit(totals[0], *item_bits[0])
    yield totals[0], other


ROUTES = (
    (("b", ("",)), ("a", ("",)), ("x", ("",)), ("y", ("",))),
    (("x", ("y", "b")), ("y", ("a", "b")), ("a", ("x", "b"))),
    (("b", ("xy",)), ("x", ("ab",)), ("y", ("ab",)), ("a", ("xy",))),
    (("a", ("bxy",)),),
)
BIT_OF = {"x": ("item", 1), "y": ("seq", 0), "a": ("seq", 1), "b": ("seq", 2)}


def glue_kernel(picks, count, place_ref, *refs):
    sources, outs, (sems,) = refs[:count], refs[count:-1], refs[-1:]
    copies = []
    for out, pick in zip(outs, picks):
        for slot, (source, row) in enumerate(pick):
            copies.append(
                pltpu.make_async_copy(sources[source].at[row], out.at[slot], sems.at[len(copies)])
            )
            copies[-1].start()
    for copy in copies:
        copy.wait()


def glue(chain, held, groups):
    arrays = []
    for group in groups:
        for name in group:
            if not any(held[name][0] is array for array in arrays):
                arrays.append(held[name][0])
    index = lambda array: next(i for i, one in enumerate(arrays) if one is array)
    picks = [[(index(held[name][0]), held[name][1]) for name in group] for group in groups]
    block = arrays[0].shape[1:]
    return chain.launch(
        functools.partial(glue_kernel, picks, len(arrays)),
        arrays,
        [shape((len(group),) + block, bf16) for group in groups],
        4,
        "glue",
        2.0,
        far_in=range(len(arrays)),
        far_out=range(len(groups)),
        scratch=[pltpu.SemaphoreType.DMA((sum(len(group) for group in groups),))],
    )


def spread_kernel(masks, place_ref, block_ref, *refs):
    outs, (wide_s, sems) = refs[4:8], refs[8:]
    seq, item = place_ref[0], place_ref[1]
    rows = wide_s.shape[1]
    copies = []
    for slot, (item_mask, seq_mask) in enumerate(masks):
        wide_s[slot] = block_ref[slot].astype(f32)
        owner_item, owner_seq = item ^ item_mask, seq ^ seq_mask
        first = owner_seq * 4 + (owner_item & 1) * 2 + (owner_item >> 1)
        target = pl.ds(pl.multiple_of(first * rows, 8), rows)
        at = 0
        for index, out in enumerate(outs):
            size = out.shape[1]
            copy = pltpu.make_async_copy(
                wide_s.at[slot, :, pl.ds(at, size)], out.at[target, :], sems.at[slot, index]
            )
            copy.start()
            copies.append(copy)
            at += size
    for copy in copies:
        copy.wait()


def spread(chain, names, sibling, blocks, outs):
    masks = [
        (2 * ("x" in name) + sibling, ("y" in name) + 2 * ("a" in name) + 4 * ("b" in name))
        for name in names
    ]
    number = len(names)
    return chain.launch(
        functools.partial(spread_kernel, masks),
        (blocks, *outs),
        [shape(out.shape, f32) for out in outs],
        16,
        "spread",
        2.3,
        far_in=range(1, 5),
        far_out=range(4),
        scratch=[
            pltpu.VMEM(blocks.shape, f32),
            pltpu.SemaphoreType.DMA((number, 4)),
        ],
        aliases={1 + i: i for i in range(4)},
    )


def blank_kernel(place_ref, *refs):
    pass


def gather_blocks(chain, keep, got, groups):
    block = plain_sum(chain, keep, got)[None]
    held = {"": (block, 0)}
    fresh = [""]
    for level, sends in enumerate(ROUTES):
        if level == 0:
            arrays = [block] * len(sends)
        else:
            *arrays, side = glue(chain, held, [group for _, group in sends] + [fresh])
            groups.append((fresh, side, swap_bit(side, "item", 0)))
            fresh = []
        for (along, group), array in zip(sends, arrays):
            moved = swap_bit(array, *BIT_OF[along])
            for row, name in enumerate(group):
                new = "".join(sorted(name + along))
                held[new] = (moved, row)
                fresh.append(new)
        yield
    last = held[fresh[0]][0]
    groups.append((fresh, last, swap_bit(last, "item", 0)))
    yield


def spread_blocks(chain, rows, widths, groups):
    outs = [shape((32 * rows, width), f32) for width in widths]
    outs = chain.launch(blank_kernel, (), outs, 4, "blanks", far_out=range(4))
    for at in range(len(ROUTES)):
        for sibling in range(2):
            outs = spread(chain, groups[at][0], sibling, groups[at][1 + sibling], outs)
            yield outs


def last_kernel(
    slab, place_ref, mine_ref, other_ref, resid_ref, lat_ref, gain_ref, wq_ref,
    value_ref, key_ref, query_ref, latent_ref, gain_kv_ref, gain_q_ref, gain_mlp_ref, resid_s,
):
    byte_width = value_ref.shape[0]
    latents, width = lat_ref.shape
    upper = place_bit(place_ref, "item", 0) != 0
    half = mine_ref.shape[0]
    rest = byte_width - half
    value_ref[pl.ds(0, half), :] = jnp.where(upper, other_ref[...], mine_ref[...]).astype(f32)
    second = jnp.where(upper, mine_ref[...], other_ref[...])
    value_ref[pl.ds(half, rest), :] = second[:rest].astype(f32)
    lower = second[rest:].astype(f32)
    for at in range(0, byte_width, QK):
        key_ref[pl.ds(at, QK), :] = lower[:, at : at + QK]
    query_t = (lower[:, byte_width : byte_width + latents] * SCALE).astype(bf16)
    gains = lower[:, byte_width + latents :]
    row = 0
    for ref in (gain_kv_ref, gain_mlp_ref):
        for at in range(0, ref.shape[1], QK):
            ref[:, pl.ds(at, QK)] = gains[row : row + 1]
            row += 1
    hat, inverse = normalize(lat_ref[...].astype(f32))
    gain = gain_ref[...]
    lat_low = (hat * gain).astype(bf16)
    query_ref[...] = dot_nt(lat_low.T, query_t)
    grad_lat = dot_nt(query_t.T, wq_ref[...])
    gain_q_ref[...] = jnp.sum(grad_lat * hat, axis=0, keepdims=True)
    parts = width // latents
    for rank in range(latents // slab):
        for part in range(parts):
            resid_s[pl.ds(rank * slab, slab), pl.ds(part * latents, latents)] = resid_ref[
                pl.ds((rank * parts + part) * slab, slab), :
            ]
    latent_ref[...] = resid_s[...] + norm_back(grad_lat * gain, hat, inverse)


def last_step(chain, n_seq, sums, resid, latent_init, gain_q, w_query):
    latents, width = latent_init.shape
    byte_width = 2 * sums[0].shape[0] - QK
    dims = [(byte_width, V), (byte_width, QK), (width, QK), (latents, width)]
    dims += [(1, byte_width), (1, width), (1, width)]
    return chain.launch(
        functools.partial(last_kernel, latents // n_seq),
        (*sums, resid, latent_init, gain_q, w_query),
        [shape(dim, f32) for dim in dims],
        16,
        "last_step",
        4.8,
        scratch=[pltpu.VMEM((latents, width), f32)],
    )


ORDER = "abc0ad1bca2badc3badcbdcAdBCD"

TAIL = "pmpssmppsspmspmspsspp"


def per_device(
    byte_in,
    lengths,
    latent_init,
    gain_kv,
    gain_q,
    gain_mlp,
    w_query,
    w_key,
    w_value,
    w_out,
    w_up,
    w_down,
    d_out,
):
    items, slot, byte_width = byte_in.shape
    latents, width = latent_init.shape
    n_item, n_seq = lax.axis_size("item"), lax.axis_size("seq")
    item_bits, seq_bits = bits_of("item"), bits_of("seq")
    ranks = jnp.stack([lax.axis_index("seq"), lax.axis_index("item")])
    chain = Chain(jnp.concatenate([ranks.astype(jnp.int32), lengths]))
    gain_kv = gain_kv[None, :]
    gain_q = gain_q[None, :]
    gain_mlp = gain_mlp[None, :]
    q_t = make_queries(chain, latent_init, gain_q, w_query)
    keys, values, acts, halves = [None] * items, [None] * items, [None] * items, [None] * items
    gas, stats = [None] * items, [None] * items
    carried = None

    def travel(item):
        keys[item], values[item], keep, send = attend(
            chain, item, byte_in, gain_kv, w_key, w_value, q_t
        )
        got = swap_bit(send, "seq", 0)
        yield
        mine = merge(chain, 0, keep, got)
        if n_seq == 8:
            inward = lax.ppermute(mine, "seq", [(0, 2), (1, 3), (6, 4), (7, 5)])
            yield
            mine = merge(chain, 2, mine, inward)
            across = lax.ppermute(mine, "seq", [(2, 4), (3, 5), (4, 2), (5, 3)])
            yield
            mine = merge(chain, 2, mine, across)
            outward = lax.ppermute(mine, "seq", [(2, 0), (3, 1), (4, 6), (5, 7)])
            yield
            mine = choose(chain, mine, outward)
        else:
            for axis, bit in seq_bits[1:]:
                got = swap_bit(mine, axis, bit)
                yield
                mine = merge(chain, bit, mine, got)
        yield mine, swap_bit(mine, "seq", 0)

    ways = [travel(item) for item in range(items)]
    for letter in ORDER:
        if letter.isdigit():
            acts[int(letter)] = cotangent(chain, int(letter), d_out, w_down)
            continue
        item = "abcd".index(letter.lower())
        if letter.islower():
            halves[item] = next(ways[item])
            continue
        for halves_item in ways[item]:
            halves[item] = halves_item
        latents_out, gas[item], stats[item], mlp, acc, *sums = latent_step(
            chain,
            item,
            width // n_seq,
            *halves[item],
            latent_init,
            gain_mlp,
            d_out,
            acts[item],
            (w_out, w_up, w_down),
            carried,
        )
        carried = (acc, mlp, latents_out)

    begun = None

    def go_back(item):
        nonlocal begun
        args = (byte_in, gain_kv, w_key, w_value, q_t, keys[item], values[item], gas[item], stats[item])
        grads, total, gains, *halves = bytes_step(chain, item, *args, mlp, 1.0 / n_seq, begun)
        begun = (total, gains, grads)
        return (grads, *halves)

    keep, send = sums
    got = swap_bit(send, *item_bits[0])
    go_back(0)
    for step, following in zip(item_bits, item_bits[1:]):
        keep, send = split_sum(chain, following, keep, got)
        got = swap_bit(send, *following)
    go_back(1)
    widths = (width, width, width, latents)
    direct = (n_item, n_seq) == (4, 8)
    if direct:
        groups = []
        latent_way = gather_blocks(chain, keep, got, groups)
        next(latent_way)
        spread_way = spread_blocks(chain, keep.shape[0], widths, groups)
    else:
        latent_piece = plain_sum(chain, keep, got)
        latent_all = lax.all_gather(latent_piece, ("item", "seq"), axis=0, tiled=False)
    go_back(2)
    byte_grad, keep, send = go_back(3)
    byte_way = whole_sum(chain, keep, send, item_bits, seq_bits)
    if direct:
        for letter in TAIL:
            if letter == "m":
                next(latent_way)
            elif letter == "s":
                whole_grads = next(spread_way)
            else:
                byte_halves = next(byte_way)
    else:
        count = len(item_bits)
        blocks = latent_all.reshape((2,) * count + (n_seq,) + latent_piece.shape)
        turn = [count] + list(range(count))[::-1] + [count + 1, count + 2]
        blocks = blocks.transpose(turn).reshape(-1, sum(widths)).astype(f32)
        whole_grads = [blocks[:, i * width : i * width + size] for i, size in enumerate(widths)]
        for byte_halves in byte_way:
            pass
    out_grad, up_grad, down_grad, resid = whole_grads
    value_grad, key_grad, query_grad, latent_grad, *gains = last_step(
        chain, n_seq, byte_halves, resid, latent_init, gain_q, w_query
    )
    gain_kv_grad, gain_q_grad, gain_mlp_grad = [gain.reshape(-1) for gain in gains]
    return (
        latents_out,
        byte_grad,
        latent_grad,
        gain_kv_grad,
        gain_q_grad,
        gain_mlp_grad,
        query_grad,
        key_grad,
        value_grad,
        out_grad,
        up_grad,
        down_grad,
    )


def solution(mesh):
    placed = (P("item", "seq", None), P("item")) + (P(),) * 10 + (P("item", None, None),)
    return jax.shard_map(
        per_device,
        mesh=mesh,
        in_specs=placed,
        out_specs=(P("item", None, None), P("item", "seq", None)) + (P(),) * 10,
        check_vma=False,
    )
```

```python
import functools

import jax
import jax.numpy as jnp
from jax import lax
from jax.experimental import pallas as pl
from jax.experimental.pallas import tpu as pltpu
from jax.sharding import PartitionSpec as P

HEADS = 8
QK = 256
V = 1280
QK_HEAD = QK // HEADS
V_HEAD = V // HEADS
SCALE = QK_HEAD**-0.5
ROWS = V + 2 * HEADS
EPS = 1e-05
NEG = -1e30
MIB = 1 << 20
f32 = jnp.float32
bf16 = jnp.bfloat16

IN_VMEM = pl.BlockSpec(memory_space=pltpu.VMEM)
IN_SMEM = pl.BlockSpec(memory_space=pltpu.SMEM)
FAR = pl.BlockSpec(memory_space=pltpu.HBM)


def dot(a, b):
    return jnp.dot(a, b, preferred_element_type=f32)


def dot_nt(a, b):
    return lax.dot_general(a, b, (((1,), (1,)), ((), ())), preferred_element_type=f32)


def shape(dims, dtype):
    return jax.ShapeDtypeStruct(dims, dtype)


def cost(microseconds):
    return pl.CostEstimate(
        flops=int(microseconds * 5e8), bytes_accessed=int(microseconds * 1.5e6), transcendentals=0
    )


class Chain:
    def __init__(self, lengths, token):
        self.lengths = lengths
        self.token = token

    def launch(self, kernel, inputs, outs, mib, name, time=0.7, far_in=(), far_out=(), scratch=(), aliases=None):
        count, made = len(inputs) + 1, len(outs)

        def body(*refs):
            refs[count + 1 + made][...] = jnp.zeros((8, 128), f32)
            kernel(*refs[:count], *refs[count + 1 : count + 1 + made], *refs[count + 2 + made :])

        *results, self.token = pl.pallas_call(
            body,
            out_shape=[*outs, shape((8, 128), f32)],
            in_specs=[IN_SMEM]
            + [FAR if i in far_in else IN_VMEM for i in range(count - 1)]
            + [FAR],
            out_specs=[FAR if i in far_out else IN_VMEM for i in range(made)] + [IN_VMEM],
            scratch_shapes=scratch,
            input_output_aliases={1 + i: o for i, o in (aliases or {}).items()},
            compiler_params=pltpu.CompilerParams(vmem_limit_bytes=mib * MIB),
            cost_estimate=cost(time),
            name=name,
        )(self.lengths, *inputs, self.token)
        return results


def row_of(ref):
    return ref[...].reshape(1, -1)


def place_bit(axis, bit):
    return (lax.axis_index(axis) >> bit) & 1


def normalize(vector, axis=-1):
    average = jnp.mean(vector, axis=axis, keepdims=True)
    centered = vector - average
    inverse = lax.rsqrt(jnp.mean(centered * centered, axis=axis, keepdims=True) + EPS)
    return (centered * inverse, inverse)


def norm_back(grad_hat, hat, inverse, axis=-1):
    return inverse * (
        grad_hat
        - jnp.mean(grad_hat, axis=axis, keepdims=True)
        - hat * jnp.mean(grad_hat * hat, axis=axis, keepdims=True)
    )


def query_kernel(lengths_ref, lat_ref, gain_ref, wq_ref, q_ref):
    hat, _ = normalize(lat_ref[...].astype(f32))
    lat_low = (hat * row_of(gain_ref)).astype(bf16)
    q_ref[...] = dot(lat_low, wq_ref[...]).T.astype(bf16)


def head_scores(keys, q_t, head):
    part = slice(head * QK_HEAD, (head + 1) * QK_HEAD)
    return dot(keys[:, part], q_t[part]) * SCALE


def attend_kernel(
    at, item, lengths_ref, x_ref, gain_ref, wk_ref, wv_ref, q_ref, k_ref, v_ref, keep_ref, send_ref
):
    low = place_bit("seq", 0)
    limit = lengths_ref[item] - lax.axis_index("seq") * x_ref.shape[1]
    hat, _ = normalize(x_ref[at].astype(f32))
    byte_low = (hat * row_of(gain_ref)).astype(bf16)
    keys = dot(byte_low, wk_ref[...]).astype(bf16)
    values = dot(byte_low, wv_ref[...])
    k_ref[...] = keys
    v_ref[...] = values.astype(bf16)
    values_t = values.T.astype(bf16)
    q_t = q_ref[...]
    latents = q_t.shape[1]
    half = latents // 2
    inside = lax.broadcasted_iota(jnp.int32, (keys.shape[0], latents), 0) < limit

    def put(first, block):
        left, right = block[:, :half], block[:, half:]
        rows = pl.ds(first, block.shape[0])
        keep_ref[rows, :] = jnp.where(low == 0, left, right).astype(bf16)
        send_ref[rows, :] = jnp.where(low == 0, right, left).astype(bf16)

    totals = []
    for head in range(HEADS):
        scores = head_scores(keys, q_t, head)
        scores = jnp.where(inside, scores, NEG)
        top = jnp.max(scores, axis=0, keepdims=True)
        powers = jnp.exp(scores - top)
        total = jnp.sum(powers, axis=0, keepdims=True)
        rows = slice(head * V_HEAD, (head + 1) * V_HEAD)
        put(head * V_HEAD, dot(values_t[rows], powers.astype(bf16)) * (1.0 / total))
        totals.append(top + jnp.log(total))
    lse = jnp.concatenate(totals, axis=0)
    high = lse.astype(bf16).astype(f32)
    put(V, jnp.concatenate([high, lse - high], axis=0))


def attend_kernels(items, queries, lengths_ref, *refs):
    if queries:
        lat_ref, gain_q_ref, wq_ref, x_ref, gain_ref, wk_ref, wv_ref, q_ref, *refs = refs
    else:
        q_ref, x_ref, gain_ref, wk_ref, wv_ref, *refs = refs
    outs, refs = refs[: 4 * len(items)], refs[4 * len(items) :]
    x_s, wk_s, wv_s, sems, *refs = refs
    rows = wv_ref.shape[0] // 4
    pairs = []
    if queries:
        lat_s, wq_s = refs
        pairs = [(lat_ref, lat_s), (wq_ref, wq_s)]
    early = len(pairs)
    pairs += [(x_ref.at[pl.ds(items[0], len(items))], x_s), (wk_ref, wk_s)]
    pairs += [(wv_ref.at[pl.ds(i * rows, rows)], wv_s.at[pl.ds(i * rows, rows)]) for i in range(4)]
    copies = [pltpu.make_async_copy(src, dst, sems.at[i]) for i, (src, dst) in enumerate(pairs)]
    for copy in copies:
        copy.start()
    for copy in copies[:early]:
        copy.wait()
    if queries:
        query_kernel(lengths_ref, lat_s, gain_q_ref, wq_s, q_ref)
    for copy in copies[early:]:
        copy.wait()
    for at, item in enumerate(items):
        attend_kernel(at, item, lengths_ref, x_s, gain_ref, wk_s, wv_s, q_ref, *outs[4 * at : 4 * at + 4])


def attend_outs(byte_in, latents):
    slot = byte_in.shape[1]
    payload = shape((ROWS, latents // 2), bf16)
    return [shape((slot, QK), bf16), shape((slot, V), bf16), payload, payload]


def attend(chain, item, byte_in, gain_kv, w_key, w_value, q_t):
    return chain.launch(
        functools.partial(attend_kernel, item, item),
        (byte_in, gain_kv, w_key, w_value, q_t),
        attend_outs(byte_in, q_t.shape[1]),
        12,
        "attend",
        3.9,
    )


def attend_first(chain, byte_in, gain_kv, w_key, w_value, latent_init, gain_q, w_query):
    latents = latent_init.shape[0]
    one = (1,) + byte_in.shape[1:]
    shapes = [one, w_key.shape, w_value.shape]
    return chain.launch(
        functools.partial(attend_kernels, (0,), True),
        (latent_init, gain_q, w_query, byte_in, gain_kv, w_key, w_value),
        [shape((QK, latents), bf16), *attend_outs(byte_in, latents)],
        60,
        "attend_first",
        6,
        far_in=(0, 2, 3, 5, 6),
        scratch=[pltpu.VMEM(dims, bf16) for dims in shapes]
        + [pltpu.SemaphoreType.DMA((8,))]
        + [pltpu.VMEM(dims, bf16) for dims in (latent_init.shape, w_query.shape)],
    )


def merge_kernel(bit, lengths_ref, mine_ref, other_ref, out_ref):
    swap = place_bit("seq", bit) != 0

    def totals(ref):
        return ref[V : V + HEADS, :].astype(f32) + ref[V + HEADS :, :].astype(f32)

    def ordered(mine, other):
        return jnp.where(swap, other, mine), jnp.where(swap, mine, other)

    lse_a, lse_b = ordered(totals(mine_ref), totals(other_ref))
    top = jnp.maximum(lse_a, lse_b)
    weight_a = jnp.exp(lse_a - top)
    weight_b = jnp.exp(lse_b - top)
    total = weight_a + weight_b
    lse = top + jnp.log(total)
    weight_a = weight_a / total
    weight_b = weight_b / total
    for head in range(HEADS):
        rows = pl.ds(head * V_HEAD, V_HEAD)
        sums_a, sums_b = ordered(mine_ref[rows, :].astype(f32), other_ref[rows, :].astype(f32))
        out_ref[rows, :] = (
            sums_a * weight_a[head : head + 1] + sums_b * weight_b[head : head + 1]
        ).astype(bf16)
    high = lse.astype(bf16).astype(f32)
    out_ref[pl.ds(V, 2 * HEADS), :] = jnp.concatenate([high, lse - high], axis=0).astype(bf16)


def merge(chain, bit, mine, other):
    kernel = functools.partial(merge_kernel, bit)
    return chain.launch(kernel, (mine, other), [shape(mine.shape, bf16)], 8, "merge")[0]


def choose_kernel(lengths_ref, mine_ref, other_ref, out_ref):
    line = lax.axis_index("seq") >> 1
    inner = (line == 1) | (line == 2)
    out_ref[...] = jnp.where(inner, mine_ref[...], other_ref[...])


def choose(chain, mine, other):
    return chain.launch(choose_kernel, (mine, other), [shape(mine.shape, bf16)], 8, "choose")[0]


def cotangent_kernel(item, lengths_ref, g_ref, w_ref, act_ref):
    for rows in range(0, w_ref.shape[0], TILE):
        act_ref[:, pl.ds(rows, TILE)] = dot_nt(g_ref[item], w_ref[pl.ds(rows, TILE), :])


def cotangent(chain, item, d_out, w_down):
    outs = [shape((d_out.shape[1], w_down.shape[0]), f32)]
    kernel = functools.partial(cotangent_kernel, item)
    return chain.launch(kernel, (d_out, w_down), outs, 12, "cotangent",
        1.6)[0]


TILE = 256
ROOT_HALF = 0.7071067811865476
ROOT_TWO_PI = 0.3989422804014327


def latent_kernel(
    item, last, lengths_ref, mine_ref, other_ref, lat_ref, gain_ref, g_ref, act_ref, w_out, w_up, w_down, *refs
):
    first = item == 0
    if not first:
        mlp_in, _, _, _, _, *refs = refs
    out_ref, ga_ref, stat_ref, mlp_ref, part_ref, branch_ref, gup_ref, *refs = refs
    if last:
        keep_ref, send_ref, *refs = refs
    out_s, att_s, turn_s, sem = refs
    low, core = place_bit("seq", 0), place_bit("item", 0)
    rank = lax.axis_index("seq")
    latents, width = lat_ref.shape
    ff = act_ref.shape[1]
    share = part_ref.shape[1]
    g = g_ref[item]
    own = pl.ds(item * latents, latents)
    mine, other = mine_ref[...], other_ref[...]
    left = jnp.where(low == 0, mine, other)
    right = jnp.where(low == 0, other, mine)
    whole = jnp.concatenate([left, right], axis=1)
    att_s[...] = whole[:V]
    stat_ref[:HEADS, :] = whole[V : V + HEADS].astype(f32) + whole[V + HEADS :].astype(f32)
    attended = whole[:V].T
    rows = pl.ds(pl.multiple_of(rank * share, 16), share)

    part_ref[0, :, own] = att_s[rows, :]
    mixed = lat_ref[...].astype(f32) + jnp.concatenate(
        [dot(attended, w_out[:, pl.ds(at, TILE)]) for at in range(0, width, TILE)], axis=1
    )
    hat, inverse = normalize(mixed)
    gain = row_of(gain_ref)
    hidden = (hat * gain).astype(bf16)
    activated, grad_up = [], []
    for at in range(0, ff, TILE):
        upward = dot(hidden, w_up[:, pl.ds(at, TILE)])
        bell = 0.5 + 0.5 * lax.erf(upward * ROOT_HALF)
        slope = bell + upward * (ROOT_TWO_PI * jnp.exp(-0.5 * upward * upward))
        activated.append((upward * bell).astype(bf16))
        grad_up.append((act_ref[:, pl.ds(at, TILE)] * slope).astype(bf16))
    activated = jnp.concatenate(activated, axis=1)
    grad_up = jnp.concatenate(grad_up, axis=1)
    for at in range(0, width, TILE):
        block = mixed[:, at : at + TILE] + dot(activated, w_down[:, pl.ds(at, TILE)])
        out_s[:, pl.ds(at, TILE)] = block.astype(bf16)
    leaving = pltpu.make_async_copy(out_s, out_ref.at[item], sem)
    leaving.start()
    turn_s[...] = activated.T
    part_ref[2, :, own] = turn_s[rows, :]
    grad_hidden = jnp.concatenate(
        [dot_nt(grad_up, w_up[pl.ds(at, TILE), :]) for at in range(0, width, TILE)], axis=1
    )
    turn_s[...] = hidden.T
    part_ref[1, :, own] = turn_s[rows, :]
    gup_ref[own, :] = grad_up
    mlp = jnp.sum(grad_hidden * hat, axis=0, keepdims=True)
    mlp_ref[...] = mlp if first else mlp + mlp_in[...]
    grad_mixed = g.astype(f32) + norm_back(grad_hidden * gain, hat, inverse)
    branch = grad_mixed.astype(bf16)
    branch_ref[own, :] = branch
    for at in range(0, V, TILE):
        ga_ref[pl.ds(at, TILE), :] = dot_nt(w_out[pl.ds(at, TILE), :], branch).astype(bf16)
    for head in range(HEADS):
        part = pl.ds(head * V_HEAD, V_HEAD)
        stat_ref[pl.ds(HEADS + head, 1), :] = jnp.sum(
            ga_ref[part, :].astype(f32) * att_s[part, :].astype(f32), axis=0, keepdims=True
        )
    if last:
        slab = latents * share // width
        few = [pl.ds(pl.multiple_of(i * latents + rank * slab, 16), slab) for i in range(item + 1)]
        resid = sum(branch_ref[one, :].astype(f32) for one in few)
        parts = (
            dot(part_ref[0], branch_ref[...]),
            dot(part_ref[1], gup_ref[...]),
            dot(part_ref[2], g_ref[...].reshape(branch_ref.shape)),
            jnp.concatenate([resid[:, at : at + latents] for at in range(0, width, latents)], axis=0),
        )
        half = share // 2
        at = 0
        for part in parts:
            lanes = pl.ds(at, part.shape[1])
            lower, upper = part[:half], part[half:]
            keep_ref[:, lanes] = jnp.where(core == 0, lower, upper).astype(bf16)
            send_ref[:, lanes] = jnp.where(core == 0, upper, lower).astype(bf16)
            at += part.shape[1]
    leaving.wait()


def latent_step(chain, item, share, mine, other, lat, gain, g, act, weights, carried):
    items, latents, width = g.shape
    ff = act.shape[1]
    total = 2 * width + ff + latents
    last = item == items - 1
    inputs = [mine, other, lat, gain, g, act, *weights]
    aliases = {}
    if carried:
        inputs += carried
        aliases = {9: 3, 10: 4, 11: 5, 12: 6, 13: 0}
    outs = [
        shape((items, latents, width), bf16),
        shape((V, latents), bf16),
        shape((2 * HEADS, latents), f32),
        shape((1, width), f32),
        shape((3, share, items * latents), bf16),
        shape((items * latents, width), bf16),
        shape((items * latents, ff), bf16),
    ]
    if last:
        outs += [shape((share // 2, total), bf16)] * 2
    return chain.launch(
        functools.partial(latent_kernel, item, last),
        inputs,
        outs,
        20,
        "latent_step",
        8.4,
        far_in=(13,),
        far_out=(0,),
        scratch=[
            pltpu.VMEM((latents, width), bf16),
            pltpu.VMEM((V, latents), bf16),
            pltpu.VMEM((width, latents), bf16),
            pltpu.SemaphoreType.DMA,
        ],
        aliases=aliases,
    )


def bytes_kernel(
    item, last, mlp_scale, lengths_ref, x_ref, gain_ref, wk_ref, wv_ref, q_ref, k_ref, v_ref, ga_ref, stat_ref, *refs
):
    first = item == 0
    if last:
        mlp_ref, *refs = refs
    if not first:
        sum_in, gain_in, _, *refs = refs
    grad_ref, sum_ref, gain_out, *refs = refs
    if last:
        keep_ref, send_ref, *refs = refs
    grad_s, sem = refs
    core = place_bit("item", 0)
    slot, width = x_ref.shape[1:]
    limit = lengths_ref[item] - lax.axis_index("seq") * slot

    def add(rows, lanes, part):
        at = (pl.ds(*rows), pl.ds(*lanes))
        sum_ref[at] = part if first else part + sum_in[at]

    hat, inverse = normalize(x_ref[item].astype(f32))
    gain = row_of(gain_ref)
    low_t = (hat * gain).T.astype(bf16)
    keys = k_ref[...]
    values = v_ref[...]
    keys_t = keys.T
    q_t = q_ref[...]
    latents = q_t.shape[1]
    inside = lax.broadcasted_iota(jnp.int32, (slot, latents), 0) < limit

    grad_values, grad_keys = [], []
    for head in range(HEADS):
        scores = head_scores(keys, q_t, head)
        scores = jnp.where(inside, scores, NEG)
        soft = jnp.exp(scores - stat_ref[pl.ds(head, 1), :])
        part = slice(head * V_HEAD, (head + 1) * V_HEAD)
        small = slice(head * QK_HEAD, (head + 1) * QK_HEAD)
        grad_attn = ga_ref[pl.ds(head * V_HEAD, V_HEAD), :]
        grad_soft = dot(values[:, part], grad_attn)
        grad_scores = (soft * (grad_soft - stat_ref[pl.ds(HEADS + head, 1), :])).astype(bf16)
        grad_values.append(dot_nt(grad_attn, soft.astype(bf16)).astype(bf16))
        grad_keys.append((dot_nt(q_t[small], grad_scores) * SCALE).astype(bf16))
        add((width + head * QK_HEAD, QK_HEAD), (width, latents), dot(keys_t[small], grad_scores))
    grad_values = jnp.concatenate(grad_values, axis=0)
    grad_keys = jnp.concatenate(grad_keys, axis=0)
    grad_low = (dot(wv_ref[...], grad_values) + dot(wk_ref[...], grad_keys)).T
    gain_part = jnp.sum(grad_low * hat, axis=0, keepdims=True)
    gain_out[...] = gain_part if first else gain_part + gain_in[...]
    grad_s[...] = norm_back(grad_low * gain, hat, inverse)
    leaving = pltpu.make_async_copy(grad_s, grad_ref.at[item], sem)
    leaving.start()
    for rows in range(0, width, TILE):
        block = low_t[rows : rows + TILE]
        add((rows, TILE), (0, V), dot_nt(block, grad_values))
        add((width, QK), (rows, TILE), dot_nt(block, grad_keys))

    if last:
        at = width
        for part in (gain_out[...], mlp_ref[...] * mlp_scale):
            for begin in range(0, part.shape[1], QK):
                sum_ref[pl.ds(at, 1), pl.ds(width + latents, QK)] = part[:, begin : begin + QK]
                at += 1
        half = sum_ref.shape[0] // 2
        kept = pl.ds(pl.multiple_of(core * half, 16), half)
        sent = pl.ds(pl.multiple_of((1 - core) * half, 16), half)
        keep_ref[...] = sum_ref[kept, :].astype(bf16)
        send_ref[...] = sum_ref[sent, :].astype(bf16)
    elif first:
        sum_ref[pl.ds(width, QK), pl.ds(width + latents, QK)] = jnp.zeros((QK, QK), f32)
    leaving.wait()


def bytes_step(chain, item, byte_in, gain_kv, w_key, w_value, q_t, keys, values, ga, stats, mlp, mlp_scale, begun):
    items, slot, width = byte_in.shape
    rows = width + QK
    last = item == items - 1
    inputs = [byte_in, gain_kv, w_key, w_value, q_t, keys, values, ga, stats]
    if last:
        inputs += [mlp]
    aliases = {}
    far_in = ()
    if begun:
        count = len(inputs)
        inputs += begun
        aliases = {count: 1, count + 1: 2, count + 2: 0}
        far_in = (count + 2,)
    outs = [shape((items, slot, width), f32), shape((rows, V), f32), shape((1, width), f32)]
    if last:
        outs += [shape((rows // 2, V), bf16)] * 2
    return chain.launch(
        functools.partial(bytes_kernel, item, last, mlp_scale),
        inputs,
        outs,
        16,
        "bytes_step",
        6.0,
        far_in=far_in,
        far_out=(0,),
        scratch=[pltpu.VMEM((slot, width), f32), pltpu.SemaphoreType.DMA],
        aliases=aliases,
    )


def swap_bit(array, axis, bit):
    size = lax.axis_size(axis)
    return lax.ppermute(array, axis, [(i, i ^ (1 << bit)) for i in range(size)])


def bit_of(axis, bit):
    return (lax.axis_index(axis) >> bit) & 1


def bits_of(axis):
    return [(axis, bit) for bit in range(lax.axis_size(axis).bit_length() - 1)]


def split_kernel(step, lengths_ref, keep_ref, got_ref, kept_ref, sent_ref):
    half = kept_ref.shape[0]
    upper = place_bit(*step) != 0
    total = (keep_ref[...].astype(f32) + got_ref[...].astype(f32)).astype(bf16)
    kept_ref[...] = jnp.where(upper, total[half:], total[:half])
    sent_ref[...] = jnp.where(upper, total[:half], total[half:])


def split_sum(chain, step, keep, got):
    rows, width = keep.shape
    half = rows // 2
    if half % 8 == 0:
        kernel = functools.partial(split_kernel, step)
        outs = [shape((half, width), bf16)] * 2
        return chain.launch(kernel, (keep, got), outs, 8, "split_sum")
    total = (keep.astype(f32) + got.astype(f32)).astype(bf16)
    take = lambda side: lax.dynamic_slice_in_dim(total, side * half, half, 0)
    bit = bit_of(*step)
    return take(bit), take(1 - bit)


def sum_kernel(lengths_ref, keep_ref, got_ref, out_ref):
    out_ref[...] = (keep_ref[...].astype(f32) + got_ref[...].astype(f32)).astype(bf16)


def plain_sum(chain, keep, got):
    return chain.launch(sum_kernel, (keep, got), [shape(keep.shape, bf16)], 8, "plain_sum")[0]


def halves_kernel(steps, cut, lengths_ref, *refs):
    count = len(steps)
    keeps, gots, outs = refs[:count], refs[count : 2 * count], refs[2 * count :]
    stacked = len(outs) == 2
    for at, (step, keep_ref, got_ref) in enumerate(zip(steps, keeps, gots)):
        upper = place_bit(*step) != 0
        rows = keep_ref.shape[0] // cut
        part = pl.ds(at * rows if cut > 1 else 0, rows)
        total = (keep_ref[part, :].astype(f32) + got_ref[part, :].astype(f32)).astype(bf16)
        half = rows // 2
        kept_ref, sent_ref = outs if stacked else (outs[at], outs[count + at])
        part = pl.ds(at * half if stacked else 0, half)
        kept_ref[part, :] = jnp.where(upper, total[half:], total[:half])
        sent_ref[part, :] = jnp.where(upper, total[:half], total[half:])


def sum_halves(chain, steps, keeps, gots, cut=1, stacked=False):
    count = len(steps)
    rows, width = keeps[0].shape[0] // cut, keeps[0].shape[1]
    kernel = functools.partial(halves_kernel, steps, cut)
    if stacked:
        outs = [shape((rows // 2 * count, width), bf16)] * 2
        return chain.launch(kernel, (*keeps, *gots), outs, 12, "sum_halves")
    outs = [shape((rows // 2, width), bf16)] * (2 * count)
    results = chain.launch(kernel, (*keeps, *gots), outs, 12, "sum_halves")
    return results[:count], results[count:]


def join_kernel(steps, split, stacked, lengths_ref, *refs):
    count = len(steps)
    arrays = 1 if split else count
    mines, others, outs = refs[:arrays], refs[arrays : 2 * arrays], refs[2 * arrays :]
    for at, step in enumerate(steps):
        upper = place_bit(*step) != 0
        mine_ref, other_ref = (mines[0], others[0]) if split else (mines[at], others[at])
        half = mine_ref.shape[0] // (count if split else 1)
        part = pl.ds(at * half if split else 0, half)
        mine, other = mine_ref[part, :], other_ref[part, :]
        out_ref = outs[0] if stacked else outs[at]
        first = 2 * half * at if stacked else 0
        out_ref[pl.ds(first, half), :] = jnp.where(upper, other, mine)
        out_ref[pl.ds(first + half, half), :] = jnp.where(upper, mine, other)


def join(chain, steps, mines, others, stacked=False):
    count = len(steps)
    rows, width = mines[0].shape
    split = len(mines) == 1
    if split:
        rows //= count
    sizes = [(2 * rows * count, width)] if stacked else [(2 * rows, width)] * count
    kernel = functools.partial(join_kernel, steps, split, stacked)
    outs = [shape(size, bf16) for size in sizes]
    return chain.launch(kernel, (*mines, *others), outs, 12, "join")


def whole_sum(chain, keep, send, item_bits, seq_bits):
    got = swap_bit(send, *item_bits[0])
    orders = (item_bits[1:] + seq_bits, seq_bits[:1] + item_bits[1:] + seq_bits[1:])
    steps = list(zip(*orders))
    common = next(i for i, step in enumerate(steps) if step[0] == step[1])
    yield
    keeps, sends = sum_halves(chain, steps[0], [keep] * 2, [got] * 2, 2, common == 0)
    for at in range(common):
        gots = [swap_bit(send, *one) for send, one in zip(sends, steps[at])]
        yield
        keeps, sends = sum_halves(chain, steps[at + 1], keeps, gots, 1, at + 1 == common)
    keep, send = keeps, sends
    shared = [step[0] for step in steps[common:]]
    for step, following in zip(shared, shared[1:-1]):
        got = swap_bit(send, *step)
        yield
        rows = keep.shape[0] // 2
        keep, send = sum_halves(chain, (following,) * 2, [keep] * 2, [got] * 2, 2, True)
    got = swap_bit(send, *shared[-2])
    yield
    total = plain_sum(chain, keep, got)
    got = swap_bit(total, *shared[-1])
    yield
    total = plain_sum(chain, total, got)
    totals = [total]
    for at in range(len(shared) - 2, -1, -1):
        got = swap_bit(totals[0], *shared[at])
        yield
        totals = join(chain, (shared[at],) * 2, totals, [got], at > 0)
    for step in steps[common - 1 :: -1]:
        gots = [swap_bit(total, *one) for total, one in zip(totals, step)]
        yield
        totals = join(chain, step, totals, gots, step == steps[0])
    other = swap_bit(totals[0], *item_bits[0])
    yield totals[0], other


ROUTES = (
    (("b", ("",)), ("a", ("",)), ("x", ("",)), ("y", ("",))),
    (("a", ("x", "b")),),
    (("x", ("y", "b")), ("y", ("a", "b"))),
    (("y", ("bx", "ab")), ("x", ("ab",)), ("a", ("xy",))),
    (("a", ("bxy",)),),
)
SWAPS = {
    1: ("", "x", "y", "a", "b"),
    3: ("ax", "ab", "xy", "bx", "ay", "by"),
    5: ("bxy", "aby", "abx", "axy", "abxy"),
}
AWAITED = {2: ("ab",), 4: ("aby", "abx", "axy")}
BIT_OF = {"x": ("item", 1), "y": ("seq", 0), "a": ("seq", 1), "b": ("seq", 2)}


def glue_kernel(picks, count, lengths_ref, *refs):
    sources, outs, (sems,) = refs[:count], refs[count:-1], refs[-1:]
    copies = []
    for out, pick in zip(outs, picks):
        for slot, (source, row) in enumerate(pick):
            copies.append(
                pltpu.make_async_copy(sources[source].at[row], out.at[slot], sems.at[len(copies)])
            )
            copies[-1].start()
    for copy in copies:
        copy.wait()


def glue(chain, held, groups, awaited, time):
    arrays = []
    for name in [name for group in groups for name in group] + list(awaited):
        if not any(held[name][0] is array for array in arrays):
            arrays.append(held[name][0])
    index = lambda array: next(i for i, one in enumerate(arrays) if one is array)
    picks = [[(index(held[name][0]), held[name][1]) for name in group] for group in groups]
    block = arrays[0].shape[1:]
    return chain.launch(
        functools.partial(glue_kernel, picks, len(arrays)),
        arrays,
        [shape((len(group),) + block, bf16) for group in groups],
        4,
        "glue",
        time,
        far_in=range(len(arrays)),
        far_out=range(len(groups)),
        scratch=[pltpu.SemaphoreType.DMA((sum(len(group) for group in groups),))],
    )


def spread_kernel(masks, lengths_ref, block_ref, *refs):
    outs, (wide_s, sems) = refs[4:8], refs[8:]
    seq, item = lax.axis_index("seq"), lax.axis_index("item")
    rows = wide_s.shape[1]
    copies = []
    for slot, (item_mask, seq_mask) in enumerate(masks):
        wide_s[slot] = block_ref[slot].astype(f32)
        owner_item, owner_seq = item ^ item_mask, seq ^ seq_mask
        first = owner_seq * 4 + (owner_item & 1) * 2 + (owner_item >> 1)
        target = pl.ds(pl.multiple_of(first * rows, 8), rows)
        at = 0
        for index, out in enumerate(outs):
            size = out.shape[1]
            copy = pltpu.make_async_copy(
                wide_s.at[slot, :, pl.ds(at, size)], out.at[target, :], sems.at[slot, index]
            )
            copy.start()
            copies.append(copy)
            at += size
    for copy in copies:
        copy.wait()


def spread(chain, names, sibling, blocks, outs):
    masks = [
        (2 * ("x" in name) + sibling, ("y" in name) + 2 * ("a" in name) + 4 * ("b" in name))
        for name in names
    ]
    number = len(names)
    return chain.launch(
        functools.partial(spread_kernel, masks),
        (blocks, *outs),
        [shape(out.shape, f32) for out in outs],
        16,
        "spread",
        2.3,
        far_in=range(1, 5),
        far_out=range(4),
        scratch=[
            pltpu.VMEM(blocks.shape, f32),
            pltpu.SemaphoreType.DMA((number, 4)),
        ],
        aliases={1 + i: i for i in range(4)},
    )


def blank_kernel(lengths_ref, *refs):
    pass


def gather_blocks(chain, keep, got, groups):
    block = plain_sum(chain, keep, got)[None]
    held = {"": (block, 0)}
    for level, sends in enumerate(ROUTES + ((),)):
        swap = SWAPS.get(level)
        if level == 0:
            arrays = [block] * len(sends)
        else:
            wanted = [names for _, names in sends] + ([swap] if swap else [])
            arrays = glue(chain, held, wanted, AWAITED.get(level, ()), 50 if level == 1 else 2)
        for (along, names), array in zip(sends, arrays):
            moved = swap_bit(array, *BIT_OF[along])
            for row, name in enumerate(names):
                held["".join(sorted(name + along))] = (moved, row)
        if swap:
            groups.append((swap, arrays[-1], swap_bit(arrays[-1], "item", 0)))
        yield


def spread_blocks(chain, rows, widths, groups):
    outs = [shape((32 * rows, width), f32) for width in widths]
    outs = chain.launch(blank_kernel, (), outs, 4, "blanks", far_out=range(4))
    while True:
        at, sibling = yield outs
        outs = spread(chain, groups[at][0], sibling, groups[at][1 + sibling], outs)


def last_kernel(
    slab, lengths_ref, mine_ref, other_ref, resid_ref, lat_ref, gain_ref, wq_ref,
    value_ref, key_ref, query_ref, latent_ref, gain_kv_ref, gain_q_ref, gain_mlp_ref, resid_s,
):
    byte_width = value_ref.shape[0]
    latents, width = lat_ref.shape
    upper = place_bit("item", 0) != 0
    half = mine_ref.shape[0]
    rest = byte_width - half
    value_ref[pl.ds(0, half), :] = jnp.where(upper, other_ref[...], mine_ref[...]).astype(f32)
    second = jnp.where(upper, mine_ref[...], other_ref[...])
    value_ref[pl.ds(half, rest), :] = second[:rest].astype(f32)
    lower = second[rest:].astype(f32)
    for at in range(0, byte_width, QK):
        key_ref[pl.ds(at, QK), :] = lower[:, at : at + QK]
    query_t = (lower[:, byte_width : byte_width + latents] * SCALE).astype(bf16)
    gains = lower[:, byte_width + latents :]
    row = 0
    for ref in (gain_kv_ref, gain_mlp_ref):
        count = ref.shape[0] // QK
        ref[...] = jnp.concatenate([gains[row + i : row + i + 1] for i in range(count)], axis=1).reshape(-1)
        row += count
    hat, inverse = normalize(lat_ref[...].astype(f32))
    gain = row_of(gain_ref)
    lat_low = (hat * gain).astype(bf16)
    query_ref[...] = dot_nt(lat_low.T, query_t)
    grad_lat = dot_nt(query_t.T, wq_ref[...])
    gain_q_ref[...] = jnp.sum(grad_lat * hat, axis=0)
    parts = width // latents
    for rank in range(latents // slab):
        for part in range(parts):
            resid_s[pl.ds(rank * slab, slab), pl.ds(part * latents, latents)] = resid_ref[
                pl.ds((rank * parts + part) * slab, slab), :
            ]
    latent_ref[...] = resid_s[...] + norm_back(grad_lat * gain, hat, inverse)


def last_step(chain, n_seq, sums, resid, latent_init, gain_q, w_query):
    latents, width = latent_init.shape
    byte_width = 2 * sums[0].shape[0] - QK
    dims = [(byte_width, V), (byte_width, QK), (width, QK), (latents, width)]
    dims += [(byte_width,), (width,), (width,)]
    return chain.launch(
        functools.partial(last_kernel, latents // n_seq),
        (*sums, resid, latent_init, gain_q, w_query),
        [shape(dim, f32) for dim in dims],
        16,
        "last_step",
        4.8,
        scratch=[pltpu.VMEM((latents, width), f32)],
    )


ORDER = "abc0ad1bca2badc3badcbdcAdBCD"

TAIL = "pmpAppmpapmBpmpmbCpc"


def per_device(
    byte_in,
    lengths,
    latent_init,
    gain_kv,
    gain_q,
    gain_mlp,
    w_query,
    w_key,
    w_value,
    w_out,
    w_up,
    w_down,
    d_out,
):
    items, slot, byte_width = byte_in.shape
    latents, width = latent_init.shape
    n_item, n_seq = lax.axis_size("item"), lax.axis_size("seq")
    item_bits, seq_bits = bits_of("item"), bits_of("seq")
    chain = Chain(lengths, byte_in)
    keys, values, acts, halves = [None] * items, [None] * items, [None] * items, [None] * items
    gas, stats = [None] * items, [None] * items
    q_t = None
    carried = None

    def travel(item):
        nonlocal q_t
        operands = (byte_in, gain_kv, w_key, w_value)
        if item == 0:
            q_t, *made = attend_first(chain, *operands, latent_init, gain_q, w_query)
        else:
            made = attend(chain, item, *operands, q_t)
        keys[item], values[item], keep, send = made
        got = swap_bit(send, "seq", 0)
        yield
        mine = merge(chain, 0, keep, got)
        if n_seq == 8:
            inward = lax.ppermute(mine, "seq", [(0, 2), (1, 3), (6, 4), (7, 5)])
            yield
            mine = merge(chain, 2, mine, inward)
            across = lax.ppermute(mine, "seq", [(2, 4), (3, 5), (4, 2), (5, 3)])
            yield
            mine = merge(chain, 2, mine, across)
            outward = lax.ppermute(mine, "seq", [(2, 0), (3, 1), (4, 6), (5, 7)])
            yield
            mine = choose(chain, mine, outward)
        else:
            for axis, bit in seq_bits[1:]:
                got = swap_bit(mine, axis, bit)
                yield
                mine = merge(chain, bit, mine, got)
        yield mine, swap_bit(mine, "seq", 0)

    ways = [travel(item) for item in range(items)]
    for letter in ORDER:
        if letter.isdigit():
            acts[int(letter)] = cotangent(chain, int(letter), d_out, w_down)
            continue
        item = "abcd".index(letter.lower())
        if letter.islower():
            halves[item] = next(ways[item])
            continue
        for halves_item in ways[item]:
            halves[item] = halves_item
        latents_out, gas[item], stats[item], mlp, *factors = latent_step(
            chain,
            item,
            width // n_seq,
            *halves[item],
            latent_init,
            gain_mlp,
            d_out,
            acts[item],
            (w_out, w_up, w_down),
            carried,
        )
        carried = (mlp, *factors[:3], latents_out)
    sums = factors[3:]

    begun = None

    def go_back(item):
        nonlocal begun
        args = (byte_in, gain_kv, w_key, w_value, q_t, keys[item], values[item], gas[item], stats[item])
        grads, total, gains, *halves = bytes_step(chain, item, *args, mlp, 1.0 / n_seq, begun)
        begun = (total, gains, grads)
        return (grads, *halves)

    keep, send = sums
    got = swap_bit(send, *item_bits[0])
    go_back(0)
    for step, following in zip(item_bits, item_bits[1:]):
        keep, send = split_sum(chain, following, keep, got)
        got = swap_bit(send, *following)
    go_back(1)
    widths = (width, width, width, latents)
    direct = (n_item, n_seq) == (4, 8)
    if direct:
        groups = []
        latent_way = gather_blocks(chain, keep, got, groups)
        next(latent_way)
        spread_way = spread_blocks(chain, keep.shape[0], widths, groups)
        next(spread_way)
    else:
        latent_piece = plain_sum(chain, keep, got)
        latent_all = lax.all_gather(latent_piece, ("item", "seq"), axis=0, tiled=False)
    go_back(2)
    byte_grad, keep, send = go_back(3)
    byte_way = whole_sum(chain, keep, send, item_bits, seq_bits)
    if direct:
        for letter in TAIL:
            if letter == "m":
                next(latent_way)
            elif letter == "p":
                byte_halves = next(byte_way)
            else:
                group = "abc".index(letter.lower()), int(letter.islower())
                whole_grads = spread_way.send(group)
    else:
        count = len(item_bits)
        blocks = latent_all.reshape((2,) * count + (n_seq,) + latent_piece.shape)
        turn = [count] + list(range(count))[::-1] + [count + 1, count + 2]
        blocks = blocks.transpose(turn).reshape(-1, sum(widths)).astype(f32)
        whole_grads = [blocks[:, i * width : i * width + size] for i, size in enumerate(widths)]
        for byte_halves in byte_way:
            pass
    out_grad, up_grad, down_grad, resid = whole_grads
    value_grad, key_grad, query_grad, latent_grad, gain_kv_grad, gain_q_grad, gain_mlp_grad = last_step(
        chain, n_seq, byte_halves, resid, latent_init, gain_q, w_query
    )
    return (
        latents_out,
        byte_grad,
        latent_grad,
        gain_kv_grad,
        gain_q_grad,
        gain_mlp_grad,
        query_grad,
        key_grad,
        value_grad,
        out_grad,
        up_grad,
        down_grad,
    )


def solution(mesh):
    placed = (P("item", "seq", None), P("item")) + (P(),) * 10 + (P("item", None, None),)
    return jax.shard_map(
        per_device,
        mesh=mesh,
        in_specs=placed,
        out_specs=(P("item", None, None), P("item", "seq", None)) + (P(),) * 10,
        check_vma=False,
    )
```

```python
import functools

import jax
import jax.numpy as jnp
from jax import lax
from jax.experimental import pallas as pl
from jax.experimental.pallas import tpu as pltpu
from jax.sharding import PartitionSpec as P

HEADS = 8
QK = 256
V = 1280
QK_HEAD = QK // HEADS
V_HEAD = V // HEADS
SCALE = QK_HEAD**-0.5
ROWS = V + 2 * HEADS
EPS = 1e-05
NEG = -1e30
MIB = 1 << 20
f32 = jnp.float32
bf16 = jnp.bfloat16

IN_VMEM = pl.BlockSpec(memory_space=pltpu.VMEM)
IN_SMEM = pl.BlockSpec(memory_space=pltpu.SMEM)
FAR = pl.BlockSpec(memory_space=pltpu.HBM)


def dot(a, b):
    return jnp.dot(a, b, preferred_element_type=f32)


def dot_nt(a, b):
    return lax.dot_general(a, b, (((1,), (1,)), ((), ())), preferred_element_type=f32)


def shape(dims, dtype):
    return jax.ShapeDtypeStruct(dims, dtype)


def cost(microseconds):
    return pl.CostEstimate(
        flops=int(microseconds * 5e8), bytes_accessed=int(microseconds * 1.5e6), transcendentals=0
    )


class Chain:
    def __init__(self, token):
        self.token = token

    def launch(
        self, kernel, inputs, outs, mib, name, time=0.7, far_in=(), far_out=(), scratch=(), aliases=None, scalars=()
    ):
        count, made = len(inputs), len(outs)

        def body(*refs):
            refs[count + 1 + made][...] = jnp.zeros((8, 128), f32)
            kernel(*refs[:count], *refs[count + 1 : count + 1 + made], *refs[count + 2 + made :])

        where = {i: FAR for i in far_in} | {i: IN_SMEM for i in scalars}
        *results, self.token = pl.pallas_call(
            body,
            out_shape=[*outs, shape((8, 128), f32)],
            in_specs=[where.get(i, IN_VMEM) for i in range(count)] + [FAR],
            out_specs=[FAR if i in far_out else IN_VMEM for i in range(made)] + [IN_VMEM],
            scratch_shapes=scratch,
            input_output_aliases=aliases or {},
            compiler_params=pltpu.CompilerParams(vmem_limit_bytes=mib * MIB),
            cost_estimate=cost(time),
            name=name,
        )(*inputs, self.token)
        return results


def row_of(ref):
    return ref[...].reshape(1, -1)


def place_bit(axis, bit):
    return (lax.axis_index(axis) >> bit) & 1


def normalize(vector, axis=-1):
    average = jnp.mean(vector, axis=axis, keepdims=True)
    centered = vector - average
    inverse = lax.rsqrt(jnp.mean(centered * centered, axis=axis, keepdims=True) + EPS)
    return (centered * inverse, inverse)


def norm_back(grad_hat, hat, inverse, axis=-1):
    return inverse * (
        grad_hat
        - jnp.mean(grad_hat, axis=axis, keepdims=True)
        - hat * jnp.mean(grad_hat * hat, axis=axis, keepdims=True)
    )


def query_kernel(lat_ref, gain_ref, wq_ref, q_ref):
    hat, _ = normalize(lat_ref[...].astype(f32))
    lat_low = (hat * row_of(gain_ref)).astype(bf16)
    q_ref[...] = dot(lat_low, wq_ref[...]).T.astype(bf16)


def spread_queries(q_t):
    channel = lax.broadcasted_iota(jnp.int32, q_t.shape, 0) // QK_HEAD
    zeros = jnp.zeros_like(q_t)
    return jnp.concatenate([jnp.where(channel == head, q_t, zeros) for head in range(HEADS)], axis=1)


def attend_kernel(
    at, item, limits_ref, x_ref, gain_ref, wk_ref, wv_ref, q_ref, k_ref, v_ref, keep_ref, send_ref
):
    low = place_bit("seq", 0)
    hat, _ = normalize(x_ref[at].astype(f32))
    byte_low = (hat * row_of(gain_ref)).astype(bf16)
    keys = dot(byte_low, wk_ref[...]).astype(bf16)
    values = dot(byte_low, wv_ref[...])
    k_ref[...] = keys
    v_ref[...] = values.astype(bf16)
    values_t = values.T.astype(bf16)
    q_t = q_ref[...]
    latents = q_t.shape[1]
    half = latents // 2
    inside = lax.broadcasted_iota(jnp.int32, (keys.shape[0], latents), 0) < limits_ref[pl.ds(item, 1), :]

    def put(first, block):
        left, right = block[:, :half], block[:, half:]
        rows = pl.ds(first, block.shape[0])
        keep_ref[rows, :] = jnp.where(low == 0, left, right).astype(bf16)
        send_ref[rows, :] = jnp.where(low == 0, right, left).astype(bf16)

    every = dot(keys, spread_queries(q_t)) * SCALE
    totals, weights, inverses = [], [], []
    for head in range(HEADS):
        scores = every[:, head * latents : (head + 1) * latents]
        scores = jnp.where(inside, scores, NEG)
        top = jnp.max(scores, axis=0, keepdims=True)
        powers = jnp.exp(scores - top)
        total = jnp.sum(powers, axis=0, keepdims=True)
        weights.append(powers.astype(bf16))
        inverses.append(1.0 / total)
        totals.append(top + jnp.log(total))
    for head in range(HEADS):
        rows = slice(head * V_HEAD, (head + 1) * V_HEAD)
        put(head * V_HEAD, dot(values_t[rows], weights[head]) * inverses[head])
    lse = jnp.concatenate(totals, axis=0)
    high = lse.astype(bf16).astype(f32)
    put(V, jnp.concatenate([high, lse - high], axis=0))


def first_kernel(
    lengths_ref, lat_ref, gain_q_ref, wq_ref, x_ref, gain_ref, wk_ref, wv_ref,
    limits_ref, q_ref, k_ref, v_ref, keep_ref, send_ref, x_s, wk_s, wv_s, sems, lat_s, wq_s,
):
    rows = wv_ref.shape[0] // 4
    pairs = [(lat_ref, lat_s), (wq_ref, wq_s), (x_ref.at[pl.ds(0, 1)], x_s), (wk_ref, wk_s)]
    pairs += [(wv_ref.at[pl.ds(i * rows, rows)], wv_s.at[pl.ds(i * rows, rows)]) for i in range(4)]
    copies = [pltpu.make_async_copy(src, dst, sems.at[i]) for i, (src, dst) in enumerate(pairs)]
    for copy in copies:
        copy.start()
    before = lax.axis_index("seq") * x_ref.shape[1]
    for item in range(x_ref.shape[0]):
        limits_ref[pl.ds(item, 1), :] = jnp.full((1, limits_ref.shape[1]), lengths_ref[item] - before, jnp.int32)
    for copy in copies[:2]:
        copy.wait()
    query_kernel(lat_s, gain_q_ref, wq_s, q_ref)
    for copy in copies[2:]:
        copy.wait()
    attend_kernel(0, 0, limits_ref, x_s, gain_ref, wk_s, wv_s, q_ref, k_ref, v_ref, keep_ref, send_ref)


def attend_outs(byte_in, latents):
    slot = byte_in.shape[1]
    payload = shape((ROWS, latents // 2), bf16)
    return [shape((slot, QK), bf16), shape((slot, V), bf16), payload, payload]


def attend(chain, item, limits, byte_in, gain_kv, w_key, w_value, q_t):
    return chain.launch(
        functools.partial(attend_kernel, item, item),
        (limits, byte_in, gain_kv, w_key, w_value, q_t),
        attend_outs(byte_in, q_t.shape[1]),
        18,
        "attend",
        3.9,
    )


def attend_first(chain, lengths, byte_in, gain_kv, w_key, w_value, latent_init, gain_q, w_query):
    latents = latent_init.shape[0]
    one = (1,) + byte_in.shape[1:]
    shapes = [one, w_key.shape, w_value.shape]
    return chain.launch(
        first_kernel,
        (lengths, latent_init, gain_q, w_query, byte_in, gain_kv, w_key, w_value),
        [shape((byte_in.shape[0], latents), jnp.int32), shape((QK, latents), bf16)]
        + attend_outs(byte_in, latents),
        60,
        "attend_first",
        6,
        far_in=(1, 3, 4, 6, 7),
        scalars=(0,),
        scratch=[pltpu.VMEM(dims, bf16) for dims in shapes]
        + [pltpu.SemaphoreType.DMA((8,))]
        + [pltpu.VMEM(dims, bf16) for dims in (latent_init.shape, w_query.shape)],
    )


def merge_kernel(bit, mine_ref, other_ref, out_ref):
    swap = place_bit("seq", bit) != 0

    def totals(ref):
        return ref[V : V + HEADS, :].astype(f32) + ref[V + HEADS :, :].astype(f32)

    def ordered(mine, other):
        return jnp.where(swap, other, mine), jnp.where(swap, mine, other)

    lse_a, lse_b = ordered(totals(mine_ref), totals(other_ref))
    top = jnp.maximum(lse_a, lse_b)
    weight_a = jnp.exp(lse_a - top)
    weight_b = jnp.exp(lse_b - top)
    total = weight_a + weight_b
    lse = top + jnp.log(total)
    weight_a = weight_a / total
    weight_b = weight_b / total
    for head in range(HEADS):
        rows = pl.ds(head * V_HEAD, V_HEAD)
        sums_a, sums_b = ordered(mine_ref[rows, :].astype(f32), other_ref[rows, :].astype(f32))
        out_ref[rows, :] = (
            sums_a * weight_a[head : head + 1] + sums_b * weight_b[head : head + 1]
        ).astype(bf16)
    high = lse.astype(bf16).astype(f32)
    out_ref[pl.ds(V, 2 * HEADS), :] = jnp.concatenate([high, lse - high], axis=0).astype(bf16)


def merge(chain, bit, mine, other):
    kernel = functools.partial(merge_kernel, bit)
    return chain.launch(kernel, (mine, other), [shape(mine.shape, bf16)], 8, "merge")[0]


def choose_kernel(mine_ref, other_ref, out_ref):
    line = lax.axis_index("seq") >> 1
    inner = (line == 1) | (line == 2)
    out_ref[...] = jnp.where(inner, mine_ref[...], other_ref[...])


def choose(chain, mine, other):
    return chain.launch(choose_kernel, (mine, other), [shape(mine.shape, bf16)], 8, "choose")[0]


def cotangent_kernel(item, g_ref, w_ref, act_ref):
    def one(at, carry):
        rows = pl.ds(pl.multiple_of(at * TILE, TILE), TILE)
        act_ref[:, rows] = dot_nt(g_ref[item], w_ref[rows, :])
        return carry

    lax.fori_loop(0, w_ref.shape[0] // TILE, one, 0)


def cotangent(chain, item, d_out, w_down):
    outs = [shape((d_out.shape[1], w_down.shape[0]), f32)]
    kernel = functools.partial(cotangent_kernel, item)
    return chain.launch(kernel, (d_out, w_down), outs, 12, "cotangent",
        1.6)[0]


TILE = 256
ROOT_HALF = 0.7071067811865476
ROOT_TWO_PI = 0.3989422804014327


def latent_kernel(
    item, last, mine_ref, other_ref, lat_ref, gain_ref, g_ref, act_ref, w_out, w_up, w_down, *refs
):
    first = item == 0
    if not first:
        mlp_in, _, _, _, *refs = refs
    out_ref, ga_ref, stat_ref, mlp_ref, part_ref, branch_ref, gup_ref, *refs = refs
    if last:
        keep_ref, send_ref, *refs = refs
    att_s, turn_s = refs
    low, core = place_bit("seq", 0), place_bit("item", 0)
    rank = lax.axis_index("seq")
    latents, width = lat_ref.shape
    ff = act_ref.shape[1]
    share = part_ref.shape[1]
    g = g_ref[item]
    own = pl.ds(item * latents, latents)
    mine, other = mine_ref[...], other_ref[...]
    left = jnp.where(low == 0, mine, other)
    right = jnp.where(low == 0, other, mine)
    whole = jnp.concatenate([left, right], axis=1)
    att_s[...] = whole[:V]
    stat_ref[:HEADS, :] = whole[V : V + HEADS].astype(f32) + whole[V + HEADS :].astype(f32)
    attended = whole[:V].T
    rows = pl.ds(pl.multiple_of(rank * share, 16), share)

    part_ref[0, :, own] = att_s[rows, :]
    mixed = lat_ref[...].astype(f32) + jnp.concatenate(
        [dot(attended, w_out[:, pl.ds(at, TILE)]) for at in range(0, width, TILE)], axis=1
    )
    hat, inverse = normalize(mixed)
    gain = row_of(gain_ref)
    hidden = (hat * gain).astype(bf16)
    activated, grad_up = [], []
    for at in range(0, ff, TILE):
        upward = dot(hidden, w_up[:, pl.ds(at, TILE)])
        bell = 0.5 + 0.5 * lax.erf(upward * ROOT_HALF)
        slope = bell + upward * (ROOT_TWO_PI * jnp.exp(-0.5 * upward * upward))
        activated.append((upward * bell).astype(bf16))
        grad_up.append((act_ref[:, pl.ds(at, TILE)] * slope).astype(bf16))
    activated = jnp.concatenate(activated, axis=1)
    grad_up = jnp.concatenate(grad_up, axis=1)
    for at in range(0, width, TILE):
        block = mixed[:, at : at + TILE] + dot(activated, w_down[:, pl.ds(at, TILE)])
        out_ref[:, pl.ds(at, TILE)] = block.astype(bf16)
    turn_s[...] = activated.T
    part_ref[2, :, own] = turn_s[rows, :]
    grad_hidden = jnp.concatenate(
        [dot_nt(grad_up, w_up[pl.ds(at, TILE), :]) for at in range(0, width, TILE)], axis=1
    )
    turn_s[...] = hidden.T
    part_ref[1, :, own] = turn_s[rows, :]
    gup_ref[own, :] = grad_up
    mlp = jnp.sum(grad_hidden * hat, axis=0, keepdims=True)
    mlp_ref[...] = mlp if first else mlp + mlp_in[...]
    grad_mixed = g.astype(f32) + norm_back(grad_hidden * gain, hat, inverse)
    branch = grad_mixed.astype(bf16)
    branch_ref[own, :] = branch
    for at in range(0, V, TILE):
        ga_ref[pl.ds(at, TILE), :] = dot_nt(w_out[pl.ds(at, TILE), :], branch).astype(bf16)
    for head in range(HEADS):
        part = pl.ds(head * V_HEAD, V_HEAD)
        stat_ref[pl.ds(HEADS + head, 1), :] = jnp.sum(
            ga_ref[part, :].astype(f32) * att_s[part, :].astype(f32), axis=0, keepdims=True
        )
    if last:
        slab = latents * share // width
        few = [pl.ds(pl.multiple_of(i * latents + rank * slab, 16), slab) for i in range(item + 1)]
        resid = sum(branch_ref[one, :].astype(f32) for one in few)
        parts = (
            dot(part_ref[0], branch_ref[...]),
            dot(part_ref[1], gup_ref[...]),
            dot(part_ref[2], g_ref[...].reshape(branch_ref.shape)),
            jnp.concatenate([resid[:, at : at + latents] for at in range(0, width, latents)], axis=0),
        )
        half = share // 2
        at = 0
        for part in parts:
            lanes = pl.ds(at, part.shape[1])
            lower, upper = part[:half], part[half:]
            keep_ref[:, lanes] = jnp.where(core == 0, lower, upper).astype(bf16)
            send_ref[:, lanes] = jnp.where(core == 0, upper, lower).astype(bf16)
            at += part.shape[1]


def latent_step(chain, item, share, mine, other, lat, gain, g, act, weights, carried):
    items, latents, width = g.shape
    ff = act.shape[1]
    total = 2 * width + ff + latents
    last = item == items - 1
    inputs = [mine, other, lat, gain, g, act, *weights]
    aliases = {}
    if carried:
        inputs += carried
        aliases = {10: 4, 11: 5, 12: 6}
    outs = [
        shape((latents, width), bf16),
        shape((V, latents), bf16),
        shape((2 * HEADS, latents), f32),
        shape((1, width), f32),
        shape((3, share, items * latents), bf16),
        shape((items * latents, width), bf16),
        shape((items * latents, ff), bf16),
    ]
    if last:
        outs += [shape((share // 2, total), bf16)] * 2
    return chain.launch(
        functools.partial(latent_kernel, item, last),
        inputs,
        outs,
        20,
        "latent_step",
        8.4,
        scratch=[pltpu.VMEM((V, latents), bf16), pltpu.VMEM((width, latents), bf16)],
        aliases=aliases,
    )


def bytes_kernel(
    item, last, mlp_scale, limits_ref, x_ref, gain_ref, wk_ref, wv_ref, q_ref, k_ref, v_ref, ga_ref, stat_ref, *refs
):
    first = item == 0
    if last:
        mlp_ref, *refs = refs
    if not first:
        sum_in, gain_in, *refs = refs
    grad_ref, sum_ref, gain_out, *refs = refs
    if last:
        keep_ref, send_ref = refs
    core = place_bit("item", 0)
    slot, width = x_ref.shape[1:]

    def add(rows, lanes, part):
        at = (pl.ds(*rows), pl.ds(*lanes))
        sum_ref[at] = part if first else part + sum_in[at]

    hat, inverse = normalize(x_ref[item].astype(f32))
    gain = row_of(gain_ref)
    low_t = (hat * gain).T.astype(bf16)
    keys = k_ref[...]
    values = v_ref[...]
    keys_t = keys.T
    q_t = q_ref[...]
    latents = q_t.shape[1]
    inside = lax.broadcasted_iota(jnp.int32, (slot, latents), 0) < limits_ref[pl.ds(item, 1), :]

    every = dot(keys, spread_queries(q_t)) * SCALE
    grad_values, grad_keys = [], []
    softs, moves = [], []
    for head in range(HEADS):
        scores = every[:, head * latents : (head + 1) * latents]
        scores = jnp.where(inside, scores, NEG)
        soft = jnp.exp(scores - stat_ref[pl.ds(head, 1), :])
        part = slice(head * V_HEAD, (head + 1) * V_HEAD)
        grad_soft = dot(values[:, part], ga_ref[pl.ds(head * V_HEAD, V_HEAD), :])
        moves.append((soft * (grad_soft - stat_ref[pl.ds(HEADS + head, 1), :])).astype(bf16))
        softs.append(soft.astype(bf16))
    for head in range(HEADS):
        grad_attn = ga_ref[pl.ds(head * V_HEAD, V_HEAD), :]
        grad_values.append(dot_nt(grad_attn, softs[head]).astype(bf16))
    for head in range(HEADS):
        small = slice(head * QK_HEAD, (head + 1) * QK_HEAD)
        grad_keys.append((dot_nt(q_t[small], moves[head]) * SCALE).astype(bf16))
        add((width + head * QK_HEAD, QK_HEAD), (width, latents), dot(keys_t[small], moves[head]))
    grad_values = jnp.concatenate(grad_values, axis=0)
    grad_keys = jnp.concatenate(grad_keys, axis=0)
    grad_low = dot_nt(grad_values.T, wv_ref[...]) + dot_nt(grad_keys.T, wk_ref[...])
    gain_part = jnp.sum(grad_low * hat, axis=0, keepdims=True)
    gain_out[...] = gain_part if first else gain_part + gain_in[...]
    grad_ref[...] = norm_back(grad_low * gain, hat, inverse)
    for rows in range(0, width, TILE):
        block = low_t[rows : rows + TILE]
        add((rows, TILE), (0, V), dot_nt(block, grad_values))
        add((width, QK), (rows, TILE), dot_nt(block, grad_keys))

    if last:
        at = width
        for part in (gain_out[...], mlp_ref[...] * mlp_scale):
            for begin in range(0, part.shape[1], QK):
                sum_ref[pl.ds(at, 1), pl.ds(width + latents, QK)] = part[:, begin : begin + QK]
                at += 1
        half = sum_ref.shape[0] // 2
        kept = pl.ds(pl.multiple_of(core * half, 16), half)
        sent = pl.ds(pl.multiple_of((1 - core) * half, 16), half)
        keep_ref[...] = sum_ref[kept, :].astype(bf16)
        send_ref[...] = sum_ref[sent, :].astype(bf16)
    elif first:
        sum_ref[pl.ds(width, QK), pl.ds(width + latents, QK)] = jnp.zeros((QK, QK), f32)


def bytes_step(chain, item, limits, byte_in, gain_kv, w_key, w_value, q_t, keys, values, ga, stats, mlp, mlp_scale, begun):
    items, slot, width = byte_in.shape
    rows = width + QK
    last = item == items - 1
    inputs = [limits, byte_in, gain_kv, w_key, w_value, q_t, keys, values, ga, stats]
    if last:
        inputs += [mlp]
    aliases = {}
    if begun:
        count = len(inputs)
        inputs += begun
        aliases = {count: 1, count + 1: 2}
    outs = [shape((slot, width), f32), shape((rows, V), f32), shape((1, width), f32)]
    if last:
        outs += [shape((rows // 2, V), bf16)] * 2
    return chain.launch(
        functools.partial(bytes_kernel, item, last, mlp_scale),
        inputs,
        outs,
        24,
        "bytes_step",
        6.0,
        aliases=aliases,
    )


def store_kernel(*refs):
    count = (len(refs) - 3) // 2
    sources, outs, (sems,) = refs[: 2 * count], refs[2 * count : -1], refs[-1:]
    copies = [
        pltpu.make_async_copy(source, outs[at // count].at[at % count], sems.at[at])
        for at, source in enumerate(sources)
    ]
    for copy in copies:
        copy.start()
    for copy in copies:
        copy.wait()


def store(chain, made, grads):
    outs = [shape((len(arrays),) + arrays[0].shape, arrays[0].dtype) for arrays in (made, grads)]
    return chain.launch(
        store_kernel,
        (*made, *grads),
        outs,
        4,
        "store",
        2,
        far_out=(0, 1),
        scratch=[pltpu.SemaphoreType.DMA((len(made) + len(grads),))],
    )


def swap_bit(array, axis, bit):
    size = lax.axis_size(axis)
    return lax.ppermute(array, axis, [(i, i ^ (1 << bit)) for i in range(size)])


def bit_of(axis, bit):
    return (lax.axis_index(axis) >> bit) & 1


def bits_of(axis):
    return [(axis, bit) for bit in range(lax.axis_size(axis).bit_length() - 1)]


def split_kernel(step, keep_ref, got_ref, kept_ref, sent_ref):
    half = kept_ref.shape[0]
    upper = place_bit(*step) != 0
    total = (keep_ref[...].astype(f32) + got_ref[...].astype(f32)).astype(bf16)
    kept_ref[...] = jnp.where(upper, total[half:], total[:half])
    sent_ref[...] = jnp.where(upper, total[:half], total[half:])


def split_sum(chain, step, keep, got):
    rows, width = keep.shape
    half = rows // 2
    if half % 8 == 0:
        kernel = functools.partial(split_kernel, step)
        outs = [shape((half, width), bf16)] * 2
        return chain.launch(kernel, (keep, got), outs, 8, "split_sum")
    total = (keep.astype(f32) + got.astype(f32)).astype(bf16)
    take = lambda side: lax.dynamic_slice_in_dim(total, side * half, half, 0)
    bit = bit_of(*step)
    return take(bit), take(1 - bit)


def sum_kernel(keep_ref, got_ref, out_ref):
    out_ref[...] = (keep_ref[...].astype(f32) + got_ref[...].astype(f32)).astype(bf16)


def plain_sum(chain, keep, got):
    return chain.launch(sum_kernel, (keep, got), [shape(keep.shape, bf16)], 8, "plain_sum")[0]


def halves_kernel(steps, cut, *refs):
    count = len(steps)
    keeps, gots, outs = refs[:count], refs[count : 2 * count], refs[2 * count :]
    stacked = len(outs) == 2
    for at, (step, keep_ref, got_ref) in enumerate(zip(steps, keeps, gots)):
        upper = place_bit(*step) != 0
        rows = keep_ref.shape[0] // cut
        part = pl.ds(at * rows if cut > 1 else 0, rows)
        total = (keep_ref[part, :].astype(f32) + got_ref[part, :].astype(f32)).astype(bf16)
        half = rows // 2
        kept_ref, sent_ref = outs if stacked else (outs[at], outs[count + at])
        part = pl.ds(at * half if stacked else 0, half)
        kept_ref[part, :] = jnp.where(upper, total[half:], total[:half])
        sent_ref[part, :] = jnp.where(upper, total[:half], total[half:])


def sum_halves(chain, steps, keeps, gots, cut=1, stacked=False):
    count = len(steps)
    rows, width = keeps[0].shape[0] // cut, keeps[0].shape[1]
    kernel = functools.partial(halves_kernel, steps, cut)
    if stacked:
        outs = [shape((rows // 2 * count, width), bf16)] * 2
        return chain.launch(kernel, (*keeps, *gots), outs, 12, "sum_halves")
    outs = [shape((rows // 2, width), bf16)] * (2 * count)
    results = chain.launch(kernel, (*keeps, *gots), outs, 12, "sum_halves")
    return results[:count], results[count:]


def join_kernel(steps, split, stacked, *refs):
    count = len(steps)
    arrays = 1 if split else count
    mines, others, outs = refs[:arrays], refs[arrays : 2 * arrays], refs[2 * arrays :]
    for at, step in enumerate(steps):
        upper = place_bit(*step) != 0
        mine_ref, other_ref = (mines[0], others[0]) if split else (mines[at], others[at])
        half = mine_ref.shape[0] // (count if split else 1)
        part = pl.ds(at * half if split else 0, half)
        mine, other = mine_ref[part, :], other_ref[part, :]
        out_ref = outs[0] if stacked else outs[at]
        first = 2 * half * at if stacked else 0
        out_ref[pl.ds(first, half), :] = jnp.where(upper, other, mine)
        out_ref[pl.ds(first + half, half), :] = jnp.where(upper, mine, other)


def join(chain, steps, mines, others, stacked=False):
    count = len(steps)
    rows, width = mines[0].shape
    split = len(mines) == 1
    if split:
        rows //= count
    sizes = [(2 * rows * count, width)] if stacked else [(2 * rows, width)] * count
    kernel = functools.partial(join_kernel, steps, split, stacked)
    outs = [shape(size, bf16) for size in sizes]
    return chain.launch(kernel, (*mines, *others), outs, 12, "join")


def whole_sum(chain, keep, send, item_bits, seq_bits):
    got = swap_bit(send, *item_bits[0])
    orders = (item_bits[1:] + seq_bits, seq_bits[:1] + item_bits[1:] + seq_bits[1:])
    steps = list(zip(*orders))
    common = next(i for i, step in enumerate(steps) if step[0] == step[1])
    yield
    keeps, sends = sum_halves(chain, steps[0], [keep] * 2, [got] * 2, 2, common == 0)
    for at in range(common):
        gots = [swap_bit(send, *one) for send, one in zip(sends, steps[at])]
        yield
        keeps, sends = sum_halves(chain, steps[at + 1], keeps, gots, 1, at + 1 == common)
    keep, send = keeps, sends
    shared = [step[0] for step in steps[common:]]
    for step, following in zip(shared, shared[1:-1]):
        got = swap_bit(send, *step)
        yield
        rows = keep.shape[0] // 2
        keep, send = sum_halves(chain, (following,) * 2, [keep] * 2, [got] * 2, 2, True)
    got = swap_bit(send, *shared[-2])
    yield
    total = plain_sum(chain, keep, got)
    got = swap_bit(total, *shared[-1])
    yield
    total = plain_sum(chain, total, got)
    totals = [total]
    for at in range(len(shared) - 2, -1, -1):
        got = swap_bit(totals[0], *shared[at])
        yield
        totals = join(chain, (shared[at],) * 2, totals, [got], at > 0)
    for step in steps[common - 1 :: -1]:
        gots = [swap_bit(total, *one) for total, one in zip(totals, step)]
        yield
        totals = join(chain, step, totals, gots, step == steps[0])
    other = swap_bit(totals[0], *item_bits[0])
    yield totals[0], other


ROUTES = (
    (("b", ("",)), ("a", ("",)), ("x", ("",)), ("y", ("",))),
    (("a", ("x", "b")),),
    (("x", ("y", "b")), ("y", ("a", "b"))),
    (("y", ("bx", "ab")), ("x", ("ab",)), ("a", ("xy",))),
    (("a", ("bxy",)),),
)
SWAPS = {
    1: ("", "x", "y", "a", "b"),
    3: ("ax", "ab", "xy", "bx", "ay", "by"),
    5: ("bxy", "aby", "abx", "axy", "abxy"),
}
AWAITED = {2: ("ab",), 4: ("aby", "abx", "axy")}
BIT_OF = {"x": ("item", 1), "y": ("seq", 0), "a": ("seq", 1), "b": ("seq", 2)}


def glue_kernel(picks, count, *refs):
    sources, outs, (sems,) = refs[:count], refs[count:-1], refs[-1:]
    copies = []
    for out, pick in zip(outs, picks):
        for slot, (source, row) in enumerate(pick):
            copies.append(
                pltpu.make_async_copy(sources[source].at[row], out.at[slot], sems.at[len(copies)])
            )
            copies[-1].start()
    for copy in copies:
        copy.wait()


def glue(chain, held, groups, awaited, time):
    arrays = []
    for name in [name for group in groups for name in group] + list(awaited):
        if not any(held[name][0] is array for array in arrays):
            arrays.append(held[name][0])
    index = lambda array: next(i for i, one in enumerate(arrays) if one is array)
    picks = [[(index(held[name][0]), held[name][1]) for name in group] for group in groups]
    block = arrays[0].shape[1:]
    return chain.launch(
        functools.partial(glue_kernel, picks, len(arrays)),
        arrays,
        [shape((len(group),) + block, bf16) for group in groups],
        4,
        "glue",
        time,
        far_in=range(len(arrays)),
        far_out=range(len(groups)),
        scratch=[pltpu.SemaphoreType.DMA((sum(len(group) for group in groups),))],
    )


def spread_kernel(masks, block_ref, *refs):
    outs, (wide_s, sems) = refs[4:8], refs[8:]
    seq, item = lax.axis_index("seq"), lax.axis_index("item")
    rows = wide_s.shape[1]
    copies = []
    for slot, (item_mask, seq_mask) in enumerate(masks):
        wide_s[slot] = block_ref[slot].astype(f32)
        owner_item, owner_seq = item ^ item_mask, seq ^ seq_mask
        first = owner_seq * 4 + (owner_item & 1) * 2 + (owner_item >> 1)
        target = pl.ds(pl.multiple_of(first * rows, 8), rows)
        at = 0
        for index, out in enumerate(outs):
            size = out.shape[1]
            copy = pltpu.make_async_copy(
                wide_s.at[slot, :, pl.ds(at, size)], out.at[target, :], sems.at[slot, index]
            )
            copy.start()
            copies.append(copy)
            at += size
    for copy in copies:
        copy.wait()


def spread(chain, names, sibling, blocks, outs):
    masks = [
        (2 * ("x" in name) + sibling, ("y" in name) + 2 * ("a" in name) + 4 * ("b" in name))
        for name in names
    ]
    number = len(names)
    return chain.launch(
        functools.partial(spread_kernel, masks),
        (blocks, *outs),
        [shape(out.shape, f32) for out in outs],
        16,
        "spread",
        2.3,
        far_in=range(1, 5),
        far_out=range(4),
        scratch=[
            pltpu.VMEM(blocks.shape, f32),
            pltpu.SemaphoreType.DMA((number, 4)),
        ],
        aliases={1 + i: i for i in range(4)},
    )


def blank_kernel(*refs):
    pass


def gather_blocks(chain, keep, got, groups):
    block = plain_sum(chain, keep, got)[None]
    held = {"": (block, 0)}
    for level, sends in enumerate(ROUTES + ((),)):
        swap = SWAPS.get(level)
        if level == 0:
            arrays = [block] * len(sends)
        else:
            wanted = [names for _, names in sends] + ([swap] if swap else [])
            arrays = glue(chain, held, wanted, AWAITED.get(level, ()), 50 if level == 1 else 2)
        for (along, names), array in zip(sends, arrays):
            moved = swap_bit(array, *BIT_OF[along])
            for row, name in enumerate(names):
                held["".join(sorted(name + along))] = (moved, row)
        if swap:
            groups.append((swap, arrays[-1], swap_bit(arrays[-1], "item", 0)))
        yield


def spread_blocks(chain, rows, widths, groups):
    outs = [shape((32 * rows, width), f32) for width in widths]
    outs = chain.launch(blank_kernel, (), outs, 4, "blanks", far_out=range(4))
    while True:
        at, sibling = yield outs
        outs = spread(chain, groups[at][0], sibling, groups[at][1 + sibling], outs)


def last_kernel(
    slab, mine_ref, other_ref, resid_ref, lat_ref, gain_ref, wq_ref,
    value_ref, key_ref, query_ref, latent_ref, gain_kv_ref, gain_q_ref, gain_mlp_ref, resid_s,
):
    byte_width = value_ref.shape[0]
    latents, width = lat_ref.shape
    upper = place_bit("item", 0) != 0
    half = mine_ref.shape[0]
    rest = byte_width - half
    value_ref[pl.ds(0, half), :] = jnp.where(upper, other_ref[...], mine_ref[...]).astype(f32)
    second = jnp.where(upper, mine_ref[...], other_ref[...])
    value_ref[pl.ds(half, rest), :] = second[:rest].astype(f32)
    lower = second[rest:].astype(f32)
    for at in range(0, byte_width, QK):
        key_ref[pl.ds(at, QK), :] = lower[:, at : at + QK]
    query_t = (lower[:, byte_width : byte_width + latents] * SCALE).astype(bf16)
    gains = lower[:, byte_width + latents :]
    row = 0
    for ref in (gain_kv_ref, gain_mlp_ref):
        count = ref.shape[0] // QK
        ref[...] = jnp.concatenate([gains[row + i : row + i + 1] for i in range(count)], axis=1).reshape(-1)
        row += count
    hat, inverse = normalize(lat_ref[...].astype(f32))
    gain = row_of(gain_ref)
    lat_low = (hat * gain).astype(bf16)
    query_ref[...] = dot_nt(lat_low.T, query_t)
    grad_lat = dot_nt(query_t.T, wq_ref[...])
    gain_q_ref[...] = jnp.sum(grad_lat * hat, axis=0)
    parts = width // latents
    for rank in range(latents // slab):
        for part in range(parts):
            resid_s[pl.ds(rank * slab, slab), pl.ds(part * latents, latents)] = resid_ref[
                pl.ds((rank * parts + part) * slab, slab), :
            ]
    latent_ref[...] = resid_s[...] + norm_back(grad_lat * gain, hat, inverse)


def last_step(chain, n_seq, sums, resid, latent_init, gain_q, w_query):
    latents, width = latent_init.shape
    byte_width = 2 * sums[0].shape[0] - QK
    dims = [(byte_width, V), (byte_width, QK), (width, QK), (latents, width)]
    dims += [(byte_width,), (width,), (width,)]
    return chain.launch(
        functools.partial(last_kernel, latents // n_seq),
        (*sums, resid, latent_init, gain_q, w_query),
        [shape(dim, f32) for dim in dims],
        16,
        "last_step",
        4.8,
        scratch=[pltpu.VMEM((latents, width), f32)],
    )


ORDER = "abcad0b1ca2badc3badcbdAcdBCD"

TAIL = "pmpAoppmpapmBpmpmbCpc"


def per_device(
    byte_in,
    lengths,
    latent_init,
    gain_kv,
    gain_q,
    gain_mlp,
    w_query,
    w_key,
    w_value,
    w_out,
    w_up,
    w_down,
    d_out,
):
    items, slot, byte_width = byte_in.shape
    latents, width = latent_init.shape
    n_item, n_seq = lax.axis_size("item"), lax.axis_size("seq")
    item_bits, seq_bits = bits_of("item"), bits_of("seq")
    chain = Chain(byte_in)
    keys, values, acts, halves = [None] * items, [None] * items, [None] * items, [None] * items
    gas, stats = [None] * items, [None] * items
    q_t, limits = None, None
    carried = None
    made, grads = [None] * items, [None] * items

    def travel(item):
        nonlocal q_t, limits
        operands = (byte_in, gain_kv, w_key, w_value)
        if item == 0:
            limits, q_t, *made = attend_first(
                chain, lengths, *operands, latent_init, gain_q, w_query
            )
        else:
            made = attend(chain, item, limits, *operands, q_t)
        keys[item], values[item], keep, send = made
        got = swap_bit(send, "seq", 0)
        yield
        mine = merge(chain, 0, keep, got)
        if n_seq == 8:
            inward = lax.ppermute(mine, "seq", [(0, 2), (1, 3), (6, 4), (7, 5)])
            yield
            mine = merge(chain, 2, mine, inward)
            across = lax.ppermute(mine, "seq", [(2, 4), (3, 5), (4, 2), (5, 3)])
            yield
            mine = merge(chain, 2, mine, across)
            outward = lax.ppermute(mine, "seq", [(2, 0), (3, 1), (4, 6), (5, 7)])
            yield
            mine = choose(chain, mine, outward)
        else:
            for axis, bit in seq_bits[1:]:
                got = swap_bit(mine, axis, bit)
                yield
                mine = merge(chain, bit, mine, got)
        yield mine, swap_bit(mine, "seq", 0)

    ways = [travel(item) for item in range(items)]
    for letter in ORDER:
        if letter.isdigit():
            acts[int(letter)] = cotangent(chain, int(letter), d_out, w_down)
            continue
        item = "abcd".index(letter.lower())
        if letter.islower():
            halves[item] = next(ways[item])
            continue
        for halves_item in ways[item]:
            halves[item] = halves_item
        made[item], gas[item], stats[item], mlp, *factors = latent_step(
            chain,
            item,
            width // n_seq,
            *halves[item],
            latent_init,
            gain_mlp,
            d_out,
            acts[item],
            (w_out, w_up, w_down),
            carried,
        )
        carried = (mlp, *factors[:3])
    sums = factors[3:]

    begun = None

    def go_back(item):
        nonlocal begun
        args = (limits, byte_in, gain_kv, w_key, w_value, q_t, keys[item], values[item], gas[item], stats[item])
        grads[item], total, gains, *halves = bytes_step(chain, item, *args, mlp, 1.0 / n_seq, begun)
        begun = (total, gains)
        return halves

    keep, send = sums
    got = swap_bit(send, *item_bits[0])
    go_back(0)
    for step, following in zip(item_bits, item_bits[1:]):
        keep, send = split_sum(chain, following, keep, got)
        got = swap_bit(send, *following)
    go_back(1)
    widths = (width, width, width, latents)
    direct = (n_item, n_seq) == (4, 8)
    if direct:
        groups = []
        latent_way = gather_blocks(chain, keep, got, groups)
        next(latent_way)
        spread_way = spread_blocks(chain, keep.shape[0], widths, groups)
        next(spread_way)
    else:
        latent_piece = plain_sum(chain, keep, got)
        latent_all = lax.all_gather(latent_piece, ("item", "seq"), axis=0, tiled=False)
    go_back(2)
    keep, send = go_back(3)
    byte_way = whole_sum(chain, keep, send, item_bits, seq_bits)
    if direct:
        for letter in TAIL:
            if letter == "o":
                latents_out, byte_grad = store(chain, made, grads)
            elif letter == "m":
                next(latent_way)
            elif letter == "p":
                byte_halves = next(byte_way)
            else:
                group = "abc".index(letter.lower()), int(letter.islower())
                whole_grads = spread_way.send(group)
    else:
        count = len(item_bits)
        blocks = latent_all.reshape((2,) * count + (n_seq,) + latent_piece.shape)
        turn = [count] + list(range(count))[::-1] + [count + 1, count + 2]
        blocks = blocks.transpose(turn).reshape(-1, sum(widths)).astype(f32)
        whole_grads = [blocks[:, i * width : i * width + size] for i, size in enumerate(widths)]
        for byte_halves in byte_way:
            pass
        latents_out, byte_grad = store(chain, made, grads)
    out_grad, up_grad, down_grad, resid = whole_grads
    value_grad, key_grad, query_grad, latent_grad, gain_kv_grad, gain_q_grad, gain_mlp_grad = last_step(
        chain, n_seq, byte_halves, resid, latent_init, gain_q, w_query
    )
    return (
        latents_out,
        byte_grad,
        latent_grad,
        gain_kv_grad,
        gain_q_grad,
        gain_mlp_grad,
        query_grad,
        key_grad,
        value_grad,
        out_grad,
        up_grad,
        down_grad,
    )


def solution(mesh):
    placed = (P("item", "seq", None), P("item")) + (P(),) * 10 + (P("item", None, None),)
    return jax.shard_map(
        per_device,
        mesh=mesh,
        in_specs=placed,
        out_specs=(P("item", None, None), P("item", "seq", None)) + (P(),) * 10,
        check_vma=False,
    )
```

```python
import functools

import jax
import jax.numpy as jnp
from jax import lax
from jax.experimental import pallas as pl
from jax.experimental.pallas import tpu as pltpu
from jax.sharding import PartitionSpec as P

HEADS = 8
QK = 256
V = 1280
QK_HEAD = QK // HEADS
V_HEAD = V // HEADS
SCALE = QK_HEAD**-0.5
ROWS = V + 2 * HEADS
EPS = 1e-05
NEG = -1e30
MIB = 1 << 20
f32 = jnp.float32
bf16 = jnp.bfloat16

IN_VMEM = pl.BlockSpec(memory_space=pltpu.VMEM)
IN_SMEM = pl.BlockSpec(memory_space=pltpu.SMEM)
FAR = pl.BlockSpec(memory_space=pltpu.HBM)


def dot(a, b):
    return jnp.dot(a, b, preferred_element_type=f32)


def dot_nt(a, b):
    return lax.dot_general(a, b, (((1,), (1,)), ((), ())), preferred_element_type=f32)


def shape(dims, dtype):
    return jax.ShapeDtypeStruct(dims, dtype)


def cost(microseconds):
    return pl.CostEstimate(
        flops=int(microseconds * 5e8), bytes_accessed=int(microseconds * 1.5e6), transcendentals=0
    )


class Chain:
    def __init__(self, token):
        self.token = token

    def launch(
        self, kernel, inputs, outs, mib, name, time=0.7, far_in=(), far_out=(), scratch=(), aliases=None, scalars=()
    ):
        count, made = len(inputs), len(outs)

        def body(*refs):
            refs[count + 1 + made][...] = jnp.zeros((8, 128), f32)
            kernel(*refs[:count], *refs[count + 1 : count + 1 + made], *refs[count + 2 + made :])

        where = {i: FAR for i in far_in} | {i: IN_SMEM for i in scalars}
        *results, self.token = pl.pallas_call(
            body,
            out_shape=[*outs, shape((8, 128), f32)],
            in_specs=[where.get(i, IN_VMEM) for i in range(count)] + [FAR],
            out_specs=[FAR if i in far_out else IN_VMEM for i in range(made)] + [IN_VMEM],
            scratch_shapes=scratch,
            input_output_aliases=aliases or {},
            compiler_params=pltpu.CompilerParams(vmem_limit_bytes=mib * MIB),
            cost_estimate=cost(time),
            name=name,
        )(*inputs, self.token)
        return results


def row_of(ref):
    return ref[...].reshape(1, -1)


def place_bit(axis, bit):
    return (lax.axis_index(axis) >> bit) & 1


def normalize(vector, axis=-1):
    average = jnp.mean(vector, axis=axis, keepdims=True)
    centered = vector - average
    inverse = lax.rsqrt(jnp.mean(centered * centered, axis=axis, keepdims=True) + EPS)
    return (centered * inverse, inverse)


def norm_back(grad_hat, hat, inverse, axis=-1):
    return inverse * (
        grad_hat
        - jnp.mean(grad_hat, axis=axis, keepdims=True)
        - hat * jnp.mean(grad_hat * hat, axis=axis, keepdims=True)
    )


def query_kernel(lat_ref, gain_ref, wq_ref, q_ref):
    hat, _ = normalize(lat_ref[...].astype(f32))
    lat_low = (hat * row_of(gain_ref)).astype(bf16)
    q_ref[...] = dot(lat_low, wq_ref[...]).T.astype(bf16)


def spread_queries(q_t):
    channel = lax.broadcasted_iota(jnp.int32, q_t.shape, 0) // QK_HEAD
    zeros = jnp.zeros_like(q_t)
    return jnp.concatenate([jnp.where(channel == head, q_t, zeros) for head in range(HEADS)], axis=1)


def attend_kernel(
    at, item, limits_ref, x_ref, gain_ref, wk_ref, wv_ref, q_ref, k_ref, v_ref, keep_ref, send_ref
):
    low = place_bit("seq", 0)
    hat, _ = normalize(x_ref[at].astype(f32))
    byte_low = (hat * row_of(gain_ref)).astype(bf16)
    keys = dot(byte_low, wk_ref[...]).astype(bf16)
    values = dot(byte_low, wv_ref[...])
    k_ref[...] = keys
    v_ref[...] = values.astype(bf16)
    values_t = values.T.astype(bf16)
    q_t = q_ref[...]
    latents = q_t.shape[1]
    half = latents // 2
    inside = lax.broadcasted_iota(jnp.int32, (keys.shape[0], latents), 0) < limits_ref[pl.ds(item, 1), :]

    def put(first, block):
        left, right = block[:, :half], block[:, half:]
        rows = pl.ds(first, block.shape[0])
        keep_ref[rows, :] = jnp.where(low == 0, left, right).astype(bf16)
        send_ref[rows, :] = jnp.where(low == 0, right, left).astype(bf16)

    every = dot(keys, spread_queries(q_t)) * SCALE
    totals, weights, inverses = [], [], []
    for head in range(HEADS):
        scores = every[:, head * latents : (head + 1) * latents]
        scores = jnp.where(inside, scores, NEG)
        top = jnp.max(scores, axis=0, keepdims=True)
        powers = jnp.exp(scores - top)
        total = jnp.sum(powers, axis=0, keepdims=True)
        weights.append(powers.astype(bf16))
        inverses.append(1.0 / total)
        totals.append(top + jnp.log(total))
    for head in range(HEADS):
        rows = slice(head * V_HEAD, (head + 1) * V_HEAD)
        put(head * V_HEAD, dot(values_t[rows], weights[head]) * inverses[head])
    lse = jnp.concatenate(totals, axis=0)
    high = lse.astype(bf16).astype(f32)
    put(V, jnp.concatenate([high, lse - high], axis=0))


def first_kernel(
    lengths_ref, lat_ref, gain_q_ref, wq_ref, x_ref, gain_ref, wk_ref, wv_ref,
    limits_ref, q_ref, k_ref, v_ref, keep_ref, send_ref, x_s, wk_s, wv_s, sems, lat_s, wq_s,
):
    rows = wv_ref.shape[0] // 4
    pairs = [(lat_ref, lat_s), (wq_ref, wq_s), (x_ref.at[pl.ds(0, 1)], x_s), (wk_ref, wk_s)]
    pairs += [(wv_ref.at[pl.ds(i * rows, rows)], wv_s.at[pl.ds(i * rows, rows)]) for i in range(4)]
    copies = [pltpu.make_async_copy(src, dst, sems.at[i]) for i, (src, dst) in enumerate(pairs)]
    for copy in copies:
        copy.start()
    before = lax.axis_index("seq") * x_ref.shape[1]
    for item in range(x_ref.shape[0]):
        limits_ref[pl.ds(item, 1), :] = jnp.full((1, limits_ref.shape[1]), lengths_ref[item] - before, jnp.int32)
    for copy in copies[:2]:
        copy.wait()
    query_kernel(lat_s, gain_q_ref, wq_s, q_ref)
    for copy in copies[2:]:
        copy.wait()
    attend_kernel(0, 0, limits_ref, x_s, gain_ref, wk_s, wv_s, q_ref, k_ref, v_ref, keep_ref, send_ref)


def attend_outs(byte_in, latents):
    slot = byte_in.shape[1]
    payload = shape((ROWS, latents // 2), bf16)
    return [shape((slot, QK), bf16), shape((slot, V), bf16), payload, payload]


def attend(chain, item, limits, byte_in, gain_kv, w_key, w_value, q_t):
    return chain.launch(
        functools.partial(attend_kernel, item, item),
        (limits, byte_in, gain_kv, w_key, w_value, q_t),
        attend_outs(byte_in, q_t.shape[1]),
        18,
        "attend",
        3.9,
    )


def attend_first(chain, lengths, byte_in, gain_kv, w_key, w_value, latent_init, gain_q, w_query):
    latents = latent_init.shape[0]
    one = (1,) + byte_in.shape[1:]
    shapes = [one, w_key.shape, w_value.shape]
    return chain.launch(
        first_kernel,
        (lengths, latent_init, gain_q, w_query, byte_in, gain_kv, w_key, w_value),
        [shape((byte_in.shape[0], latents), jnp.int32), shape((QK, latents), bf16)]
        + attend_outs(byte_in, latents),
        60,
        "attend_first",
        6,
        far_in=(1, 3, 4, 6, 7),
        scalars=(0,),
        scratch=[pltpu.VMEM(dims, bf16) for dims in shapes]
        + [pltpu.SemaphoreType.DMA((8,))]
        + [pltpu.VMEM(dims, bf16) for dims in (latent_init.shape, w_query.shape)],
    )


def merge_kernel(bit, mine_ref, other_ref, out_ref):
    swap = place_bit("seq", bit) != 0

    def totals(ref):
        return ref[V : V + HEADS, :].astype(f32) + ref[V + HEADS :, :].astype(f32)

    def ordered(mine, other):
        return jnp.where(swap, other, mine), jnp.where(swap, mine, other)

    lse_a, lse_b = ordered(totals(mine_ref), totals(other_ref))
    top = jnp.maximum(lse_a, lse_b)
    weight_a = jnp.exp(lse_a - top)
    weight_b = jnp.exp(lse_b - top)
    total = weight_a + weight_b
    lse = top + jnp.log(total)
    weight_a = weight_a / total
    weight_b = weight_b / total
    for head in range(HEADS):
        rows = pl.ds(head * V_HEAD, V_HEAD)
        sums_a, sums_b = ordered(mine_ref[rows, :].astype(f32), other_ref[rows, :].astype(f32))
        out_ref[rows, :] = (
            sums_a * weight_a[head : head + 1] + sums_b * weight_b[head : head + 1]
        ).astype(bf16)
    high = lse.astype(bf16).astype(f32)
    out_ref[pl.ds(V, 2 * HEADS), :] = jnp.concatenate([high, lse - high], axis=0).astype(bf16)


def merge(chain, bit, mine, other):
    kernel = functools.partial(merge_kernel, bit)
    return chain.launch(kernel, (mine, other), [shape(mine.shape, bf16)], 8, "merge")[0]


def choose_kernel(mine_ref, other_ref, out_ref):
    line = lax.axis_index("seq") >> 1
    inner = (line == 1) | (line == 2)
    out_ref[...] = jnp.where(inner, mine_ref[...], other_ref[...])


def choose(chain, mine, other):
    return chain.launch(choose_kernel, (mine, other), [shape(mine.shape, bf16)], 8, "choose")[0]


def cotangent_kernel(item, g_ref, w_ref, act_ref):
    def one(at, carry):
        rows = pl.ds(pl.multiple_of(at * TILE, TILE), TILE)
        act_ref[:, rows] = dot_nt(g_ref[item], w_ref[rows, :])
        return carry

    lax.fori_loop(0, w_ref.shape[0] // TILE, one, 0)


def cotangent(chain, item, d_out, w_down):
    outs = [shape((d_out.shape[1], w_down.shape[0]), f32)]
    kernel = functools.partial(cotangent_kernel, item)
    return chain.launch(kernel, (d_out, w_down), outs, 12, "cotangent",
        1.6)[0]


TILE = 256
ROOT_HALF = 0.7071067811865476
ROOT_TWO_PI = 0.3989422804014327


def latent_kernel(
    item, last, mine_ref, other_ref, lat_ref, gain_ref, g_ref, act_ref, w_out, w_up, w_down, *refs
):
    first = item == 0
    if not first:
        mlp_in, _, _, _, *refs = refs
    out_ref, ga_ref, stat_ref, mlp_ref, part_ref, branch_ref, gup_ref, *refs = refs
    if last:
        keep_ref, send_ref, *refs = refs
    att_s, turn_s = refs
    low, core = place_bit("seq", 0), place_bit("item", 0)
    rank = lax.axis_index("seq")
    latents, width = lat_ref.shape
    ff = act_ref.shape[1]
    share = part_ref.shape[1]
    g = g_ref[item]
    own = pl.ds(item * latents, latents)
    mine, other = mine_ref[...], other_ref[...]
    left = jnp.where(low == 0, mine, other)
    right = jnp.where(low == 0, other, mine)
    whole = jnp.concatenate([left, right], axis=1)
    att_s[...] = whole[:V]
    stat_ref[:HEADS, :] = whole[V : V + HEADS].astype(f32) + whole[V + HEADS :].astype(f32)
    attended = whole[:V].T
    rows = pl.ds(pl.multiple_of(rank * share, 16), share)

    part_ref[0, :, own] = att_s[rows, :]
    mixed = lat_ref[...].astype(f32) + jnp.concatenate(
        [dot(attended, w_out[:, pl.ds(at, TILE)]) for at in range(0, width, TILE)], axis=1
    )
    hat, inverse = normalize(mixed)
    gain = row_of(gain_ref)
    hidden = (hat * gain).astype(bf16)
    activated, grad_up = [], []
    for at in range(0, ff, TILE):
        upward = dot(hidden, w_up[:, pl.ds(at, TILE)])
        bell = 0.5 + 0.5 * lax.erf(upward * ROOT_HALF)
        slope = bell + upward * (ROOT_TWO_PI * jnp.exp(-0.5 * upward * upward))
        activated.append((upward * bell).astype(bf16))
        grad_up.append((act_ref[:, pl.ds(at, TILE)] * slope).astype(bf16))
    activated = jnp.concatenate(activated, axis=1)
    grad_up = jnp.concatenate(grad_up, axis=1)
    for at in range(0, width, TILE):
        block = mixed[:, at : at + TILE] + dot(activated, w_down[:, pl.ds(at, TILE)])
        out_ref[:, pl.ds(at, TILE)] = block.astype(bf16)
    turn_s[...] = activated.T
    part_ref[2, :, own] = turn_s[rows, :]
    grad_hidden = jnp.concatenate(
        [dot_nt(grad_up, w_up[pl.ds(at, TILE), :]) for at in range(0, width, TILE)], axis=1
    )
    turn_s[...] = hidden.T
    part_ref[1, :, own] = turn_s[rows, :]
    gup_ref[own, :] = grad_up
    mlp = jnp.sum(grad_hidden * hat, axis=0, keepdims=True)
    mlp_ref[...] = mlp if first else mlp + mlp_in[...]
    grad_mixed = g.astype(f32) + norm_back(grad_hidden * gain, hat, inverse)
    branch = grad_mixed.astype(bf16)
    branch_ref[own, :] = branch
    for at in range(0, V, TILE):
        ga_ref[pl.ds(at, TILE), :] = dot_nt(w_out[pl.ds(at, TILE), :], branch).astype(bf16)
    for head in range(HEADS):
        part = pl.ds(head * V_HEAD, V_HEAD)
        stat_ref[pl.ds(HEADS + head, 1), :] = jnp.sum(
            ga_ref[part, :].astype(f32) * att_s[part, :].astype(f32), axis=0, keepdims=True
        )
    if last:
        slab = latents * share // width
        few = [pl.ds(pl.multiple_of(i * latents + rank * slab, 16), slab) for i in range(item + 1)]
        resid = sum(branch_ref[one, :].astype(f32) for one in few)
        parts = (
            dot(part_ref[0], branch_ref[...]),
            dot(part_ref[1], gup_ref[...]),
            dot(part_ref[2], g_ref[...].reshape(branch_ref.shape)),
            jnp.concatenate([resid[:, at : at + latents] for at in range(0, width, latents)], axis=0),
        )
        half = share // 2
        at = 0
        for part in parts:
            lanes = pl.ds(at, part.shape[1])
            lower, upper = part[:half], part[half:]
            keep_ref[:, lanes] = jnp.where(core == 0, lower, upper).astype(bf16)
            send_ref[:, lanes] = jnp.where(core == 0, upper, lower).astype(bf16)
            at += part.shape[1]


def latent_step(chain, item, share, mine, other, lat, gain, g, act, weights, carried):
    items, latents, width = g.shape
    ff = act.shape[1]
    total = 2 * width + ff + latents
    last = item == items - 1
    inputs = [mine, other, lat, gain, g, act, *weights]
    aliases = {}
    if carried:
        inputs += carried
        aliases = {10: 4, 11: 5, 12: 6}
    outs = [
        shape((latents, width), bf16),
        shape((V, latents), bf16),
        shape((2 * HEADS, latents), f32),
        shape((1, width), f32),
        shape((3, share, items * latents), bf16),
        shape((items * latents, width), bf16),
        shape((items * latents, ff), bf16),
    ]
    if last:
        outs += [shape((share // 2, total), bf16)] * 2
    return chain.launch(
        functools.partial(latent_kernel, item, last),
        inputs,
        outs,
        20,
        "latent_step",
        8.4,
        scratch=[pltpu.VMEM((V, latents), bf16), pltpu.VMEM((width, latents), bf16)],
        aliases=aliases,
    )


def bytes_kernel(
    item, last, mlp_scale, limits_ref, x_ref, gain_ref, wk_ref, wv_ref, q_ref, k_ref, v_ref, ga_ref, stat_ref, *refs
):
    first = item == 0
    if last:
        mlp_ref, *refs = refs
    if not first:
        sum_in, gain_in, *refs = refs
    grad_ref, sum_ref, gain_out, *refs = refs
    if last:
        keep_ref, send_ref = refs
    core = place_bit("item", 0)
    slot, width = x_ref.shape[1:]

    def add(rows, lanes, part):
        at = (pl.ds(*rows), pl.ds(*lanes))
        sum_ref[at] = part if first else part + sum_in[at]

    hat, inverse = normalize(x_ref[item].astype(f32))
    gain = row_of(gain_ref)
    low_t = (hat * gain).T.astype(bf16)
    keys = k_ref[...]
    values = v_ref[...]
    keys_t = keys.T
    q_t = q_ref[...]
    latents = q_t.shape[1]
    inside = lax.broadcasted_iota(jnp.int32, (slot, latents), 0) < limits_ref[pl.ds(item, 1), :]

    every = dot(keys, spread_queries(q_t)) * SCALE
    grad_values, grad_keys = [], []
    softs, moves = [], []
    for head in range(HEADS):
        scores = every[:, head * latents : (head + 1) * latents]
        scores = jnp.where(inside, scores, NEG)
        soft = jnp.exp(scores - stat_ref[pl.ds(head, 1), :])
        part = slice(head * V_HEAD, (head + 1) * V_HEAD)
        grad_soft = dot(values[:, part], ga_ref[pl.ds(head * V_HEAD, V_HEAD), :])
        moves.append((soft * (grad_soft - stat_ref[pl.ds(HEADS + head, 1), :])).astype(bf16))
        softs.append(soft.astype(bf16))
    for head in range(HEADS):
        grad_attn = ga_ref[pl.ds(head * V_HEAD, V_HEAD), :]
        grad_values.append(dot_nt(grad_attn, softs[head]).astype(bf16))
    for head in range(HEADS):
        small = slice(head * QK_HEAD, (head + 1) * QK_HEAD)
        grad_keys.append((dot_nt(q_t[small], moves[head]) * SCALE).astype(bf16))
        add((width + head * QK_HEAD, QK_HEAD), (width, latents), dot(keys_t[small], moves[head]))
    grad_values = jnp.concatenate(grad_values, axis=0)
    grad_keys = jnp.concatenate(grad_keys, axis=0)
    grad_low = dot_nt(grad_values.T, wv_ref[...]) + dot_nt(grad_keys.T, wk_ref[...])
    gain_part = jnp.sum(grad_low * hat, axis=0, keepdims=True)
    gain_out[...] = gain_part if first else gain_part + gain_in[...]
    grad_ref[...] = norm_back(grad_low * gain, hat, inverse)
    for rows in range(0, width, TILE):
        block = low_t[rows : rows + TILE]
        add((rows, TILE), (0, V), dot_nt(block, grad_values))
        add((width, QK), (rows, TILE), dot_nt(block, grad_keys))

    if last:
        at = width
        for part in (gain_out[...], mlp_ref[...] * mlp_scale):
            for begin in range(0, part.shape[1], QK):
                sum_ref[pl.ds(at, 1), pl.ds(width + latents, QK)] = part[:, begin : begin + QK]
                at += 1
        half = sum_ref.shape[0] // 2
        kept = pl.ds(pl.multiple_of(core * half, 16), half)
        sent = pl.ds(pl.multiple_of((1 - core) * half, 16), half)
        keep_ref[...] = sum_ref[kept, :].astype(bf16)
        send_ref[...] = sum_ref[sent, :].astype(bf16)
    elif first:
        sum_ref[pl.ds(width, QK), pl.ds(width + latents, QK)] = jnp.zeros((QK, QK), f32)


def bytes_step(chain, item, limits, byte_in, gain_kv, w_key, w_value, q_t, keys, values, ga, stats, mlp, mlp_scale, begun):
    items, slot, width = byte_in.shape
    rows = width + QK
    last = item == items - 1
    inputs = [limits, byte_in, gain_kv, w_key, w_value, q_t, keys, values, ga, stats]
    if last:
        inputs += [mlp]
    aliases = {}
    if begun:
        count = len(inputs)
        inputs += begun
        aliases = {count: 1, count + 1: 2}
    outs = [shape((slot, width), f32), shape((rows, V), f32), shape((1, width), f32)]
    if last:
        outs += [shape((rows // 2, V), bf16)] * 2
    return chain.launch(
        functools.partial(bytes_kernel, item, last, mlp_scale),
        inputs,
        outs,
        24,
        "bytes_step",
        6.0,
        aliases=aliases,
    )


def store_kernel(*refs):
    count = (len(refs) - 3) // 2
    sources, outs, (sems,) = refs[: 2 * count], refs[2 * count : -1], refs[-1:]
    copies = [
        pltpu.make_async_copy(source, outs[at // count].at[at % count], sems.at[at])
        for at, source in enumerate(sources)
    ]
    for copy in copies:
        copy.start()
    for copy in copies:
        copy.wait()


def store(chain, made, grads):
    outs = [shape((len(arrays),) + arrays[0].shape, arrays[0].dtype) for arrays in (made, grads)]
    return chain.launch(
        store_kernel,
        (*made, *grads),
        outs,
        4,
        "store",
        2,
        far_out=(0, 1),
        scratch=[pltpu.SemaphoreType.DMA((len(made) + len(grads),))],
    )


def swap_bit(array, axis, bit):
    size = lax.axis_size(axis)
    return lax.ppermute(array, axis, [(i, i ^ (1 << bit)) for i in range(size)])


def bit_of(axis, bit):
    return (lax.axis_index(axis) >> bit) & 1


def bits_of(axis):
    return [(axis, bit) for bit in range(lax.axis_size(axis).bit_length() - 1)]


def split_kernel(step, keep_ref, got_ref, kept_ref, sent_ref):
    half = kept_ref.shape[0]
    upper = place_bit(*step) != 0
    total = (keep_ref[...].astype(f32) + got_ref[...].astype(f32)).astype(bf16)
    kept_ref[...] = jnp.where(upper, total[half:], total[:half])
    sent_ref[...] = jnp.where(upper, total[:half], total[half:])


def split_sum(chain, step, keep, got):
    rows, width = keep.shape
    half = rows // 2
    if half % 8 == 0:
        kernel = functools.partial(split_kernel, step)
        outs = [shape((half, width), bf16)] * 2
        return chain.launch(kernel, (keep, got), outs, 8, "split_sum")
    total = (keep.astype(f32) + got.astype(f32)).astype(bf16)
    take = lambda side: lax.dynamic_slice_in_dim(total, side * half, half, 0)
    bit = bit_of(*step)
    return take(bit), take(1 - bit)


def sum_kernel(keep_ref, got_ref, out_ref):
    out_ref[...] = (keep_ref[...].astype(f32) + got_ref[...].astype(f32)).astype(bf16)


def plain_sum(chain, keep, got):
    return chain.launch(sum_kernel, (keep, got), [shape(keep.shape, bf16)], 8, "plain_sum")[0]


def halves_kernel(steps, cut, *refs):
    count = len(steps)
    keeps, gots, outs = refs[:count], refs[count : 2 * count], refs[2 * count :]
    stacked = len(outs) == 2
    for at, (step, keep_ref, got_ref) in enumerate(zip(steps, keeps, gots)):
        upper = place_bit(*step) != 0
        rows = keep_ref.shape[0] // cut
        part = pl.ds(at * rows if cut > 1 else 0, rows)
        total = (keep_ref[part, :].astype(f32) + got_ref[part, :].astype(f32)).astype(bf16)
        half = rows // 2
        kept_ref, sent_ref = outs if stacked else (outs[at], outs[count + at])
        part = pl.ds(at * half if stacked else 0, half)
        kept_ref[part, :] = jnp.where(upper, total[half:], total[:half])
        sent_ref[part, :] = jnp.where(upper, total[:half], total[half:])


def sum_halves(chain, steps, keeps, gots, cut=1, stacked=False):
    count = len(steps)
    rows, width = keeps[0].shape[0] // cut, keeps[0].shape[1]
    kernel = functools.partial(halves_kernel, steps, cut)
    if stacked:
        outs = [shape((rows // 2 * count, width), bf16)] * 2
        return chain.launch(kernel, (*keeps, *gots), outs, 12, "sum_halves")
    outs = [shape((rows // 2, width), bf16)] * (2 * count)
    results = chain.launch(kernel, (*keeps, *gots), outs, 12, "sum_halves")
    return results[:count], results[count:]


def join_kernel(steps, split, stacked, *refs):
    count = len(steps)
    arrays = 1 if split else count
    mines, others, outs = refs[:arrays], refs[arrays : 2 * arrays], refs[2 * arrays :]
    for at, step in enumerate(steps):
        upper = place_bit(*step) != 0
        mine_ref, other_ref = (mines[0], others[0]) if split else (mines[at], others[at])
        half = mine_ref.shape[0] // (count if split else 1)
        part = pl.ds(at * half if split else 0, half)
        mine, other = mine_ref[part, :], other_ref[part, :]
        out_ref = outs[0] if stacked else outs[at]
        first = 2 * half * at if stacked else 0
        out_ref[pl.ds(first, half), :] = jnp.where(upper, other, mine)
        out_ref[pl.ds(first + half, half), :] = jnp.where(upper, mine, other)


def join(chain, steps, mines, others, stacked=False):
    count = len(steps)
    rows, width = mines[0].shape
    split = len(mines) == 1
    if split:
        rows //= count
    sizes = [(2 * rows * count, width)] if stacked else [(2 * rows, width)] * count
    kernel = functools.partial(join_kernel, steps, split, stacked)
    outs = [shape(size, bf16) for size in sizes]
    return chain.launch(kernel, (*mines, *others), outs, 12, "join")


def whole_sum(chain, keep, send, item_bits, seq_bits):
    got = swap_bit(send, *item_bits[0])
    orders = (item_bits[1:] + seq_bits, seq_bits[:1] + item_bits[1:] + seq_bits[1:])
    steps = list(zip(*orders))
    common = next(i for i, step in enumerate(steps) if step[0] == step[1])
    yield
    keeps, sends = sum_halves(chain, steps[0], [keep] * 2, [got] * 2, 2, common == 0)
    for at in range(common):
        gots = [swap_bit(send, *one) for send, one in zip(sends, steps[at])]
        yield
        keeps, sends = sum_halves(chain, steps[at + 1], keeps, gots, 1, at + 1 == common)
    keep, send = keeps, sends
    shared = [step[0] for step in steps[common:]]
    for step, following in zip(shared, shared[1:-1]):
        got = swap_bit(send, *step)
        yield
        rows = keep.shape[0] // 2
        keep, send = sum_halves(chain, (following,) * 2, [keep] * 2, [got] * 2, 2, True)
    got = swap_bit(send, *shared[-2])
    yield
    total = plain_sum(chain, keep, got)
    got = swap_bit(total, *shared[-1])
    yield
    total = plain_sum(chain, total, got)
    totals = [total]
    for at in range(len(shared) - 2, -1, -1):
        got = swap_bit(totals[0], *shared[at])
        yield
        totals = join(chain, (shared[at],) * 2, totals, [got], at > 0)
    for step in steps[common - 1 :: -1]:
        gots = [swap_bit(total, *one) for total, one in zip(totals, step)]
        yield
        totals = join(chain, step, totals, gots, step == steps[0])
    other = swap_bit(totals[0], *item_bits[0])
    yield totals[0], other


ROUTES = (
    (("b", ("",)), ("a", ("",)), ("x", ("",)), ("y", ("",))),
    (("a", ("x", "b")),),
    (("x", ("y", "b")), ("y", ("a", "b"))),
    (("y", ("bx", "ab")), ("x", ("ab",)), ("a", ("xy",))),
    (("a", ("bxy",)),),
)
SWAPS = {
    1: ("", "x", "y", "a", "b"),
    3: ("ax", "ab", "xy", "bx", "ay", "by"),
    5: ("bxy", "aby", "abx", "axy", "abxy"),
}
AWAITED = {2: ("ab",), 4: ("aby", "abx", "axy")}
BIT_OF = {"x": ("item", 1), "y": ("seq", 0), "a": ("seq", 1), "b": ("seq", 2)}


def glue_kernel(picks, count, *refs):
    sources, outs, (sems,) = refs[:count], refs[count:-1], refs[-1:]
    copies = []
    for out, pick in zip(outs, picks):
        for slot, (source, row) in enumerate(pick):
            copies.append(
                pltpu.make_async_copy(sources[source].at[row], out.at[slot], sems.at[len(copies)])
            )
            copies[-1].start()
    for copy in copies:
        copy.wait()


def glue(chain, held, groups, awaited, time):
    arrays = []
    for name in [name for group in groups for name in group] + list(awaited):
        if not any(held[name][0] is array for array in arrays):
            arrays.append(held[name][0])
    index = lambda array: next(i for i, one in enumerate(arrays) if one is array)
    picks = [[(index(held[name][0]), held[name][1]) for name in group] for group in groups]
    block = arrays[0].shape[1:]
    return chain.launch(
        functools.partial(glue_kernel, picks, len(arrays)),
        arrays,
        [shape((len(group),) + block, bf16) for group in groups],
        4,
        "glue",
        time,
        far_in=range(len(arrays)),
        far_out=range(len(groups)),
        scratch=[pltpu.SemaphoreType.DMA((sum(len(group) for group in groups),))],
    )


def spread_kernel(masks, block_ref, *refs):
    outs, (wide_s, sems) = refs[4:8], refs[8:]
    seq, item = lax.axis_index("seq"), lax.axis_index("item")
    rows = wide_s.shape[1]
    copies = []
    for slot, (item_mask, seq_mask) in enumerate(masks):
        wide_s[slot] = block_ref[slot].astype(f32)
        owner_item, owner_seq = item ^ item_mask, seq ^ seq_mask
        first = owner_seq * 4 + (owner_item & 1) * 2 + (owner_item >> 1)
        target = pl.ds(pl.multiple_of(first * rows, 8), rows)
        at = 0
        for index, out in enumerate(outs):
            size = out.shape[1]
            copy = pltpu.make_async_copy(
                wide_s.at[slot, :, pl.ds(at, size)], out.at[target, :], sems.at[slot, index]
            )
            copy.start()
            copies.append(copy)
            at += size
    for copy in copies:
        copy.wait()


def spread(chain, names, sibling, blocks, outs):
    masks = [
        (2 * ("x" in name) + sibling, ("y" in name) + 2 * ("a" in name) + 4 * ("b" in name))
        for name in names
    ]
    number = len(names)
    return chain.launch(
        functools.partial(spread_kernel, masks),
        (blocks, *outs),
        [shape(out.shape, f32) for out in outs],
        16,
        "spread",
        2.3,
        far_in=range(1, 5),
        far_out=range(4),
        scratch=[
            pltpu.VMEM(blocks.shape, f32),
            pltpu.SemaphoreType.DMA((number, 4)),
        ],
        aliases={1 + i: i for i in range(4)},
    )


def blank_kernel(*refs):
    pass


def gather_blocks(chain, keep, got, groups):
    block = plain_sum(chain, keep, got)[None]
    held = {"": (block, 0)}
    for level, sends in enumerate(ROUTES + ((),)):
        swap = SWAPS.get(level)
        if level == 0:
            arrays = [block] * len(sends)
        else:
            wanted = [names for _, names in sends] + ([swap] if swap else [])
            arrays = glue(chain, held, wanted, AWAITED.get(level, ()), 50 if level == 1 else 2)
        for (along, names), array in zip(sends, arrays):
            moved = swap_bit(array, *BIT_OF[along])
            for row, name in enumerate(names):
                held["".join(sorted(name + along))] = (moved, row)
        if swap:
            groups.append((swap, arrays[-1], swap_bit(arrays[-1], "item", 0)))
        yield


def spread_blocks(chain, rows, widths, groups):
    outs = [shape((32 * rows, width), f32) for width in widths]
    outs = chain.launch(blank_kernel, (), outs, 4, "blanks", far_out=range(4))
    while True:
        at, sibling = yield outs
        outs = spread(chain, groups[at][0], sibling, groups[at][1 + sibling], outs)


def last_kernel(
    slab, mine_ref, other_ref, resid_ref, lat_ref, gain_ref, wq_ref,
    value_ref, key_ref, query_ref, latent_ref, gain_kv_ref, gain_q_ref, gain_mlp_ref, resid_s,
):
    byte_width = value_ref.shape[0]
    latents, width = lat_ref.shape
    upper = place_bit("item", 0) != 0
    half = mine_ref.shape[0]
    rest = byte_width - half
    value_ref[pl.ds(0, half), :] = jnp.where(upper, other_ref[...], mine_ref[...]).astype(f32)
    second = jnp.where(upper, mine_ref[...], other_ref[...])
    value_ref[pl.ds(half, rest), :] = second[:rest].astype(f32)
    lower = second[rest:].astype(f32)
    for at in range(0, byte_width, QK):
        key_ref[pl.ds(at, QK), :] = lower[:, at : at + QK]
    query_t = (lower[:, byte_width : byte_width + latents] * SCALE).astype(bf16)
    gains = lower[:, byte_width + latents :]
    row = 0
    for ref in (gain_kv_ref, gain_mlp_ref):
        count = ref.shape[0] // QK
        ref[...] = jnp.concatenate([gains[row + i : row + i + 1] for i in range(count)], axis=1).reshape(-1)
        row += count
    hat, inverse = normalize(lat_ref[...].astype(f32))
    gain = row_of(gain_ref)
    lat_low = (hat * gain).astype(bf16)
    query_ref[...] = dot_nt(lat_low.T, query_t)
    grad_lat = dot_nt(query_t.T, wq_ref[...])
    gain_q_ref[...] = jnp.sum(grad_lat * hat, axis=0)
    parts = width // latents
    for rank in range(latents // slab):
        for part in range(parts):
            resid_s[pl.ds(rank * slab, slab), pl.ds(part * latents, latents)] = resid_ref[
                pl.ds((rank * parts + part) * slab, slab), :
            ]
    latent_ref[...] = resid_s[...] + norm_back(grad_lat * gain, hat, inverse)


def last_step(chain, n_seq, sums, resid, latent_init, gain_q, w_query):
    latents, width = latent_init.shape
    byte_width = 2 * sums[0].shape[0] - QK
    dims = [(byte_width, V), (byte_width, QK), (width, QK), (latents, width)]
    dims += [(byte_width,), (width,), (width,)]
    return chain.launch(
        functools.partial(last_kernel, latents // n_seq),
        (*sums, resid, latent_init, gain_q, w_query),
        [shape(dim, f32) for dim in dims],
        16,
        "last_step",
        4.8,
        scratch=[pltpu.VMEM((latents, width), f32)],
    )


ORDER = "abcad0ba1cbad2cbad3cbdAcdBCD"

TAIL = "pmpAoppmpapmBpmpmbCpc"


def per_device(
    byte_in,
    lengths,
    latent_init,
    gain_kv,
    gain_q,
    gain_mlp,
    w_query,
    w_key,
    w_value,
    w_out,
    w_up,
    w_down,
    d_out,
):
    items, slot, byte_width = byte_in.shape
    latents, width = latent_init.shape
    n_item, n_seq = lax.axis_size("item"), lax.axis_size("seq")
    item_bits, seq_bits = bits_of("item"), bits_of("seq")
    chain = Chain(byte_in)
    keys, values, acts, halves = [None] * items, [None] * items, [None] * items, [None] * items
    gas, stats = [None] * items, [None] * items
    q_t, limits = None, None
    carried = None
    made, grads = [None] * items, [None] * items

    def travel(item):
        nonlocal q_t, limits
        operands = (byte_in, gain_kv, w_key, w_value)
        if item == 0:
            limits, q_t, *made = attend_first(
                chain, lengths, *operands, latent_init, gain_q, w_query
            )
        else:
            made = attend(chain, item, limits, *operands, q_t)
        keys[item], values[item], keep, send = made
        got = swap_bit(send, "seq", 0)
        yield
        mine = merge(chain, 0, keep, got)
        if n_seq == 8:
            inward = lax.ppermute(mine, "seq", [(0, 2), (1, 3), (6, 4), (7, 5)])
            yield
            mine = merge(chain, 2, mine, inward)
            across = lax.ppermute(mine, "seq", [(2, 4), (3, 5), (4, 2), (5, 3)])
            yield
            mine = merge(chain, 2, mine, across)
            outward = lax.ppermute(mine, "seq", [(2, 0), (3, 1), (4, 6), (5, 7)])
            yield
            mine = choose(chain, mine, outward)
        else:
            for axis, bit in seq_bits[1:]:
                got = swap_bit(mine, axis, bit)
                yield
                mine = merge(chain, bit, mine, got)
        yield mine, swap_bit(mine, "seq", 0)

    ways = [travel(item) for item in range(items)]
    for letter in ORDER:
        if letter.isdigit():
            acts[int(letter)] = cotangent(chain, int(letter), d_out, w_down)
            continue
        item = "abcd".index(letter.lower())
        if letter.islower():
            halves[item] = next(ways[item])
            continue
        for halves_item in ways[item]:
            halves[item] = halves_item
        made[item], gas[item], stats[item], mlp, *factors = latent_step(
            chain,
            item,
            width // n_seq,
            *halves[item],
            latent_init,
            gain_mlp,
            d_out,
            acts[item],
            (w_out, w_up, w_down),
            carried,
        )
        carried = (mlp, *factors[:3])
    sums = factors[3:]

    begun = None

    def go_back(item):
        nonlocal begun
        args = (limits, byte_in, gain_kv, w_key, w_value, q_t, keys[item], values[item], gas[item], stats[item])
        grads[item], total, gains, *halves = bytes_step(chain, item, *args, mlp, 1.0 / n_seq, begun)
        begun = (total, gains)
        return halves

    keep, send = sums
    got = swap_bit(send, *item_bits[0])
    go_back(0)
    for step, following in zip(item_bits, item_bits[1:]):
        keep, send = split_sum(chain, following, keep, got)
        got = swap_bit(send, *following)
    go_back(1)
    go_back(2)
    widths = (width, width, width, latents)
    direct = (n_item, n_seq) == (4, 8)
    if direct:
        groups = []
        latent_way = gather_blocks(chain, keep, got, groups)
        next(latent_way)
        spread_way = spread_blocks(chain, keep.shape[0], widths, groups)
        next(spread_way)
    else:
        latent_piece = plain_sum(chain, keep, got)
        latent_all = lax.all_gather(latent_piece, ("item", "seq"), axis=0, tiled=False)
    keep, send = go_back(3)
    byte_way = whole_sum(chain, keep, send, item_bits, seq_bits)
    if direct:
        for letter in TAIL:
            if letter == "o":
                latents_out, byte_grad = store(chain, made, grads)
            elif letter == "m":
                next(latent_way)
            elif letter == "p":
                byte_halves = next(byte_way)
            else:
                group = "abc".index(letter.lower()), int(letter.islower())
                whole_grads = spread_way.send(group)
    else:
        count = len(item_bits)
        blocks = latent_all.reshape((2,) * count + (n_seq,) + latent_piece.shape)
        turn = [count] + list(range(count))[::-1] + [count + 1, count + 2]
        blocks = blocks.transpose(turn).reshape(-1, sum(widths)).astype(f32)
        whole_grads = [blocks[:, i * width : i * width + size] for i, size in enumerate(widths)]
        for byte_halves in byte_way:
            pass
        latents_out, byte_grad = store(chain, made, grads)
    out_grad, up_grad, down_grad, resid = whole_grads
    value_grad, key_grad, query_grad, latent_grad, gain_kv_grad, gain_q_grad, gain_mlp_grad = last_step(
        chain, n_seq, byte_halves, resid, latent_init, gain_q, w_query
    )
    return (
        latents_out,
        byte_grad,
        latent_grad,
        gain_kv_grad,
        gain_q_grad,
        gain_mlp_grad,
        query_grad,
        key_grad,
        value_grad,
        out_grad,
        up_grad,
        down_grad,
    )


def solution(mesh):
    placed = (P("item", "seq", None), P("item")) + (P(),) * 10 + (P("item", None, None),)
    return jax.shard_map(
        per_device,
        mesh=mesh,
        in_specs=placed,
        out_specs=(P("item", None, None), P("item", "seq", None)) + (P(),) * 10,
        check_vma=False,
    )
```

```python
import functools

import jax
import jax.numpy as jnp
from jax import lax
from jax.experimental import pallas as pl
from jax.experimental.pallas import tpu as pltpu
from jax.sharding import PartitionSpec as P

HEADS = 8
QK = 256
V = 1280
QK_HEAD = QK // HEADS
V_HEAD = V // HEADS
SCALE = QK_HEAD**-0.5
ROWS = V + 2 * HEADS
EPS = 1e-05
NEG = -1e30
MIB = 1 << 20
f32 = jnp.float32
bf16 = jnp.bfloat16

IN_VMEM = pl.BlockSpec(memory_space=pltpu.VMEM)
IN_SMEM = pl.BlockSpec(memory_space=pltpu.SMEM)
FAR = pl.BlockSpec(memory_space=pltpu.HBM)


def dot(a, b):
    return jnp.dot(a, b, preferred_element_type=f32)


def dot_nt(a, b):
    return lax.dot_general(a, b, (((1,), (1,)), ((), ())), preferred_element_type=f32)


def shape(dims, dtype):
    return jax.ShapeDtypeStruct(dims, dtype)


def cost(microseconds):
    return pl.CostEstimate(
        flops=int(microseconds * 5e8), bytes_accessed=int(microseconds * 1.5e6), transcendentals=0
    )


class Chain:
    def __init__(self, token):
        self.token = token

    def launch(
        self, kernel, inputs, outs, mib, name, time=0.7, far_in=(), far_out=(), scratch=(), aliases=None, scalars=()
    ):
        count, made = len(inputs), len(outs)

        def body(*refs):
            refs[count + 1 + made][...] = jnp.zeros((8, 128), f32)
            kernel(*refs[:count], *refs[count + 1 : count + 1 + made], *refs[count + 2 + made :])

        where = {i: FAR for i in far_in} | {i: IN_SMEM for i in scalars}
        *results, self.token = pl.pallas_call(
            body,
            out_shape=[*outs, shape((8, 128), f32)],
            in_specs=[where.get(i, IN_VMEM) for i in range(count)] + [FAR],
            out_specs=[FAR if i in far_out else IN_VMEM for i in range(made)] + [IN_VMEM],
            scratch_shapes=scratch,
            input_output_aliases=aliases or {},
            compiler_params=pltpu.CompilerParams(vmem_limit_bytes=mib * MIB),
            cost_estimate=cost(time),
            name=name,
        )(*inputs, self.token)
        return results


def row_of(ref):
    return ref[...].reshape(1, -1)


def place_bit(axis, bit):
    return (lax.axis_index(axis) >> bit) & 1


def normalize(vector, axis=-1):
    average = jnp.mean(vector, axis=axis, keepdims=True)
    centered = vector - average
    inverse = lax.rsqrt(jnp.mean(centered * centered, axis=axis, keepdims=True) + EPS)
    return (centered * inverse, inverse)


def norm_back(grad_hat, hat, inverse, axis=-1):
    return inverse * (
        grad_hat
        - jnp.mean(grad_hat, axis=axis, keepdims=True)
        - hat * jnp.mean(grad_hat * hat, axis=axis, keepdims=True)
    )


def query_kernel(lat_ref, gain_ref, wq_ref, q_ref):
    hat, _ = normalize(lat_ref[...].astype(f32))
    lat_low = (hat * row_of(gain_ref)).astype(bf16)
    q_ref[...] = dot(lat_low, wq_ref[...]).T.astype(bf16)


def spread_queries(q_t):
    channel = lax.broadcasted_iota(jnp.int32, q_t.shape, 0) // QK_HEAD
    zeros = jnp.zeros_like(q_t)
    return jnp.concatenate([jnp.where(channel == head, q_t, zeros) for head in range(HEADS)], axis=1)


def attend_kernel(
    at, item, limits_ref, x_ref, gain_ref, wk_ref, wv_ref, q_ref, k_ref, v_ref, keep_ref, send_ref
):
    low = place_bit("seq", 0)
    hat, _ = normalize(x_ref[at].astype(f32))
    byte_low = (hat * row_of(gain_ref)).astype(bf16)
    keys = dot(byte_low, wk_ref[...]).astype(bf16)
    values = dot(byte_low, wv_ref[...])
    k_ref[...] = keys
    v_ref[...] = values.astype(bf16)
    values_t = values.T.astype(bf16)
    q_t = q_ref[...]
    latents = q_t.shape[1]
    half = latents // 2
    inside = lax.broadcasted_iota(jnp.int32, (keys.shape[0], latents), 0) < limits_ref[pl.ds(item, 1), :]

    def put(first, block):
        left, right = block[:, :half], block[:, half:]
        rows = pl.ds(first, block.shape[0])
        keep_ref[rows, :] = jnp.where(low == 0, left, right).astype(bf16)
        send_ref[rows, :] = jnp.where(low == 0, right, left).astype(bf16)

    every = dot(keys, spread_queries(q_t)) * SCALE
    totals, weights, inverses = [], [], []
    for head in range(HEADS):
        scores = every[:, head * latents : (head + 1) * latents]
        scores = jnp.where(inside, scores, NEG)
        top = jnp.max(scores, axis=0, keepdims=True)
        powers = jnp.exp(scores - top)
        total = jnp.sum(powers, axis=0, keepdims=True)
        weights.append(powers.astype(bf16))
        inverses.append(1.0 / total)
        totals.append(top + jnp.log(total))
    for head in range(HEADS):
        rows = slice(head * V_HEAD, (head + 1) * V_HEAD)
        put(head * V_HEAD, dot(values_t[rows], weights[head]) * inverses[head])
    lse = jnp.concatenate(totals, axis=0)
    high = lse.astype(bf16).astype(f32)
    put(V, jnp.concatenate([high, lse - high], axis=0))


def first_kernel(
    lengths_ref, lat_ref, gain_q_ref, wq_ref, x_ref, gain_ref, wk_ref, wv_ref,
    limits_ref, q_ref, k_ref, v_ref, keep_ref, send_ref, x_s, wk_s, wv_s, sems, lat_s, wq_s,
):
    rows = wv_ref.shape[0] // 4
    pairs = [(lat_ref, lat_s), (wq_ref, wq_s), (x_ref.at[pl.ds(0, 1)], x_s), (wk_ref, wk_s)]
    pairs += [(wv_ref.at[pl.ds(i * rows, rows)], wv_s.at[pl.ds(i * rows, rows)]) for i in range(4)]
    copies = [pltpu.make_async_copy(src, dst, sems.at[i]) for i, (src, dst) in enumerate(pairs)]
    for copy in copies:
        copy.start()
    before = lax.axis_index("seq") * x_ref.shape[1]
    for item in range(x_ref.shape[0]):
        limits_ref[pl.ds(item, 1), :] = jnp.full((1, limits_ref.shape[1]), lengths_ref[item] - before, jnp.int32)
    for copy in copies[:2]:
        copy.wait()
    query_kernel(lat_s, gain_q_ref, wq_s, q_ref)
    for copy in copies[2:]:
        copy.wait()
    attend_kernel(0, 0, limits_ref, x_s, gain_ref, wk_s, wv_s, q_ref, k_ref, v_ref, keep_ref, send_ref)


def attend_outs(byte_in, latents):
    slot = byte_in.shape[1]
    payload = shape((ROWS, latents // 2), bf16)
    return [shape((slot, QK), bf16), shape((slot, V), bf16), payload, payload]


def attend(chain, item, limits, byte_in, gain_kv, w_key, w_value, q_t):
    return chain.launch(
        functools.partial(attend_kernel, item, item),
        (limits, byte_in, gain_kv, w_key, w_value, q_t),
        attend_outs(byte_in, q_t.shape[1]),
        18,
        "attend",
        3.9,
    )


def attend_first(chain, lengths, byte_in, gain_kv, w_key, w_value, latent_init, gain_q, w_query):
    latents = latent_init.shape[0]
    one = (1,) + byte_in.shape[1:]
    shapes = [one, w_key.shape, w_value.shape]
    return chain.launch(
        first_kernel,
        (lengths, latent_init, gain_q, w_query, byte_in, gain_kv, w_key, w_value),
        [shape((byte_in.shape[0], latents), jnp.int32), shape((QK, latents), bf16)]
        + attend_outs(byte_in, latents),
        60,
        "attend_first",
        6,
        far_in=(1, 3, 4, 6, 7),
        scalars=(0,),
        scratch=[pltpu.VMEM(dims, bf16) for dims in shapes]
        + [pltpu.SemaphoreType.DMA((8,))]
        + [pltpu.VMEM(dims, bf16) for dims in (latent_init.shape, w_query.shape)],
    )


def merge_kernel(bit, mine_ref, other_ref, out_ref):
    swap = place_bit("seq", bit) != 0

    def totals(ref):
        return ref[V : V + HEADS, :].astype(f32) + ref[V + HEADS :, :].astype(f32)

    def ordered(mine, other):
        return jnp.where(swap, other, mine), jnp.where(swap, mine, other)

    lse_a, lse_b = ordered(totals(mine_ref), totals(other_ref))
    top = jnp.maximum(lse_a, lse_b)
    weight_a = jnp.exp(lse_a - top)
    weight_b = jnp.exp(lse_b - top)
    total = weight_a + weight_b
    lse = top + jnp.log(total)
    weight_a = weight_a / total
    weight_b = weight_b / total
    for head in range(HEADS):
        rows = pl.ds(head * V_HEAD, V_HEAD)
        sums_a, sums_b = ordered(mine_ref[rows, :].astype(f32), other_ref[rows, :].astype(f32))
        out_ref[rows, :] = (
            sums_a * weight_a[head : head + 1] + sums_b * weight_b[head : head + 1]
        ).astype(bf16)
    high = lse.astype(bf16).astype(f32)
    out_ref[pl.ds(V, 2 * HEADS), :] = jnp.concatenate([high, lse - high], axis=0).astype(bf16)


def merge(chain, bit, mine, other):
    kernel = functools.partial(merge_kernel, bit)
    return chain.launch(kernel, (mine, other), [shape(mine.shape, bf16)], 8, "merge")[0]


def choose_kernel(mine_ref, other_ref, out_ref):
    line = lax.axis_index("seq") >> 1
    inner = (line == 1) | (line == 2)
    out_ref[...] = jnp.where(inner, mine_ref[...], other_ref[...])


def choose(chain, mine, other):
    return chain.launch(choose_kernel, (mine, other), [shape(mine.shape, bf16)], 8, "choose")[0]


def cotangent_kernel(item, g_ref, w_ref, act_ref):
    def one(at, carry):
        rows = pl.ds(pl.multiple_of(at * TILE, TILE), TILE)
        act_ref[:, rows] = dot_nt(g_ref[item], w_ref[rows, :])
        return carry

    lax.fori_loop(0, w_ref.shape[0] // TILE, one, 0)


def cotangent(chain, item, d_out, w_down):
    outs = [shape((d_out.shape[1], w_down.shape[0]), f32)]
    kernel = functools.partial(cotangent_kernel, item)
    return chain.launch(kernel, (d_out, w_down), outs, 12, "cotangent",
        1.6)[0]


TILE = 256
ROOT_HALF = 0.7071067811865476
ROOT_TWO_PI = 0.3989422804014327


def latent_kernel(
    item, last, mine_ref, other_ref, lat_ref, gain_ref, g_ref, act_ref, w_out, w_up, w_down, *refs
):
    first = item == 0
    if not first:
        mlp_in, _, _, _, *refs = refs
    out_ref, ga_ref, stat_ref, mlp_ref, part_ref, branch_ref, gup_ref, *refs = refs
    if last:
        keep_ref, send_ref, *refs = refs
    att_s, turn_s = refs
    low, core = place_bit("seq", 0), place_bit("item", 0)
    rank = lax.axis_index("seq")
    latents, width = lat_ref.shape
    ff = act_ref.shape[1]
    share = part_ref.shape[1]
    g = g_ref[item]
    own = pl.ds(item * latents, latents)
    mine, other = mine_ref[...], other_ref[...]
    left = jnp.where(low == 0, mine, other)
    right = jnp.where(low == 0, other, mine)
    whole = jnp.concatenate([left, right], axis=1)
    att_s[...] = whole[:V]
    stat_ref[:HEADS, :] = whole[V : V + HEADS].astype(f32) + whole[V + HEADS :].astype(f32)
    attended = whole[:V].T
    rows = pl.ds(pl.multiple_of(rank * share, 16), share)

    part_ref[0, :, own] = att_s[rows, :]
    mixed = lat_ref[...].astype(f32) + jnp.concatenate(
        [dot(attended, w_out[:, pl.ds(at, TILE)]) for at in range(0, width, TILE)], axis=1
    )
    hat, inverse = normalize(mixed)
    gain = row_of(gain_ref)
    hidden = (hat * gain).astype(bf16)
    activated, grad_up = [], []
    for at in range(0, ff, TILE):
        upward = dot(hidden, w_up[:, pl.ds(at, TILE)])
        bell = 0.5 + 0.5 * lax.erf(upward * ROOT_HALF)
        slope = bell + upward * (ROOT_TWO_PI * jnp.exp(-0.5 * upward * upward))
        activated.append((upward * bell).astype(bf16))
        grad_up.append((act_ref[:, pl.ds(at, TILE)] * slope).astype(bf16))
    activated = jnp.concatenate(activated, axis=1)
    grad_up = jnp.concatenate(grad_up, axis=1)
    for at in range(0, width, TILE):
        block = mixed[:, at : at + TILE] + dot(activated, w_down[:, pl.ds(at, TILE)])
        out_ref[:, pl.ds(at, TILE)] = block.astype(bf16)
    turn_s[...] = activated.T
    part_ref[2, :, own] = turn_s[rows, :]
    grad_hidden = jnp.concatenate(
        [dot_nt(grad_up, w_up[pl.ds(at, TILE), :]) for at in range(0, width, TILE)], axis=1
    )
    turn_s[...] = hidden.T
    part_ref[1, :, own] = turn_s[rows, :]
    gup_ref[own, :] = grad_up
    mlp = jnp.sum(grad_hidden * hat, axis=0, keepdims=True)
    mlp_ref[...] = mlp if first else mlp + mlp_in[...]
    grad_mixed = g.astype(f32) + norm_back(grad_hidden * gain, hat, inverse)
    branch = grad_mixed.astype(bf16)
    branch_ref[own, :] = branch
    for at in range(0, V, TILE):
        ga_ref[pl.ds(at, TILE), :] = dot_nt(w_out[pl.ds(at, TILE), :], branch).astype(bf16)
    for head in range(HEADS):
        part = pl.ds(head * V_HEAD, V_HEAD)
        stat_ref[pl.ds(HEADS + head, 1), :] = jnp.sum(
            ga_ref[part, :].astype(f32) * att_s[part, :].astype(f32), axis=0, keepdims=True
        )
    if last:
        slab = latents * share // width
        few = [pl.ds(pl.multiple_of(i * latents + rank * slab, 16), slab) for i in range(item + 1)]
        resid = sum(branch_ref[one, :].astype(f32) for one in few)
        parts = (
            dot(part_ref[0], branch_ref[...]),
            dot(part_ref[1], gup_ref[...]),
            dot(part_ref[2], g_ref[...].reshape(branch_ref.shape)),
            jnp.concatenate([resid[:, at : at + latents] for at in range(0, width, latents)], axis=0),
        )
        half = share // 2
        at = 0
        for part in parts:
            lanes = pl.ds(at, part.shape[1])
            lower, upper = part[:half], part[half:]
            keep_ref[:, lanes] = jnp.where(core == 0, lower, upper).astype(bf16)
            send_ref[:, lanes] = jnp.where(core == 0, upper, lower).astype(bf16)
            at += part.shape[1]


def latent_step(chain, item, share, mine, other, lat, gain, g, act, weights, carried):
    items, latents, width = g.shape
    ff = act.shape[1]
    total = 2 * width + ff + latents
    last = item == items - 1
    inputs = [mine, other, lat, gain, g, act, *weights]
    aliases = {}
    if carried:
        inputs += carried
        aliases = {10: 4, 11: 5, 12: 6}
    outs = [
        shape((latents, width), bf16),
        shape((V, latents), bf16),
        shape((2 * HEADS, latents), f32),
        shape((1, width), f32),
        shape((3, share, items * latents), bf16),
        shape((items * latents, width), bf16),
        shape((items * latents, ff), bf16),
    ]
    if last:
        outs += [shape((share // 2, total), bf16)] * 2
    return chain.launch(
        functools.partial(latent_kernel, item, last),
        inputs,
        outs,
        20,
        "latent_step",
        8.4,
        scratch=[pltpu.VMEM((V, latents), bf16), pltpu.VMEM((width, latents), bf16)],
        aliases=aliases,
    )


def bytes_kernel(
    item, last, mlp_scale, limits_ref, x_ref, gain_ref, wk_ref, wv_ref, q_ref, k_ref, v_ref, ga_ref, stat_ref, *refs
):
    first = item == 0
    if last:
        mlp_ref, *refs = refs
    if not first:
        sum_in, gain_in, *refs = refs
    grad_ref, sum_ref, gain_out, *refs = refs
    if last:
        keep_ref, send_ref = refs
    core = place_bit("item", 0)
    slot, width = x_ref.shape[1:]

    def add(rows, lanes, part):
        at = (pl.ds(*rows), pl.ds(*lanes))
        sum_ref[at] = part if first else part + sum_in[at]

    hat, inverse = normalize(x_ref[item].astype(f32))
    gain = row_of(gain_ref)
    low_t = (hat * gain).T.astype(bf16)
    keys = k_ref[...]
    values = v_ref[...]
    keys_t = keys.T
    q_t = q_ref[...]
    latents = q_t.shape[1]
    inside = lax.broadcasted_iota(jnp.int32, (slot, latents), 0) < limits_ref[pl.ds(item, 1), :]

    every = dot(keys, spread_queries(q_t)) * SCALE
    grad_values, grad_keys = [], []
    softs, moves = [], []
    for head in range(HEADS):
        scores = every[:, head * latents : (head + 1) * latents]
        scores = jnp.where(inside, scores, NEG)
        soft = jnp.exp(scores - stat_ref[pl.ds(head, 1), :])
        part = slice(head * V_HEAD, (head + 1) * V_HEAD)
        grad_soft = dot(values[:, part], ga_ref[pl.ds(head * V_HEAD, V_HEAD), :])
        moves.append((soft * (grad_soft - stat_ref[pl.ds(HEADS + head, 1), :])).astype(bf16))
        softs.append(soft.astype(bf16))
    for head in range(HEADS):
        grad_attn = ga_ref[pl.ds(head * V_HEAD, V_HEAD), :]
        grad_values.append(dot_nt(grad_attn, softs[head]).astype(bf16))
    for head in range(HEADS):
        small = slice(head * QK_HEAD, (head + 1) * QK_HEAD)
        grad_keys.append((dot_nt(q_t[small], moves[head]) * SCALE).astype(bf16))
        add((width + head * QK_HEAD, QK_HEAD), (width, latents), dot(keys_t[small], moves[head]))
    grad_values = jnp.concatenate(grad_values, axis=0)
    grad_keys = jnp.concatenate(grad_keys, axis=0)
    grad_low = dot_nt(grad_values.T, wv_ref[...]) + dot_nt(grad_keys.T, wk_ref[...])
    gain_part = jnp.sum(grad_low * hat, axis=0, keepdims=True)
    gain_out[...] = gain_part if first else gain_part + gain_in[...]
    grad_ref[...] = norm_back(grad_low * gain, hat, inverse)
    for rows in range(0, width, TILE):
        block = low_t[rows : rows + TILE]
        add((rows, TILE), (0, V), dot_nt(block, grad_values))
        add((width, QK), (rows, TILE), dot_nt(block, grad_keys))

    if last:
        at = width
        for part in (gain_out[...], mlp_ref[...] * mlp_scale):
            for begin in range(0, part.shape[1], QK):
                sum_ref[pl.ds(at, 1), pl.ds(width + latents, QK)] = part[:, begin : begin + QK]
                at += 1
        half = sum_ref.shape[0] // 2
        kept = pl.ds(pl.multiple_of(core * half, 16), half)
        sent = pl.ds(pl.multiple_of((1 - core) * half, 16), half)
        keep_ref[...] = sum_ref[kept, :].astype(bf16)
        send_ref[...] = sum_ref[sent, :].astype(bf16)
    elif first:
        sum_ref[pl.ds(width, QK), pl.ds(width + latents, QK)] = jnp.zeros((QK, QK), f32)


def bytes_step(chain, item, limits, byte_in, gain_kv, w_key, w_value, q_t, keys, values, ga, stats, mlp, mlp_scale, begun):
    items, slot, width = byte_in.shape
    rows = width + QK
    last = item == items - 1
    inputs = [limits, byte_in, gain_kv, w_key, w_value, q_t, keys, values, ga, stats]
    if last:
        inputs += [mlp]
    aliases = {}
    if begun:
        count = len(inputs)
        inputs += begun
        aliases = {count: 1, count + 1: 2}
    outs = [shape((slot, width), f32), shape((rows, V), f32), shape((1, width), f32)]
    if last:
        outs += [shape((rows // 2, V), bf16)] * 2
    return chain.launch(
        functools.partial(bytes_kernel, item, last, mlp_scale),
        inputs,
        outs,
        24,
        "bytes_step",
        6.0,
        aliases=aliases,
    )


def store_kernel(*refs):
    count = (len(refs) - 3) // 2
    sources, outs, (sems,) = refs[: 2 * count], refs[2 * count : -1], refs[-1:]
    copies = [
        pltpu.make_async_copy(source, outs[at // count].at[at % count], sems.at[at])
        for at, source in enumerate(sources)
    ]
    for copy in copies:
        copy.start()
    for copy in copies:
        copy.wait()


def store(chain, made, grads):
    outs = [shape((len(arrays),) + arrays[0].shape, arrays[0].dtype) for arrays in (made, grads)]
    return chain.launch(
        store_kernel,
        (*made, *grads),
        outs,
        4,
        "store",
        2,
        far_out=(0, 1),
        scratch=[pltpu.SemaphoreType.DMA((len(made) + len(grads),))],
    )


def swap_bit(array, axis, bit):
    size = lax.axis_size(axis)
    return lax.ppermute(array, axis, [(i, i ^ (1 << bit)) for i in range(size)])


def bit_of(axis, bit):
    return (lax.axis_index(axis) >> bit) & 1


def bits_of(axis):
    return [(axis, bit) for bit in range(lax.axis_size(axis).bit_length() - 1)]


def split_kernel(step, keep_ref, got_ref, kept_ref, sent_ref):
    half = kept_ref.shape[0]
    upper = place_bit(*step) != 0
    total = (keep_ref[...].astype(f32) + got_ref[...].astype(f32)).astype(bf16)
    kept_ref[...] = jnp.where(upper, total[half:], total[:half])
    sent_ref[...] = jnp.where(upper, total[:half], total[half:])


def split_sum(chain, step, keep, got):
    rows, width = keep.shape
    half = rows // 2
    if half % 8 == 0:
        kernel = functools.partial(split_kernel, step)
        outs = [shape((half, width), bf16)] * 2
        return chain.launch(kernel, (keep, got), outs, 8, "split_sum")
    total = (keep.astype(f32) + got.astype(f32)).astype(bf16)
    take = lambda side: lax.dynamic_slice_in_dim(total, side * half, half, 0)
    bit = bit_of(*step)
    return take(bit), take(1 - bit)


def sum_kernel(keep_ref, got_ref, out_ref):
    out_ref[...] = (keep_ref[...].astype(f32) + got_ref[...].astype(f32)).astype(bf16)


def plain_sum(chain, keep, got):
    return chain.launch(sum_kernel, (keep, got), [shape(keep.shape, bf16)], 8, "plain_sum")[0]


def halves_kernel(steps, cut, *refs):
    count = len(steps)
    keeps, gots, outs = refs[:count], refs[count : 2 * count], refs[2 * count :]
    stacked = len(outs) == 2
    for at, (step, keep_ref, got_ref) in enumerate(zip(steps, keeps, gots)):
        upper = place_bit(*step) != 0
        rows = keep_ref.shape[0] // cut
        part = pl.ds(at * rows if cut > 1 else 0, rows)
        total = (keep_ref[part, :].astype(f32) + got_ref[part, :].astype(f32)).astype(bf16)
        half = rows // 2
        kept_ref, sent_ref = outs if stacked else (outs[at], outs[count + at])
        part = pl.ds(at * half if stacked else 0, half)
        kept_ref[part, :] = jnp.where(upper, total[half:], total[:half])
        sent_ref[part, :] = jnp.where(upper, total[:half], total[half:])


def sum_halves(chain, steps, keeps, gots, cut=1, stacked=False):
    count = len(steps)
    rows, width = keeps[0].shape[0] // cut, keeps[0].shape[1]
    kernel = functools.partial(halves_kernel, steps, cut)
    if stacked:
        outs = [shape((rows // 2 * count, width), bf16)] * 2
        return chain.launch(kernel, (*keeps, *gots), outs, 12, "sum_halves")
    outs = [shape((rows // 2, width), bf16)] * (2 * count)
    results = chain.launch(kernel, (*keeps, *gots), outs, 12, "sum_halves")
    return results[:count], results[count:]


def join_kernel(steps, split, stacked, *refs):
    count = len(steps)
    arrays = 1 if split else count
    mines, others, outs = refs[:arrays], refs[arrays : 2 * arrays], refs[2 * arrays :]
    for at, step in enumerate(steps):
        upper = place_bit(*step) != 0
        mine_ref, other_ref = (mines[0], others[0]) if split else (mines[at], others[at])
        half = mine_ref.shape[0] // (count if split else 1)
        part = pl.ds(at * half if split else 0, half)
        mine, other = mine_ref[part, :], other_ref[part, :]
        out_ref = outs[0] if stacked else outs[at]
        first = 2 * half * at if stacked else 0
        out_ref[pl.ds(first, half), :] = jnp.where(upper, other, mine)
        out_ref[pl.ds(first + half, half), :] = jnp.where(upper, mine, other)


def join(chain, steps, mines, others, stacked=False):
    count = len(steps)
    rows, width = mines[0].shape
    split = len(mines) == 1
    if split:
        rows //= count
    sizes = [(2 * rows * count, width)] if stacked else [(2 * rows, width)] * count
    kernel = functools.partial(join_kernel, steps, split, stacked)
    outs = [shape(size, bf16) for size in sizes]
    return chain.launch(kernel, (*mines, *others), outs, 12, "join")


def whole_sum(chain, keep, send, item_bits, seq_bits):
    got = swap_bit(send, *item_bits[0])
    orders = (item_bits[1:] + seq_bits, seq_bits[:1] + item_bits[1:] + seq_bits[1:])
    steps = list(zip(*orders))
    common = next(i for i, step in enumerate(steps) if step[0] == step[1])
    yield
    keeps, sends = sum_halves(chain, steps[0], [keep] * 2, [got] * 2, 2, common == 0)
    for at in range(common):
        gots = [swap_bit(send, *one) for send, one in zip(sends, steps[at])]
        yield
        keeps, sends = sum_halves(chain, steps[at + 1], keeps, gots, 1, at + 1 == common)
    keep, send = keeps, sends
    shared = [step[0] for step in steps[common:]]
    for step, following in zip(shared, shared[1:-1]):
        got = swap_bit(send, *step)
        yield
        rows = keep.shape[0] // 2
        keep, send = sum_halves(chain, (following,) * 2, [keep] * 2, [got] * 2, 2, True)
    got = swap_bit(send, *shared[-2])
    yield
    total = plain_sum(chain, keep, got)
    got = swap_bit(total, *shared[-1])
    yield
    total = plain_sum(chain, total, got)
    totals = [total]
    for at in range(len(shared) - 2, -1, -1):
        got = swap_bit(totals[0], *shared[at])
        yield
        totals = join(chain, (shared[at],) * 2, totals, [got], at > 0)
    for step in steps[common - 1 :: -1]:
        gots = [swap_bit(total, *one) for total, one in zip(totals, step)]
        yield
        totals = join(chain, step, totals, gots, step == steps[0])
    other = swap_bit(totals[0], *item_bits[0])
    yield totals[0], other


ROUTES = (
    (("b", ("",)), ("a", ("",)), ("x", ("",)), ("y", ("",))),
    (("a", ("x", "b")),),
    (("x", ("y", "b")), ("y", ("a", "b"))),
    (("y", ("bx", "ab")), ("x", ("ab",)), ("a", ("xy",))),
    (("a", ("bxy",)),),
)
SWAPS = {
    1: ("", "x", "y", "a", "b"),
    3: ("ax", "ab", "xy", "bx", "ay", "by"),
    5: ("bxy", "aby", "abx", "axy", "abxy"),
}
AWAITED = {2: ("ab",), 4: ("aby", "abx", "axy")}
BIT_OF = {"x": ("item", 1), "y": ("seq", 0), "a": ("seq", 1), "b": ("seq", 2)}


def glue_kernel(picks, count, *refs):
    sources, outs, (sems,) = refs[:count], refs[count:-1], refs[-1:]
    copies = []
    for out, pick in zip(outs, picks):
        for slot, (source, row) in enumerate(pick):
            copies.append(
                pltpu.make_async_copy(sources[source].at[row], out.at[slot], sems.at[len(copies)])
            )
            copies[-1].start()
    for copy in copies:
        copy.wait()


def glue(chain, held, groups, awaited, time):
    arrays = []
    for name in [name for group in groups for name in group] + list(awaited):
        if not any(held[name][0] is array for array in arrays):
            arrays.append(held[name][0])
    index = lambda array: next(i for i, one in enumerate(arrays) if one is array)
    picks = [[(index(held[name][0]), held[name][1]) for name in group] for group in groups]
    block = arrays[0].shape[1:]
    return chain.launch(
        functools.partial(glue_kernel, picks, len(arrays)),
        arrays,
        [shape((len(group),) + block, bf16) for group in groups],
        4,
        "glue",
        time,
        far_in=range(len(arrays)),
        far_out=range(len(groups)),
        scratch=[pltpu.SemaphoreType.DMA((sum(len(group) for group in groups),))],
    )


def spread_kernel(masks, block_ref, *refs):
    outs, (wide_s, sems) = refs[4:8], refs[8:]
    seq, item = lax.axis_index("seq"), lax.axis_index("item")
    rows = wide_s.shape[1]
    copies = []
    for slot, (item_mask, seq_mask) in enumerate(masks):
        wide_s[slot] = block_ref[slot].astype(f32)
        owner_item, owner_seq = item ^ item_mask, seq ^ seq_mask
        first = owner_seq * 4 + (owner_item & 1) * 2 + (owner_item >> 1)
        target = pl.ds(pl.multiple_of(first * rows, 8), rows)
        at = 0
        for index, out in enumerate(outs):
            size = out.shape[1]
            copy = pltpu.make_async_copy(
                wide_s.at[slot, :, pl.ds(at, size)], out.at[target, :], sems.at[slot, index]
            )
            copy.start()
            copies.append(copy)
            at += size
    for copy in copies:
        copy.wait()


def spread(chain, names, sibling, blocks, outs):
    masks = [
        (2 * ("x" in name) + sibling, ("y" in name) + 2 * ("a" in name) + 4 * ("b" in name))
        for name in names
    ]
    number = len(names)
    return chain.launch(
        functools.partial(spread_kernel, masks),
        (blocks, *outs),
        [shape(out.shape, f32) for out in outs],
        16,
        "spread",
        2.3,
        far_in=range(1, 5),
        far_out=range(4),
        scratch=[
            pltpu.VMEM(blocks.shape, f32),
            pltpu.SemaphoreType.DMA((number, 4)),
        ],
        aliases={1 + i: i for i in range(4)},
    )


def blank_kernel(*refs):
    pass


def gather_blocks(chain, keep, got, groups):
    block = plain_sum(chain, keep, got)[None]
    held = {"": (block, 0)}
    for level, sends in enumerate(ROUTES + ((),)):
        swap = SWAPS.get(level)
        if level == 0:
            arrays = [block] * len(sends)
        else:
            wanted = [names for _, names in sends] + ([swap] if swap else [])
            arrays = glue(chain, held, wanted, AWAITED.get(level, ()), 50 if level == 1 else 2)
        for (along, names), array in zip(sends, arrays):
            moved = swap_bit(array, *BIT_OF[along])
            for row, name in enumerate(names):
                held["".join(sorted(name + along))] = (moved, row)
        if swap:
            groups.append((swap, arrays[-1], swap_bit(arrays[-1], "item", 0)))
        yield


def spread_blocks(chain, rows, widths, groups):
    outs = [shape((32 * rows, width), f32) for width in widths]
    outs = chain.launch(blank_kernel, (), outs, 4, "blanks", far_out=range(4))
    while True:
        at, sibling = yield outs
        outs = spread(chain, groups[at][0], sibling, groups[at][1 + sibling], outs)


def last_kernel(
    slab, mine_ref, other_ref, resid_ref, lat_ref, gain_ref, wq_ref,
    value_ref, key_ref, query_ref, latent_ref, gain_kv_ref, gain_q_ref, gain_mlp_ref, resid_s,
):
    byte_width = value_ref.shape[0]
    latents, width = lat_ref.shape
    upper = place_bit("item", 0) != 0
    half = mine_ref.shape[0]
    rest = byte_width - half
    value_ref[pl.ds(0, half), :] = jnp.where(upper, other_ref[...], mine_ref[...]).astype(f32)
    second = jnp.where(upper, mine_ref[...], other_ref[...])
    value_ref[pl.ds(half, rest), :] = second[:rest].astype(f32)
    lower = second[rest:].astype(f32)
    for at in range(0, byte_width, QK):
        key_ref[pl.ds(at, QK), :] = lower[:, at : at + QK]
    query_t = (lower[:, byte_width : byte_width + latents] * SCALE).astype(bf16)
    gains = lower[:, byte_width + latents :]
    row = 0
    for ref in (gain_kv_ref, gain_mlp_ref):
        count = ref.shape[0] // QK
        ref[...] = jnp.concatenate([gains[row + i : row + i + 1] for i in range(count)], axis=1).reshape(-1)
        row += count
    hat, inverse = normalize(lat_ref[...].astype(f32))
    gain = row_of(gain_ref)
    lat_low = (hat * gain).astype(bf16)
    query_ref[...] = dot_nt(lat_low.T, query_t)
    grad_lat = dot_nt(query_t.T, wq_ref[...])
    gain_q_ref[...] = jnp.sum(grad_lat * hat, axis=0)
    parts = width // latents
    for rank in range(latents // slab):
        for part in range(parts):
            resid_s[pl.ds(rank * slab, slab), pl.ds(part * latents, latents)] = resid_ref[
                pl.ds((rank * parts + part) * slab, slab), :
            ]
    latent_ref[...] = resid_s[...] + norm_back(grad_lat * gain, hat, inverse)


def last_step(chain, n_seq, sums, resid, latent_init, gain_q, w_query):
    latents, width = latent_init.shape
    byte_width = 2 * sums[0].shape[0] - QK
    dims = [(byte_width, V), (byte_width, QK), (width, QK), (latents, width)]
    dims += [(byte_width,), (width,), (width,)]
    return chain.launch(
        functools.partial(last_kernel, latents // n_seq),
        (*sums, resid, latent_init, gain_q, w_query),
        [shape(dim, f32) for dim in dims],
        16,
        "last_step",
        4.8,
        scratch=[pltpu.VMEM((latents, width), f32)],
    )


ORDER = "abcad0ba1cbad2cbadcb3dAcdBCD"

TAIL = "pmpAoppmpapmBpmpmbCpc"


def per_device(
    byte_in,
    lengths,
    latent_init,
    gain_kv,
    gain_q,
    gain_mlp,
    w_query,
    w_key,
    w_value,
    w_out,
    w_up,
    w_down,
    d_out,
):
    items, slot, byte_width = byte_in.shape
    latents, width = latent_init.shape
    n_item, n_seq = lax.axis_size("item"), lax.axis_size("seq")
    item_bits, seq_bits = bits_of("item"), bits_of("seq")
    chain = Chain(byte_in)
    keys, values, acts, halves = [None] * items, [None] * items, [None] * items, [None] * items
    gas, stats = [None] * items, [None] * items
    q_t, limits = None, None
    carried = None
    made, grads = [None] * items, [None] * items

    def travel(item):
        nonlocal q_t, limits
        operands = (byte_in, gain_kv, w_key, w_value)
        if item == 0:
            limits, q_t, *made = attend_first(
                chain, lengths, *operands, latent_init, gain_q, w_query
            )
        else:
            made = attend(chain, item, limits, *operands, q_t)
        keys[item], values[item], keep, send = made
        got = swap_bit(send, "seq", 0)
        yield
        mine = merge(chain, 0, keep, got)
        if n_seq == 8:
            inward = lax.ppermute(mine, "seq", [(0, 2), (1, 3), (6, 4), (7, 5)])
            yield
            mine = merge(chain, 2, mine, inward)
            across = lax.ppermute(mine, "seq", [(2, 4), (3, 5), (4, 2), (5, 3)])
            yield
            mine = merge(chain, 2, mine, across)
            outward = lax.ppermute(mine, "seq", [(2, 0), (3, 1), (4, 6), (5, 7)])
            yield
            mine = choose(chain, mine, outward)
        else:
            for axis, bit in seq_bits[1:]:
                got = swap_bit(mine, axis, bit)
                yield
                mine = merge(chain, bit, mine, got)
        yield mine, swap_bit(mine, "seq", 0)

    ways = [travel(item) for item in range(items)]
    for letter in ORDER:
        if letter.isdigit():
            acts[int(letter)] = cotangent(chain, int(letter), d_out, w_down)
            continue
        item = "abcd".index(letter.lower())
        if letter.islower():
            halves[item] = next(ways[item])
            continue
        for halves_item in ways[item]:
            halves[item] = halves_item
        made[item], gas[item], stats[item], mlp, *factors = latent_step(
            chain,
            item,
            width // n_seq,
            *halves[item],
            latent_init,
            gain_mlp,
            d_out,
            acts[item],
            (w_out, w_up, w_down),
            carried,
        )
        carried = (mlp, *factors[:3])
    sums = factors[3:]

    begun = None

    def go_back(item):
        nonlocal begun
        args = (limits, byte_in, gain_kv, w_key, w_value, q_t, keys[item], values[item], gas[item], stats[item])
        grads[item], total, gains, *halves = bytes_step(chain, item, *args, mlp, 1.0 / n_seq, begun)
        begun = (total, gains)
        return halves

    keep, send = sums
    got = swap_bit(send, *item_bits[0])
    go_back(0)
    for step, following in zip(item_bits, item_bits[1:]):
        keep, send = split_sum(chain, following, keep, got)
        got = swap_bit(send, *following)
    go_back(1)
    go_back(2)
    widths = (width, width, width, latents)
    direct = (n_item, n_seq) == (4, 8)
    if direct:
        groups = []
        latent_way = gather_blocks(chain, keep, got, groups)
        next(latent_way)
        spread_way = spread_blocks(chain, keep.shape[0], widths, groups)
        next(spread_way)
    else:
        latent_piece = plain_sum(chain, keep, got)
        latent_all = lax.all_gather(latent_piece, ("item", "seq"), axis=0, tiled=False)
    keep, send = go_back(3)
    byte_way = whole_sum(chain, keep, send, item_bits, seq_bits)
    if direct:
        for letter in TAIL:
            if letter == "o":
                latents_out, byte_grad = store(chain, made, grads)
            elif letter == "m":
                next(latent_way)
            elif letter == "p":
                byte_halves = next(byte_way)
            else:
                group = "abc".index(letter.lower()), int(letter.islower())
                whole_grads = spread_way.send(group)
    else:
        count = len(item_bits)
        blocks = latent_all.reshape((2,) * count + (n_seq,) + latent_piece.shape)
        turn = [count] + list(range(count))[::-1] + [count + 1, count + 2]
        blocks = blocks.transpose(turn).reshape(-1, sum(widths)).astype(f32)
        whole_grads = [blocks[:, i * width : i * width + size] for i, size in enumerate(widths)]
        for byte_halves in byte_way:
            pass
        latents_out, byte_grad = store(chain, made, grads)
    out_grad, up_grad, down_grad, resid = whole_grads
    value_grad, key_grad, query_grad, latent_grad, gain_kv_grad, gain_q_grad, gain_mlp_grad = last_step(
        chain, n_seq, byte_halves, resid, latent_init, gain_q, w_query
    )
    return (
        latents_out,
        byte_grad,
        latent_grad,
        gain_kv_grad,
        gain_q_grad,
        gain_mlp_grad,
        query_grad,
        key_grad,
        value_grad,
        out_grad,
        up_grad,
        down_grad,
    )


def solution(mesh):
    placed = (P("item", "seq", None), P("item")) + (P(),) * 10 + (P("item", None, None),)
    return jax.shard_map(
        per_device,
        mesh=mesh,
        in_specs=placed,
        out_specs=(P("item", None, None), P("item", "seq", None)) + (P(),) * 10,
        check_vma=False,
    )
```
